32 devices in a mesh: dp: 4 (over y, x), expert: 8 (over z, core).
Axes of the slice: x: 2, y: 2, z: 4, core: 2. Of those that a mesh axis runs over, the one named last changes fastest.
Arguments:
- tokens: bfloat16 [4, 1536, 1280], P('dp', 'expert'), may hold values from -6 to 6
- cotangent: bfloat16 [4, 1536, 1280], P('dp', 'expert'), may hold values from -6 to 6
- lengths: int32 [4, 4], P('dp'), may hold values from 1 to 1532, as said below
- routes: int32 [4, 1536, 7], P('dp', 'expert'), may hold values from 0 to 15, all different within a row; in each aligned block of 192 rows (0 to 191, 192 to 383, ..., all dimensions but the last counted through in order) at most 120 rows name the same one
- attn_qkv: float32 [1280, 3840], P(('dp', 'expert')), may hold values from -0.25 to 0.25
- attn_out: float32 [1280, 1280], P(None, ('dp', 'expert')), may hold values from -1.25 to 1.25
- shared_gate: float32 [1280, 896], P(('dp', 'expert')), may hold values from -0.15625 to 0.15625
- shared_up: float32 [1280, 896], P(('dp', 'expert')), may hold values from -0.15625 to 0.15625
- shared_down: float32 [896, 1280], P(None, ('dp', 'expert')), may hold values from -0.375 to 0.375
- router: float32 [1280, 16], P(('dp', 'expert')), may hold values from -0.078125 to 0.078125
- gains: float32 [2, 1280], P(None, ('dp', 'expert')), may hold values from 0.5 to 1.5
- expert_gate: float32 [16, 1280, 896], P('expert', 'dp'), may hold values from -0.15625 to 0.15625
- expert_up: float32 [16, 1280, 896], P('expert', 'dp'), may hold values from -0.15625 to 0.15625
- expert_down: float32 [16, 896, 1280], P('expert', None, 'dp'), may hold values from -0.5 to 0.5
Outputs:
- output: bfloat16 [4, 1536, 1280], P('dp', 'expert')
- input_grad: bfloat16 [4, 1536, 1280], P('dp', 'expert')
- grad_attn_qkv: float32 [1280, 3840], P(('dp', 'expert'))
- grad_attn_out: float32 [1280, 1280], P(None, ('dp', 'expert'))
- grad_shared_gate: float32 [1280, 896], P(('dp', 'expert'))
- grad_shared_up: float32 [1280, 896], P(('dp', 'expert'))
- grad_shared_down: float32 [896, 1280], P(None, ('dp', 'expert'))
- grad_router: float32 [1280, 16], P(('dp', 'expert'))
- grad_gains: float32 [2, 1280], P(None, ('dp', 'expert'))
- grad_expert_gate: float32 [16, 1280, 896], P('expert', 'dp')
- grad_expert_up: float32 [16, 1280, 896], P('expert', 'dp')
- grad_expert_down: float32 [16, 896, 1280], P('expert', None, 'dp')
The draws below stay inside these ranges and needn't reach their ends.
Inputs may be any that keep to these rules, and one draw needn't show every extreme that they name: Each row's lengths sum to less than 1536; one document of each row, at a drawn place, starts among the first 192 positions and ends among the last 192; in one drawn row all other documents have length 1 and one padding position follows. `routes`: each position names 7 different experts; within the 192 positions of one device no expert is named more than 120 times.
All inputs are finite; a program needn't handle non-finite values.
Results may differ from the reference program's by a relative error of at most 0.025.
The reference program's roundings to bfloat16 on the way count: a program that leaves them out, or rounds other values in their place, can miss the bound.
Values may be sent and summed in bfloat16 or wider, within the bound.
A program may use at most 320 MiB of HBM per device.

```python
import math
import jax
import jax.numpy as jnp
import numpy as np
from jax import lax

D = 1280
H = 10
HD = 128
FF = 896
TOP = 7
DOCS = 4
TOK_DEV = 192
SEQ = 1536
EXPERTS = 16
CAP = 120
N_DP = 4
N_EXPERT = 8


def draw_lengths(key, part):
    key = jax.random.fold_in(key, 7)
    first_key, second_key, third_key, fourth_key = jax.random.split(key, 4)
    quarter = TOK_DEV // 4
    others = jax.random.randint(first_key, (N_DP, DOCS), 1, quarter)
    padding = jax.random.randint(second_key, (N_DP, 1), 1, quarter + 1)
    longest = jax.random.randint(third_key, (N_DP, 1), 0, DOCS)
    tight_row = jax.random.randint(fourth_key, (), 0, N_DP)
    is_tight = (jnp.arange(N_DP, dtype=jnp.int32) == tight_row)[:, None]
    others = jnp.where(is_tight, 1, others)
    padding = jnp.where(is_tight, 1, padding)
    chosen = jnp.arange(DOCS, dtype=jnp.int32)[None, :] == longest
    others_total = jnp.sum(jnp.where(chosen, 0, others), axis=1, keepdims=True)
    return jnp.where(chosen, SEQ - padding - others_total, others).astype(jnp.int32)


def block_scale(key, shape, pieces, smallest, largest):
    def one(dim, shards_of):
        draws = jax.random.uniform(jax.random.fold_in(jax.random.fold_in(key, 6), dim), (shards_of,), jnp.float32, smallest / len(pieces), largest / len(pieces))
        return jnp.repeat(jnp.exp(draws), shape[dim] // shards_of).reshape((-1,) + (1,) * (len(shape) - dim - 1))

    loudness = one(*pieces[0])
    for cut in pieces[1:]:
        loudness = loudness * one(*cut)
    return loudness


def routed_block(own_key, own, number, rows, amount, top, limit, lean):
    order = jax.random.permutation(own_key, amount)
    heavy_load, ordinary = portions_of(amount, rows * top, limit, lean, True), portions_of(amount, rows * top, limit, lean, False)
    places = jnp.arange(amount)

    def named(sizes, turn):
        used = int((sizes > 0).sum())
        fixed = max(1, used // 4)
        shifted = fixed + (places - fixed + turn * (used - fixed)) % max(1, amount - fixed)
        return jnp.zeros((amount,), jnp.int32).at[order[jnp.where(places < fixed, places, shifted)]].set(jnp.asarray(sizes, jnp.int32))

    sizes = jnp.where(number % 4 == 0, named(heavy_load, number // 4), named(ordinary, number - number // 4 - 1))
    mixed = jax.random.permutation(jax.random.fold_in(own, 3), amount)
    donor, taker = mixed[0:amount // 2 * 2:2], mixed[1:amount // 2 * 2:2]
    slack = jnp.minimum(sizes[donor] - 1, limit - sizes[taker]) // 2
    slack = jnp.where((donor == order[0]) | (taker == order[0]) | (sizes[taker] == 0), 0, jnp.maximum(slack, 0))
    shifted = jax.random.randint(jax.random.fold_in(own, 4), (amount // 2,), 0, 1 << 20) % (slack + 1)
    sizes = sizes.at[donor].add(-shifted).at[taker].add(shifted)
    labels = jnp.searchsorted(jnp.cumsum(sizes), jnp.arange(rows * top), side="right").astype(jnp.int32)
    grid = labels.reshape(top, rows).T
    grid = grid[jax.random.permutation(jax.random.fold_in(own, 1), rows)]
    turn = jax.random.randint(jax.random.fold_in(own, 2), (rows, 1), 0, top)
    return jnp.take_along_axis(grid, (jnp.arange(top)[None, :] + turn) % top, axis=1)


def portions_of(number_of, total, most, lean, full):
    loads = [(1 << 20) // math.isqrt(standing ** lean) + 1 for standing in range(1, number_of + 1)]
    largest = most if full else min(most, max(-(-total // number_of), total * loads[0] // sum(loads)))
    least = 1 if total - largest >= number_of - 1 else 0
    given, rest = [largest] + [least] * (number_of - 1), total - largest - least * (number_of - 1)
    while rest > 0:
        movable = [i for i in range(1, number_of) if given[i] < largest] or [i for i in range(1, number_of) if given[i] < most]
        whole, left = sum([loads[i] for i in movable]), rest
        for i in movable:
            extra = min(most - given[i], max(1, left * loads[i] // whole), rest)
            given[i] = given[i] + extra
            rest = rest - extra
    return np.array(given)


def centred(own_key, shape, deviation, bound, pieces=(), kind=jnp.bfloat16):
    factor_of = block_scale(own_key, shape, pieces, -0.22, 0.18) if pieces else 1.0
    entries = jax.random.normal(own_key, shape, jnp.float32) * deviation * factor_of
    return jnp.minimum(jnp.maximum(entries, -bound), bound).astype(kind)


def setup_inputs(seed: int = 0) -> dict:
    key_list = jax.random.split(jax.random.key(seed), 15)
    tokens = centred(key_list[0], (N_DP, SEQ, D), 1.0, 6.0, ((0, 4), (1, 8)))
    cotangent = centred(key_list[1], (N_DP, SEQ, D), 1.0, 6.0, ((0, 4), (1, 8)))
    lengths = draw_lengths(jax.random.fold_in(key_list[14], 71), 0)
    routes_keys = jax.random.split(jax.random.fold_in(key_list[3], 1), N_DP * SEQ // TOK_DEV)
    routes_turns = jax.random.permutation(jax.random.fold_in(key_list[3], 3), N_DP * SEQ // TOK_DEV)
    routes = jax.vmap(lambda own, number: routed_block(jax.random.fold_in(key_list[3], 2), own, number, TOK_DEV, EXPERTS, TOP, CAP, 1))(routes_keys, routes_turns).reshape((N_DP, SEQ, TOP))
    attn_qkv = centred(key_list[4], (D, 3 * H * HD), (D // 2) ** -0.5, 0.25, ((0, 32),), jnp.float32)
    attn_out = centred(key_list[5], (H * HD, D), (H * HD // 64) ** -0.5, 1.25, ((1, 32),), jnp.float32)
    shared_gate = centred(key_list[6], (D, FF), D ** -0.5, 0.15625, ((0, 32),), jnp.float32)
    shared_up = centred(key_list[7], (D, FF), D ** -0.5, 0.15625, ((0, 32),), jnp.float32)
    shared_down = centred(key_list[8], (FF, D), (FF // 4) ** -0.5, 0.375, ((1, 32),), jnp.float32)
    router = centred(key_list[9], (D, EXPERTS), (4 * D) ** -0.5, 0.078125, ((0, 32),), jnp.float32)
    gains = jnp.clip(1.0 + 0.1 * jax.random.normal(key_list[10], (2, D), jnp.float32), 0.5, 1.5)
    expert_gate = centred(key_list[11], (EXPERTS, D, FF), D ** -0.5, 0.15625, ((0, 8), (1, 4)), jnp.float32)
    expert_up = centred(key_list[12], (EXPERTS, D, FF), D ** -0.5, 0.15625, ((0, 8), (1, 4)), jnp.float32)
    expert_down = centred(key_list[13], (EXPERTS, FF, D), (FF // 8) ** -0.5, 0.5, ((0, 8), (2, 4)), jnp.float32)
    return {"tokens": tokens, "cotangent": cotangent, "lengths": lengths, "routes": routes, "attn_qkv": attn_qkv, "attn_out": attn_out, "shared_gate": shared_gate, "shared_up": shared_up, "shared_down": shared_down, "router": router, "gains": gains, "expert_gate": expert_gate, "expert_up": expert_up, "expert_down": expert_down}


@jax.custom_vjp
def low(v):
    return lax.optimization_barrier(v.astype(jnp.bfloat16)).astype(jnp.float32)

@jax.custom_vjp
def low_back(v):
    return v

def low_keep(v):
    return (low(v), None)

def low_pass(kept, grad):
    return (grad,)

def back_keep(v):
    return (v, None)

def back_low(kept, grad):
    return (low(grad),)
low.defvjp(low_keep, low_pass)
low_back.defvjp(back_keep, back_low)
epsilon = 1e-06
highest = lax.Precision.HIGHEST

def segments(lengths, places):
    doc_ends = jnp.cumsum(lengths).astype(jnp.int32)
    doc_starts = (doc_ends - lengths).astype(jnp.int32)
    live_total = doc_ends[-1]
    doc_index = lax.optimization_barrier(jnp.sum((places[:, None] >= doc_ends[None, :]).astype(jnp.int32), axis=1)).astype(jnp.int32)
    is_live = places < live_total
    segment = jnp.where(is_live, doc_index, lengths.shape[0] + places)
    matches = doc_index[:, None] == jnp.arange(lengths.shape[0], dtype=jnp.int32)[None, :]
    doc_first = lax.optimization_barrier(jnp.sum(jnp.where(matches, doc_starts[None, :], 0), axis=1)).astype(jnp.int32)
    rope_pos = places - jnp.where(is_live, doc_first, live_total)
    return (segment, rope_pos)

def rotate(values, rope_pos, direction):
    half_width = values.shape[-1] // 2
    frequency = 10000.0 ** (-jnp.arange(half_width, dtype=jnp.float32) / half_width)
    angles = rope_pos.astype(jnp.float32)[:, None] * frequency[None, :]
    cosine = jnp.cos(angles)[:, None, :]
    sine_row = direction * jnp.sin(angles)[:, None, :]
    front_half = values[..., :half_width]
    rear_half = values[..., half_width:]
    return jnp.concatenate([front_half * cosine - rear_half * sine_row, front_half * sine_row + rear_half * cosine], axis=-1)

def normalize(values, gain_row):
    return values * lax.rsqrt(lax.optimization_barrier(jnp.mean(values * values, axis=-1, keepdims=True)) + epsilon) * gain_row

def slots_of(route_rows, expert_total):
    flat_ids = route_rows.reshape(-1)
    onehot = (flat_ids[:, None] == jnp.arange(expert_total, dtype=jnp.int32)[None, :]).astype(jnp.int32)
    earlier = (jnp.cumsum(onehot, axis=0) - onehot).astype(jnp.int32)
    return lax.optimization_barrier(jnp.sum(earlier * onehot, axis=1)).astype(jnp.int32).reshape(route_rows.shape)

def attend(queries, key_rows, value_rows, segment):
    row_count = queries.shape[0]
    block_size = min(512, row_count)
    places = jnp.arange(row_count, dtype=jnp.int32)
    score_scale = HD ** (-0.5)

    def one_block(block_index):
        first_row = block_index * block_size
        query_part = lax.dynamic_slice_in_dim(queries, first_row, block_size, 0)
        query_seg = lax.dynamic_slice_in_dim(segment, first_row, block_size, 0)
        query_place = lax.dynamic_slice_in_dim(places, first_row, block_size, 0)
        products = low_back(jnp.einsum('qhd,khd->hqk', query_part, key_rows, precision=highest))
        scores = products * score_scale
        allowed = (query_seg[:, None] == segment[None, :]) & (places[None, :] <= query_place[:, None])
        scores = jnp.where(allowed[None], scores, -1e+30)
        row_max = lax.optimization_barrier(jnp.max(scores, axis=-1, keepdims=True))
        weights = jnp.where(allowed[None], jnp.exp(scores - row_max), 0.0)
        probabilities = weights / lax.optimization_barrier(jnp.sum(weights, axis=-1, keepdims=True))
        return jnp.einsum('hqk,khd->qhd', low(probabilities), value_rows, precision=highest)
    block_outputs = lax.map(jax.checkpoint(one_block), jnp.arange(row_count // block_size, dtype=jnp.int32))
    return block_outputs.reshape(queries.shape)

def layer_group(inputs, lengths, route_ids, weights_b):
    qkv_weight, out_weight, gate_shared, up_shared, down_shared, route_weight, gain_pair, gate_expert, up_expert, down_expert = weights_b
    places = jnp.arange(SEQ, dtype=jnp.int32)
    segment, rope_pos = segments(lengths, places)
    normed = low(normalize(inputs, gain_pair[0]))
    projected = low_back(jnp.dot(normed, qkv_weight, precision=highest)).reshape(SEQ, 3, H, HD)
    queries = low(rotate(projected[:, 0], rope_pos, 1.0))
    key_rows = low(rotate(projected[:, 1], rope_pos, 1.0))
    value_rows = low(projected[:, 2])
    attended = low(low_back(attend(queries, key_rows, value_rows, segment).reshape(SEQ, H * HD)))
    middle = inputs + low_back(jnp.dot(attended, out_weight, precision=highest))
    normed_moe = low(normalize(middle, gain_pair[1]))
    shared_gate_v = low_back(jnp.dot(normed_moe, gate_shared, precision=highest))
    shared_up_v = low_back(jnp.dot(normed_moe, up_shared, precision=highest))
    shared_mid = low(jax.nn.silu(shared_gate_v) * shared_up_v)
    shared_out = low_back(jnp.dot(shared_mid, down_shared, precision=highest))
    logits = low_back(jnp.dot(normed_moe, route_weight, precision=highest))
    route_probs = jax.nn.softmax(logits, axis=-1)
    chosen = jnp.take_along_axis(route_probs, route_ids, axis=1)
    gates = chosen / lax.optimization_barrier(jnp.sum(chosen, axis=1, keepdims=True))
    token_blocks = normed_moe.reshape(N_EXPERT, TOK_DEV, D)
    route_blocks = route_ids.reshape(N_EXPERT, TOK_DEV, TOP)

    def block_slots(block_routes):
        return slots_of(block_routes, EXPERTS)
    slot_blocks = jax.vmap(block_slots)(route_blocks)

    def fill_slots(block_rows, block_routes, slot_rows):
        buffer_rows = jnp.zeros((EXPERTS, CAP, D), block_rows.dtype)
        spread = jnp.broadcast_to(block_rows[:, None, :], (TOK_DEV, TOP, D))
        return buffer_rows.at[block_routes, slot_rows].set(spread)
    dispatched = low_back(jax.vmap(fill_slots)(token_blocks, route_blocks, slot_blocks))
    expert_rows = jnp.transpose(dispatched, (1, 0, 2, 3)).reshape(EXPERTS, N_EXPERT * CAP, D)
    gate_values = low_back(jnp.einsum('erd,edf->erf', expert_rows, gate_expert, precision=highest))
    up_values = low_back(jnp.einsum('erd,edf->erf', expert_rows, up_expert, precision=highest))
    expert_mid = low(jax.nn.silu(gate_values) * up_values)
    expert_out = low(low_back(jnp.einsum('erf,efd->erd', expert_mid, down_expert, precision=highest)))
    returned = jnp.transpose(expert_out.reshape(EXPERTS, N_EXPERT, CAP, D), (1, 0, 2, 3))

    def pick_rows(block_back, block_routes, slot_rows):
        return block_back[block_routes, slot_rows]
    picked = jax.vmap(pick_rows)(returned, route_blocks, slot_blocks).reshape(SEQ, TOP, D)
    mixture = lax.optimization_barrier(jnp.sum(gates[:, :, None] * picked, axis=1))
    return middle + shared_out + mixture

def reference(tokens, cotangent, lengths, routes, attn_qkv, attn_out, shared_gate, shared_up, shared_down, router, gains, expert_gate, expert_up, expert_down):
    masters = (attn_qkv, attn_out, shared_gate, shared_up, shared_down, router, gains, expert_gate, expert_up, expert_down)

    def forward(inputs, *weight_list):
        weights_b = tuple((low(weight) for weight in weight_list))

        def one_group(group_args):
            return layer_group(group_args[0], group_args[1], group_args[2], weights_b)
        return lax.map(one_group, (inputs, lengths, routes))
    output, pullback = jax.vjp(forward, tokens.astype(jnp.float32), *masters)
    gradients = pullback(cotangent.astype(jnp.float32))
    return (output.astype(jnp.bfloat16), gradients[0].astype(jnp.bfloat16), gradients[1], gradients[2], gradients[3], gradients[4], gradients[5], gradients[6], gradients[7], gradients[8], gradients[9], gradients[10])
```

```python
import functools

import jax
import jax.numpy as jnp
from jax import lax
from jax.experimental import pallas as pl
from jax.experimental.pallas import tpu as pltpu
from jax.sharding import PartitionSpec as P

H = 10
HD = 128
TOP = 7
EXP_DEV = 2
EPS = 1e-06
NEG = -1e30
BF = jnp.bfloat16
F32 = jnp.float32
VMEM_LIMIT = 56 * 1024 * 1024


def params(**kw):
    return pltpu.CompilerParams(vmem_limit_bytes=VMEM_LIMIT, **kw)


def nn(a, b):
    return jnp.dot(a, b, preferred_element_type=F32)


def nt(a, b):
    return lax.dot_general(a, b, (((1,), (1,)), ((), ())), preferred_element_type=F32)


def tn(a, b):
    return lax.dot_general(a, b, (((0,), (0,)), ((), ())), preferred_element_type=F32)


def doc_starts_of(lengths, places):
    doc_ends = jnp.cumsum(lengths)
    doc_starts = doc_ends - lengths
    total = doc_ends[-1]
    doc_index = jnp.sum((places[:, None] >= doc_ends[None, :]).astype(jnp.int32), axis=1)
    live = places < total
    matches = doc_index[:, None] == jnp.arange(lengths.shape[0], dtype=jnp.int32)[None, :]
    first = jnp.sum(jnp.where(matches, doc_starts[None, :], 0), axis=1)
    return jnp.where(live, first, places), places - jnp.where(live, first, total)


def turn_tables(rope_pos):
    half = HD // 2
    frequency = 10000.0 ** (-jnp.arange(half, dtype=F32) / half)
    angles = rope_pos.astype(F32)[:, None] * frequency[None, :]
    cosine = jnp.cos(angles)
    sine = jnp.sin(angles)
    return (
        jnp.concatenate([cosine, cosine], axis=1),
        jnp.concatenate([-sine, sine], axis=1),
    )


def inverse_rms(values):
    return lax.rsqrt(jnp.mean(values * values, axis=-1, keepdims=True) + EPS)


MESH = pl.DeviceIdType.MESH


def sent(src, dst, send_sem, recv_sem, device):
    return pltpu.make_async_remote_copy(
        src_ref=src,
        dst_ref=dst,
        send_sem=send_sem,
        recv_sem=recv_sem,
        device_id=device,
        device_id_type=MESH,
    )


class Place:
    def __init__(self, chips):
        self.d = lax.axis_index("dp")
        self.e = lax.axis_index("expert")
        self.z = self.e // 2
        self.c = self.e % 2
        self.y = self.d // 2
        self.x = self.d % 2
        self.chips = chips
        self.sibling = (self.d, self.e + 1 - 2 * self.c)
        self.across_x = (self.d + 1 - 2 * self.x, self.e)
        self.across_y = (self.d + 2 - 4 * self.y, self.e)
        self.up = (self.d, self.e + 2)
        self.down = (self.d, self.e - 2)


def greet(devices, conditions):
    barrier = pltpu.get_barrier_semaphore()
    count = 0
    for device, condition in zip(devices, conditions):
        if condition is None:
            pl.semaphore_signal(barrier, inc=1, device_id=device, device_id_type=MESH)
            count = count + 1
        else:

            @pl.when(condition)
            def _(device=device):
                pl.semaphore_signal(barrier, inc=1, device_id=device, device_id_type=MESH)

            count = count + condition.astype(jnp.int32)
    pl.semaphore_wait(barrier, count)


def gather_kernel(chips, n_full, n_chain, *refs):
    n = n_full + n_chain
    ins, outs, sems = refs[:n], refs[n : 2 * n], refs[2 * n :]
    at = Place(chips)
    chain = 2 * chips
    z, c = at.z, at.c
    has_up, has_down = z < chips - 1, z > 0
    devices = [at.sibling, at.up, at.down]
    conditions = [None, has_up, has_down]
    if n_full:
        devices += [at.across_x, at.across_y]
        conditions += [None, None]
    greet(devices, conditions)
    x_dp, y_dp = at.across_x[0], at.across_y[0]
    far_dp = 3 - at.d

    class Array:
        pass

    arrays = []
    position = 0
    for i in range(n):
        a = Array()
        a.full = i < n_full
        a.own, a.out = ins[i], outs[i]
        a.local, a.s_chain, a.r_chain, a.s_core, a.r_core = sems[position : position + 5]
        position += 5
        if a.full:
            a.s_side, a.r_side, a.s_half, a.r_half = sems[position : position + 4]
            position += 4
            half = a.own.shape[-1] // 2
            a.halves = (pl.ds(0, half), pl.ds(half, half))
        arrays.append(a)

    def slot(a, dd, zz, cc):
        return a.out.at[dd * chain + 2 * zz + cc] if a.full else a.out.at[2 * zz + cc]

    def core_index(a, dd, zz):
        return dd * chips + zz if a.full else zz

    def to_core(a, dd, zz, src=None):
        ref = slot(a, dd, zz, c)
        k = core_index(a, dd, zz)
        return sent(ref if src is None else src, ref, a.s_core.at[k], a.r_core.at[k], at.sibling)

    def from_core(a, dd, zz):
        ref = slot(a, dd, zz, 1 - c)
        k = core_index(a, dd, zz)
        return sent(ref, ref, a.s_core.at[k], a.r_core.at[k], at.sibling)

    def along(a, zz, direction, src=None):
        ref = slot(a, at.d, zz, c)
        device = at.up if direction == 0 else at.down
        return sent(ref if src is None else src, ref, a.s_chain.at[direction, zz], a.r_chain.at[zz], device)

    def side(a, dd, zz, axis, src=None):
        ref = slot(a, dd, zz, c)
        device = at.across_x if axis == 0 else at.across_y
        return sent(
            ref if src is None else src, ref, a.s_side.at[axis, zz], a.r_side.at[axis, zz], device
        )

    def half(a, dd, zz, which):
        ref = slot(a, dd, zz, c).at[:, a.halves[which]]
        device = at.across_y if which == 0 else at.across_x
        return sent(ref, ref, a.s_half.at[which, zz], a.r_half.at[which, zz], device)

    def present(zz):
        return (zz >= 0) & (zz < chips)

    def block_here(zz, distance, direction):
        for a in arrays:
            along(a, zz, direction).wait_recv()
            if direction == 0:

                @pl.when(has_up)
                def _(a=a):
                    along(a, zz, 0).start()
            else:

                @pl.when(has_down)
                def _(a=a):
                    along(a, zz, 1).start()

            if a.full:
                side(a, at.d, zz, 0).start()
                side(a, at.d, zz, 1).start()
            to_core(a, at.d, zz).start()

    def side_here(zz):
        for a in arrays[:n_full]:
            side(a, x_dp, zz, 0).wait_recv()
            half(a, x_dp, zz, 0).start()
            to_core(a, x_dp, zz).start()
            side(a, y_dp, zz, 1).wait_recv()
            half(a, y_dp, zz, 1).start()
            to_core(a, y_dp, zz).start()

    def far_here(zz):
        for a in arrays[:n_full]:
            half(a, far_dp, zz, 0).wait_recv()
            half(a, far_dp, zz, 1).wait_recv()
            to_core(a, far_dp, zz).start()

    for a in arrays:

        @pl.when(has_up)
        def _(a=a):
            along(a, z, 0, a.own).start()

        @pl.when(has_down)
        def _(a=a):
            along(a, z, 1, a.own).start()

        if a.full:
            side(a, at.d, z, 0, a.own).start()
            side(a, at.d, z, 1, a.own).start()
        to_core(a, at.d, z, a.own).start()
    for a in arrays:
        pltpu.make_async_copy(a.own, slot(a, at.d, z, c), a.local).start()

    def at_distance(k, fn):
        @pl.when((k >= 0) & present(z - k))
        def _():
            fn(z - k)

        @pl.when((k >= 1) & present(z + k))
        def _():
            fn(z + k)

    def step(k, carry):
        @pl.when(present(z - k))
        def _():
            block_here(z - k, k, 0)

        @pl.when(present(z + k))
        def _():
            block_here(z + k, k, 1)

        if n_full:
            at_distance(k - 1, side_here)
            at_distance(k - 2, far_here)
        return carry

    lax.fori_loop(1, chips + (2 if n_full else 0), step, 0)

    def finish(zz, carry):
        for a in arrays:
            for dd in range(4) if a.full else (0,):
                from_core(a, dd, zz).wait_recv()
                to_core(a, dd, zz).wait_send()

            @pl.when((zz <= z) & has_up)
            def _(a=a):
                along(a, zz, 0).wait_send()

            @pl.when((zz >= z) & has_down)
            def _(a=a):
                along(a, zz, 1).wait_send()

            if a.full:
                for axis in (0, 1):
                    side(a, at.d, zz, axis).wait_send()
                half(a, x_dp, zz, 0).wait_send()
                half(a, y_dp, zz, 1).wait_send()
        return carry

    lax.fori_loop(0, chips, finish, 0)
    for a in arrays:
        pltpu.make_async_copy(a.own, slot(a, at.d, z, c), a.local).wait()


def gather(full, chained, collective_id):
    chain = lax.axis_size("expert")
    chips = chain // 2
    spread = lax.axis_size("dp")
    assert spread == 4 and chain % 2 == 0
    dma = pltpu.SemaphoreType.DMA
    scratch = []
    for array in full:
        scratch += [dma, dma((2, chips)), dma((chips,)), dma((4 * chips,)), dma((4 * chips,))]
        scratch += [dma((2, chips))] * 4
    for array in chained:
        scratch += [dma, dma((2, chips)), dma((chips,)), dma((chips,)), dma((chips,))]
    shapes = [jax.ShapeDtypeStruct((spread * chain,) + a.shape, a.dtype) for a in full]
    shapes += [jax.ShapeDtypeStruct((chain,) + a.shape, a.dtype) for a in chained]
    n = len(full) + len(chained)
    moved = sum(s.size * s.dtype.itemsize for s in shapes)
    return pl.pallas_call(
        functools.partial(gather_kernel, chips, len(full), len(chained)),
        out_shape=shapes,
        in_specs=[pl.BlockSpec(memory_space=pl.ANY)] * n,
        out_specs=[pl.BlockSpec(memory_space=pl.ANY)] * n,
        scratch_shapes=scratch,
        compiler_params=params(collective_id=collective_id, has_side_effects=True),
        cost_estimate=pl.CostEstimate(flops=0, bytes_accessed=16 * moved, transcendentals=0),
    )(*full, *chained)


def to_owner_kernel(chips, wide_ref, thin_ref, out_ref, thin_out, mine, other, came, sems_in, s_core, r_core, s_chain, r_chain, s_thin, r_thin):
    at = Place(chips)
    chain = 2 * chips
    z, c = at.z, at.c
    devices = [(at.d, lax.rem(at.e + k, chain)) for k in range(1, chain)]
    greet(devices, [None] * (chain - 1))

    def load(zz):
        return pltpu.make_async_copy(wide_ref.at[2 * zz + c], mine.at[zz], sems_in.at[zz])

    def to_core(zz):
        return sent(
            wide_ref.at[2 * zz + 1 - c], other.at[zz], s_core.at[zz], r_core.at[zz], at.sibling
        )

    def thin(k):
        target = lax.rem(at.e + k, chain)
        return sent(
            thin_ref.at[target], thin_out.at[at.e], s_thin.at[k], r_thin.at[k], (at.d, target)
        )

    def over(k):
        zz = lax.rem(z + k, chips)
        return sent(
            mine.at[zz], came.at[k], s_chain.at[k], r_chain.at[k], (at.d, 2 * zz + c)
        )

    order = [lax.rem(z + k, chips) for k in range(1, chips)] + [z]
    for zz in order:
        to_core(zz).start()
        load(zz).start()
    for k in range(1, chain):
        thin(k).start()
    own_thin = pltpu.make_async_copy(thin_ref.at[at.e], thin_out.at[at.e], s_thin.at[0])
    own_thin.start()
    for k, zz in enumerate(order):
        to_core(zz).wait_recv()
        load(zz).wait()
        total = mine[zz].astype(F32) + other[zz].astype(F32)
        if k < chips - 1:
            mine[zz] = total.astype(BF)
            over(k + 1).start()
        else:
            out_ref[...] = total
    for k in range(1, chips):
        over(k).wait_recv()
        out_ref[...] += came[k].astype(F32)
    for k in range(1, chips):
        over(k).wait_send()
    for zz in order:
        to_core(zz).wait_send()
    own_thin.wait()
    for k in range(1, chain):
        thin(k).wait()


def to_owner(wide, thin, collective_id):
    chain, rows, width = wide.shape
    chips = chain // 2
    dma = pltpu.SemaphoreType.DMA
    return pl.pallas_call(
        functools.partial(to_owner_kernel, chips),
        out_shape=[
            jax.ShapeDtypeStruct((rows, width), F32),
            jax.ShapeDtypeStruct(thin.shape, thin.dtype),
        ],
        in_specs=[pl.BlockSpec(memory_space=pl.ANY), pl.BlockSpec(memory_space=pltpu.VMEM)],
        out_specs=[pl.BlockSpec(memory_space=pltpu.VMEM), pl.BlockSpec(memory_space=pltpu.VMEM)],
        scratch_shapes=[
            pltpu.VMEM((chips, rows, width), BF),
            pltpu.VMEM((chips, rows, width), BF),
            pltpu.VMEM((chips, rows, width), BF),
            dma((chips,)),
            dma((chips,)),
            dma((chips,)),
            dma((chips,)),
            dma((chips,)),
            dma((chain,)),
            dma((chain,)),
        ],
        compiler_params=params(collective_id=collective_id, has_side_effects=True),
        cost_estimate=pl.CostEstimate(
            flops=0, bytes_accessed=16 * wide.size * 2, transcendentals=0
        ),
    )(wide, thin)


def sum_dense_kernel(chips, chunks, n_in, *refs):
    ins, outs = refs[:n_in], refs[n_in : 2 * n_in]
    n_chunks = len(chunks)
    rest = refs[2 * n_in :]
    sems = rest[:10]
    s_in, s_core, r_core, s_one, r_one, s_two, r_two, s_end, r_end = sems[:9]
    buffers = rest[9:]
    at = Place(chips)
    z, c, x, y = at.z, at.c, at.x, at.y
    others = [(at.d, 2 * lax.rem(z + k, chips) + c) for k in range(1, chips)]
    devices = [at.sibling, at.across_x, at.across_y] + others
    greet(devices, [None] * len(devices))

    class Chunk:
        def __init__(self, q):
            i, first, wide = chunks[q]
            self.i, self.first, self.wide = i, first, wide
            self.q = q
            self.mine, self.other, self.one, self.two, self.end = buffers[5 * q : 5 * q + 5]
            self.cols = pl.ds(first, wide)
            self.half = (pl.ds(0, wide // 2), pl.ds(wide // 2, wide // 2))

        def load(self):
            return pltpu.make_async_copy(
                ins[self.i].at[:, :, :, c, :, self.cols], self.mine, s_in.at[self.q]
            )

        def core(self):
            return sent(
                ins[self.i].at[:, :, :, 1 - c, :, self.cols],
                self.other,
                s_core.at[self.q],
                r_core.at[self.q],
                at.sibling,
            )

        def first_x(self):
            return sent(
                self.mine.at[:, 1 - x, :, :, self.half[0]],
                self.one.at[0],
                s_one.at[self.q, 0],
                r_one.at[self.q, 0],
                at.across_x,
            )

        def first_y(self):
            return sent(
                self.mine.at[1 - y, :, :, :, self.half[1]],
                self.one.at[1],
                s_one.at[self.q, 1],
                r_one.at[self.q, 1],
                at.across_y,
            )

        def second_y(self):
            return sent(
                self.mine.at[1 - y, x, :, :, self.half[0]],
                self.two.at[0],
                s_two.at[self.q, 0],
                r_two.at[self.q, 0],
                at.across_y,
            )

        def second_x(self):
            return sent(
                self.mine.at[y, 1 - x, :, :, self.half[1]],
                self.two.at[1],
                s_two.at[self.q, 1],
                r_two.at[self.q, 1],
                at.across_x,
            )

        def last(self, k):
            zz = lax.rem(z + k, chips)
            return sent(
                self.mine.at[y, x, zz],
                self.end.at[k - 1],
                s_end.at[self.q, k - 1],
                r_end.at[self.q, k - 1],
                (at.d, 2 * zz + c),
            )

    parts = [Chunk(q) for q in range(n_chunks)]

    def add(ref, place, more):
        ref[place] = (ref[place].astype(F32) + more.astype(F32)).astype(BF)

    def stage_one(p):
        p.core().wait_recv()
        p.load().wait()

        def body(k, carry):
            yy, xx, zz = k // (2 * chips), (k // chips) % 2, k % chips
            p.mine[yy, xx, zz] = (
                p.mine[yy, xx, zz].astype(F32) + p.other[yy, xx, zz].astype(F32)
            ).astype(BF)
            return carry

        lax.fori_loop(0, 4 * chips, body, 0)
        p.first_x().start()
        p.first_y().start()

    def stage_two(p):
        p.first_x().wait_recv()
        p.first_y().wait_recv()

        def body(k, carry):
            v, zz = k // chips, k % chips
            a, b = p.half
            p.mine[v, x, zz, :, a] = (
                p.mine[v, x, zz, :, a].astype(F32) + p.one[0, v, zz].astype(F32)
            ).astype(BF)
            p.mine[y, v, zz, :, b] = (
                p.mine[y, v, zz, :, b].astype(F32) + p.one[1, v, zz].astype(F32)
            ).astype(BF)
            return carry

        lax.fori_loop(0, 2 * chips, body, 0)
        p.second_y().start()
        p.second_x().start()

    def stage_three(p):
        p.second_y().wait_recv()
        p.second_x().wait_recv()

        def body(zz, carry):
            for w in (0, 1):
                s = p.half[w]
                p.mine[y, x, zz, :, s] = (
                    p.mine[y, x, zz, :, s].astype(F32) + p.two[w, zz].astype(F32)
                ).astype(BF)
            return carry

        lax.fori_loop(0, chips, body, 0)
        for k in range(1, chips):
            p.last(k).start()

    def stage_four(p):
        total = p.mine[y, x, z].astype(F32)
        for k in range(1, chips):
            p.last(k).wait_recv()
            total = total + p.end[k - 1].astype(F32)
        outs[p.i][:, p.first : p.first + p.wide] = total

    for p in parts:
        p.core().start()
        p.load().start()
    stages = (stage_one, stage_two, stage_three, stage_four)
    for t in range(n_chunks + len(stages) - 1):
        for s, stage in enumerate(stages):
            if 0 <= t - s < n_chunks:
                stage(parts[t - s])
    for p in parts:
        p.core().wait_send()
        p.first_x().wait_send()
        p.first_y().wait_send()
        p.second_x().wait_send()
        p.second_y().wait_send()
        for k in range(1, chips):
            p.last(k).wait_send()


def sum_dense(arrays, chunk_widths, collective_id):
    chain = lax.axis_size("expert")
    chips = chain // 2
    assert lax.axis_size("dp") == 4
    block = arrays[0].shape[0] // (4 * chain)
    dma = pltpu.SemaphoreType.DMA
    chunks = []
    for i, (array, wide) in enumerate(zip(arrays, chunk_widths)):
        assert array.shape[1] % wide == 0 and wide % 256 == 0
        chunks += [(i, first, wide) for first in range(0, array.shape[1], wide)]
    q = len(chunks)
    scratch = [dma((q,)), dma((q,)), dma((q,))] + [dma((q, 2))] * 4 + [dma((q, max(1, chips - 1)))] * 2
    for i, first, wide in chunks:
        scratch += [
            pltpu.VMEM((2, 2, chips, block, wide), BF),
            pltpu.VMEM((2, 2, chips, block, wide), BF),
            pltpu.VMEM((2, 2, chips, block, wide // 2), BF),
            pltpu.VMEM((2, chips, block, wide // 2), BF),
            pltpu.VMEM((max(1, chips - 1), block, wide), BF),
        ]
    n = len(arrays)
    return pl.pallas_call(
        functools.partial(sum_dense_kernel, chips, tuple(chunks), n),
        out_shape=[jax.ShapeDtypeStruct((block, a.shape[1]), F32) for a in arrays],
        in_specs=[pl.BlockSpec(memory_space=pl.ANY)] * n,
        out_specs=[pl.BlockSpec(memory_space=pltpu.VMEM)] * n,
        scratch_shapes=scratch,
        compiler_params=params(collective_id=collective_id, has_side_effects=True),
        cost_estimate=pl.CostEstimate(
            flops=0, bytes_accessed=16 * sum(a.size for a in arrays), transcendentals=0
        ),
    )(*[a.reshape(2, 2, chips, 2, block, a.shape[1]) for a in arrays])


def qkv_kernel(per_block, x_ref, w_ref, cos_ref, sin_ref, o_ref):
    column = pl.program_id(1)
    product = nn(x_ref[...], w_ref[...])
    for k in range(per_block):
        part = product[:, k * HD : (k + 1) * HD]
        head = column * per_block + k
        turned = part * cos_ref[...] + pltpu.roll(part, HD // 2, 1) * sin_ref[...]
        o_ref[:, k * HD : (k + 1) * HD] = jnp.where(head < 2 * H, turned, part).astype(BF)


def project_qkv(normed, weight, cosine, sine):
    rows, width = normed.shape
    columns = weight.shape[1]
    per_block = 2
    tile_m = min(rows, 1536)
    return pl.pallas_call(
        functools.partial(qkv_kernel, per_block),
        out_shape=jax.ShapeDtypeStruct((rows, columns), BF),
        grid=(rows // tile_m, columns // (per_block * HD)),
        in_specs=[
            pl.BlockSpec((tile_m, width), lambda m, n: (m, 0)),
            pl.BlockSpec((width, per_block * HD), lambda m, n: (0, n)),
            pl.BlockSpec((tile_m, HD), lambda m, n: (m, 0)),
            pl.BlockSpec((tile_m, HD), lambda m, n: (m, 0)),
        ],
        out_specs=pl.BlockSpec((tile_m, per_block * HD), lambda m, n: (m, n)),
        compiler_params=params(),
        cost_estimate=pl.CostEstimate(
            flops=2 * rows * width * columns,
            bytes_accessed=2 * (rows * width + width * columns + rows * columns),
            transcendentals=0,
        ),
    )(normed, weight, cosine, sine)


def attend_kernel(scale, me_ref, q_ref, k_ref, v_ref, first_ref, o_ref, log_ref, bias):
    rows, keys = bias.shape

    @pl.when(pl.program_id(0) == 0)
    def _():
        key_place = lax.broadcasted_iota(jnp.int32, (rows, keys), 1)
        query_place = me_ref[0] * rows + lax.broadcasted_iota(jnp.int32, (rows, keys), 0)
        allowed = (key_place <= query_place) & (key_place >= first_ref[...])
        bias[...] = jnp.where(allowed, 0.0, NEG)

    scores = nt(q_ref[...], k_ref[...]) * scale + bias[...]
    top = jnp.max(scores, axis=-1, keepdims=True)
    weights = jnp.exp(scores - top)
    total = jnp.sum(weights, axis=-1, keepdims=True)
    o_ref[...] = nn(weights.astype(BF), v_ref[...]) / total
    log_ref[...] = jnp.broadcast_to(top + jnp.log(total), (rows, 8))[None]


def attend(me, qkv, first_own):
    keys = qkv.shape[0]
    rows = first_own.shape[0]
    return pl.pallas_call(
        functools.partial(attend_kernel, HD**-0.5),
        out_shape=[
            jax.ShapeDtypeStruct((rows, H * HD), F32),
            jax.ShapeDtypeStruct((H, rows, 8), F32),
        ],
        grid_spec=pltpu.PrefetchScalarGridSpec(
            num_scalar_prefetch=1,
            grid=(H,),
            in_specs=[
                pl.BlockSpec((rows, HD), lambda h, me: (me[0], h)),
                pl.BlockSpec((keys, HD), lambda h, me: (0, H + h)),
                pl.BlockSpec((keys, HD), lambda h, me: (0, 2 * H + h)),
                pl.BlockSpec((rows, 1), lambda h, me: (0, 0)),
            ],
            out_specs=[
                pl.BlockSpec((rows, HD), lambda h, me: (0, h)),
                pl.BlockSpec((1, rows, 8), lambda h, me: (h, 0, 0)),
            ],
            scratch_shapes=[pltpu.VMEM((rows, keys), F32)],
        ),
        compiler_params=params(),
        cost_estimate=pl.CostEstimate(
            flops=4 * rows * keys * H * HD,
            bytes_accessed=4 * keys * H * HD,
            transcendentals=H * rows * keys,
        ),
    )(me, qkv, qkv, qkv, first_own[:, None])


def attend_back_kernel(
    scale,
    me_ref,
    q_ref,
    k_ref,
    v_ref,
    qa_ref,
    ko_ref,
    vo_ref,
    do_ref,
    da_ref,
    log_ref,
    delta_ref,
    loga_ref,
    deltaa_ref,
    first_ref,
    firsta_ref,
    cos_ref,
    sin_ref,
    o_ref,
    bias,
    biast,
):
    rows, keys = bias.shape

    @pl.when(pl.program_id(0) == 0)
    def _():
        place = lax.broadcasted_iota(jnp.int32, (rows, keys), 1)
        own = me_ref[0] * rows + lax.broadcasted_iota(jnp.int32, (rows, keys), 0)
        bias[...] = jnp.where((place <= own) & (place >= first_ref[...]), 0.0, NEG)
        biast[...] = jnp.where((own <= place) & (own >= firsta_ref[...]), 0.0, NEG)

    def unturn(value):
        return value * cos_ref[...] - pltpu.roll(value, HD // 2, 1) * sin_ref[...]

    log_own = log_ref[0][:, :1]
    delta_own = delta_ref[0][:, :1]
    weights = jnp.exp(nt(q_ref[...], k_ref[...]) * scale + bias[...] - log_own)
    back = nt(do_ref[...], v_ref[...])
    grad = (weights * (back - delta_own) * scale).astype(BF)
    o_ref[0] = unturn(nn(grad, k_ref[...])).astype(BF)

    weights = jnp.exp(nt(ko_ref[...], qa_ref[...]) * scale + biast[...] - loga_ref[0])
    o_ref[2] = nn(weights.astype(BF), da_ref[...]).astype(BF)
    back = nt(vo_ref[...], da_ref[...])
    grad = (weights * (back - deltaa_ref[0]) * scale).astype(BF)
    o_ref[1] = unturn(nn(grad, qa_ref[...])).astype(BF)


def attend_back(me, qkv, grad_own, grad_all, log_own, delta_own, log_all, delta_all, first, cosine, sine):
    keys = qkv.shape[0]
    rows = grad_own.shape[0]
    first_own, first_all = first
    return pl.pallas_call(
        functools.partial(attend_back_kernel, HD**-0.5),
        out_shape=jax.ShapeDtypeStruct((3, rows, H * HD), BF),
        grid_spec=pltpu.PrefetchScalarGridSpec(
            num_scalar_prefetch=1,
            grid=(H,),
            in_specs=[
                pl.BlockSpec((rows, HD), lambda h, me: (me[0], h)),
                pl.BlockSpec((keys, HD), lambda h, me: (0, H + h)),
                pl.BlockSpec((keys, HD), lambda h, me: (0, 2 * H + h)),
                pl.BlockSpec((keys, HD), lambda h, me: (0, h)),
                pl.BlockSpec((rows, HD), lambda h, me: (me[0], H + h)),
                pl.BlockSpec((rows, HD), lambda h, me: (me[0], 2 * H + h)),
                pl.BlockSpec((rows, HD), lambda h, me: (0, h)),
                pl.BlockSpec((keys, HD), lambda h, me: (0, h)),
                pl.BlockSpec((1, rows, 8), lambda h, me: (h, 0, 0)),
                pl.BlockSpec((1, rows, 8), lambda h, me: (h, 0, 0)),
                pl.BlockSpec((1, 1, keys), lambda h, me: (h, 0, 0)),
                pl.BlockSpec((1, 1, keys), lambda h, me: (h, 0, 0)),
                pl.BlockSpec((rows, 1), lambda h, me: (0, 0)),
                pl.BlockSpec((1, keys), lambda h, me: (0, 0)),
                pl.BlockSpec((rows, HD), lambda h, me: (0, 0)),
                pl.BlockSpec((rows, HD), lambda h, me: (0, 0)),
            ],
            out_specs=pl.BlockSpec((3, rows, HD), lambda h, me: (0, 0, h)),
            scratch_shapes=[pltpu.VMEM((rows, keys), F32)] * 2,
        ),
        compiler_params=params(),
        cost_estimate=pl.CostEstimate(
            flops=14 * rows * keys * H * HD,
            bytes_accessed=8 * keys * H * HD,
            transcendentals=2 * H * rows * keys,
        ),
    )(
        me,
        qkv,
        qkv,
        qkv,
        qkv,
        qkv,
        qkv,
        grad_own,
        grad_all,
        log_own,
        delta_own,
        log_all,
        delta_all,
        first_own[:, None],
        first_all[None, :],
        cosine,
        sine,
    )


def silu_parts(values):
    s = jax.nn.sigmoid(values)
    return values * s, s * (1.0 + values * (1.0 - s))


def local(
    tokens,
    cotangent,
    lengths,
    routes,
    attn_qkv,
    attn_out,
    shared_gate,
    shared_up,
    shared_down,
    router,
    gains,
    expert_gate,
    expert_up,
    expert_down,
):
    rows = tokens.shape[1]
    width = tokens.shape[2]
    hidden = shared_gate.shape[1]
    chain = lax.axis_size("expert")
    index = lax.axis_index("expert")
    experts = EXP_DEV * chain
    everyone = ("dp", "expert")
    keys = rows * chain
    own_first = index * rows
    me = index.reshape(1).astype(jnp.int32)

    route_pad = 128 * (-(-(experts + 2) // 128))
    misc = jnp.concatenate([router.astype(BF), gains.astype(BF).T], axis=1)
    misc = jnp.pad(misc, ((0, 0), (0, route_pad - experts - 2)))
    rest = jnp.concatenate(
        [
            misc,
            attn_out.astype(BF).T,
            shared_gate.astype(BF),
            shared_up.astype(BF),
            shared_down.astype(BF).T,
        ],
        axis=1,
    )
    qkv_weight, rest, tokens_all, routes_all, grads_all = gather(
        [attn_qkv.astype(BF), rest], [tokens[0], routes[0], cotangent[0]], 0
    )
    qkv_weight = qkv_weight.reshape(width, 3 * H * HD)
    rest = rest.reshape(width, rest.shape[-1])
    tokens_all = tokens_all.reshape(keys, width)
    routes_all = routes_all.reshape(keys, TOP)
    grads_all = grads_all.reshape(keys, width)
    cuts = [route_pad, route_pad + width]
    cuts += [cuts[-1] + hidden, cuts[-1] + 2 * hidden]
    misc, out_t, gate_shared, up_shared, down_t = jnp.split(rest, cuts, axis=1)
    route_weight = misc[:, :experts]
    gain_attn = misc[:, experts].astype(F32)
    gain_moe = misc[:, experts + 1].astype(F32)
    expert_shard = jnp.stack(
        [expert_gate.astype(BF), expert_up.astype(BF), jnp.swapaxes(expert_down.astype(BF), 1, 2)]
    )
    expert_shard, tokens_all = lax.optimization_barrier((expert_shard, tokens_all))
    expert_weight = lax.all_gather(expert_shard, "dp", axis=2, tiled=True)

    first_all, rope_all = doc_starts_of(lengths[0], jnp.arange(keys, dtype=jnp.int32))
    first_own = lax.dynamic_slice_in_dim(first_all, own_first, rows, 0)
    cosine, sine = turn_tables(rope_all)
    cosine_own = lax.dynamic_slice_in_dim(cosine, own_first, rows, 0)
    sine_own = lax.dynamic_slice_in_dim(sine, own_first, rows, 0)
    wide = tokens_all.astype(F32)
    normed_all = (wide * inverse_rms(wide) * gain_attn).astype(BF)
    inputs = tokens[0].astype(F32)
    inverse_one = inverse_rms(inputs)
    unit_one = inputs * inverse_one
    normed = (unit_one * gain_attn).astype(BF)
    qkv = project_qkv(normed_all, qkv_weight, cosine, sine)
    attended_full, log_own = attend(me, qkv, first_own)
    attended = attended_full.astype(BF)
    middle = inputs + nt(attended, out_t)
    inverse_two = inverse_rms(middle)
    unit_two = middle * inverse_two
    normed_moe = (unit_two * gain_moe).astype(BF)
    moe_all = gather([], [normed_moe], 1)[0].reshape(keys, width)

    def routing(activations, route_ids):
        logits = nn(activations, route_weight)
        probs = jax.nn.softmax(logits, axis=-1)
        named = route_ids[:, :, None] == jnp.arange(experts, dtype=jnp.int32)[None, None, :]
        named = jnp.any(named, axis=1)
        chosen = jnp.where(named, probs, 0.0)
        total = jnp.sum(chosen, axis=1, keepdims=True)
        return probs, named, chosen / total, total

    probs, named, gates, chosen_total = routing(normed_moe, routes[0])
    unused, unused, gates_all, unused = routing(moe_all, routes_all)
    gates_here = lax.dynamic_slice_in_dim(gates_all, index * EXP_DEV, EXP_DEV, 1)

    shared_gate_v = nn(normed_moe, gate_shared)
    shared_up_v = nn(normed_moe, up_shared)
    shared_act, shared_slope = silu_parts(shared_gate_v)
    shared_mid = (shared_act * shared_up_v).astype(BF)
    shared_out = nt(shared_mid, down_t)
    grad_out = cotangent[0].astype(F32)
    grad_bf = cotangent[0]
    grad_shared_mid = nn(grad_bf, down_t)
    grad_shared_gate_v = (grad_shared_mid * shared_up_v * shared_slope).astype(BF)
    grad_shared_up_v = (grad_shared_mid * shared_act).astype(BF)
    grad_down_t = tn(grad_bf, shared_mid)
    grad_gate_shared = tn(normed_moe, grad_shared_gate_v)
    grad_up_shared = tn(normed_moe, grad_shared_up_v)
    grad_normed_moe = nt(grad_shared_gate_v, gate_shared) + nt(grad_shared_up_v, up_shared)

    mixture = jnp.zeros((keys, width), F32)
    row_grads = jnp.zeros((keys, width), F32)
    wide_grads = grads_all.astype(F32)
    gate_grads = []
    weight_grads = []
    for e in range(EXP_DEV):
        gate_w, up_w, down_w = expert_weight[0, e], expert_weight[1, e], expert_weight[2, e]
        weight = gates_here[:, e : e + 1]
        gate_v = nn(moe_all, gate_w)
        up_v = nn(moe_all, up_w)
        act, slope = silu_parts(gate_v)
        mid = (act * up_v).astype(BF)
        branch = (weight * wide_grads).astype(BF)
        grad_mid = nn(branch, down_w)
        grad_gate_v = (grad_mid * up_v * slope).astype(BF)
        grad_up_v = (grad_mid * act).astype(BF)
        row = (nt(grad_gate_v, gate_w) + nt(grad_up_v, up_w)).astype(BF)
        row_grads = row_grads + row.astype(F32)
        out = nt(mid, down_w).astype(BF).astype(F32)
        mixture = mixture + weight * out
        gate_grads.append(jnp.sum(out * wide_grads, axis=1))
        weight_grads.append(
            jnp.stack(
                [
                    tn(moe_all, grad_gate_v).astype(BF),
                    tn(moe_all, grad_up_v).astype(BF),
                    tn(branch, mid).astype(BF),
                ]
            )
        )
    gate_grads = jnp.transpose(jnp.stack(gate_grads, axis=0).reshape(EXP_DEV, chain, rows), (1, 0, 2))
    row_sum, gate_grads = to_owner(
        row_grads.astype(BF).reshape(chain, rows, width), gate_grads, 2
    )
    mixture_own = lax.psum_scatter(mixture.astype(BF), "expert", scatter_dimension=0, tiled=True)
    gate_grads = gate_grads.reshape(experts, rows).T
    expert_sum = lax.psum_scatter(
        jnp.stack(weight_grads, axis=1), "dp", scatter_dimension=2, tiled=True
    ).astype(F32)
    output = (middle + shared_out + mixture_own.astype(F32)).astype(BF)

    grad_chosen = (gate_grads - jnp.sum(gates * gate_grads, axis=1, keepdims=True)) / chosen_total
    grad_probs = jnp.where(named, grad_chosen, 0.0)
    grad_logits = (
        probs * (grad_probs - jnp.sum(probs * grad_probs, axis=1, keepdims=True))
    ).astype(BF)
    grad_route = tn(normed_moe, grad_logits)
    grad_normed_moe = grad_normed_moe + row_sum + nt(grad_logits, route_weight)
    grad_gain_moe = jnp.sum(grad_normed_moe * unit_two, axis=0)
    scaled_two = grad_normed_moe * gain_moe
    grad_middle = grad_out + inverse_two * (
        scaled_two - unit_two * jnp.mean(scaled_two * unit_two, axis=-1, keepdims=True)
    )
    grad_attn = grad_middle.astype(BF)
    grad_attended = nn(grad_attn, out_t).astype(BF)
    grad_out_t = tn(grad_attn, attended)

    delta = jnp.sum((grad_attended.astype(F32) * attended_full).reshape(rows, H, HD), axis=-1).T
    side = jnp.concatenate([log_own[:, :, 0], delta], axis=0)
    grad_all, side_all = gather([], [grad_attended, side], 3)
    grad_all = grad_all.reshape(keys, H * HD)
    side_all = jnp.transpose(side_all, (1, 0, 2)).reshape(2, H, 1, keys)
    grads = attend_back(
        me,
        qkv,
        grad_attended,
        grad_all,
        log_own,
        jnp.broadcast_to(delta[:, :, None], (H, rows, 8)),
        side_all[0],
        side_all[1],
        (first_own, first_all),
        cosine_own,
        sine_own,
    )
    grad_projected = jnp.concatenate([grads[0], grads[1], grads[2]], axis=1)
    grad_qkv = tn(normed, grad_projected)
    grad_normed_one = nt(grad_projected, qkv_weight)
    grad_gain_attn = jnp.sum(grad_normed_one * unit_one, axis=0)
    scaled_one = grad_normed_one * gain_attn
    grad_inputs = grad_middle + inverse_one * (
        scaled_one - unit_one * jnp.mean(scaled_one * unit_one, axis=-1, keepdims=True)
    )

    grad_misc = jnp.concatenate([grad_route, grad_gain_attn[:, None], grad_gain_moe[:, None]], axis=1)
    grad_misc = jnp.pad(grad_misc, ((0, 0), (0, route_pad - experts - 2)))
    rest_sum, qkv_sum = sum_dense(
        [
            jnp.concatenate(
                [
                    grad_misc.astype(BF),
                    grad_out_t.astype(BF),
                    grad_gate_shared.astype(BF),
                    grad_up_shared.astype(BF),
                    grad_down_t.astype(BF),
                ],
                axis=1,
            ),
            grad_qkv.astype(BF),
        ],
        (1024, 768),
        4,
    )
    misc_sum, out_sum, gate_sum, up_sum, down_sum = jnp.split(rest_sum, cuts, axis=1)
    return (
        output[None],
        grad_inputs.astype(BF)[None],
        qkv_sum,
        out_sum.T,
        gate_sum,
        up_sum,
        down_sum.T,
        misc_sum[:, :experts],
        misc_sum[:, experts : experts + 2].T,
        expert_sum[0],
        expert_sum[1],
        jnp.swapaxes(expert_sum[2], 1, 2),
    )


def solution(mesh):
    everyone = ("dp", "expert")
    in_specs = (
        P("dp", "expert", None),
        P("dp", "expert", None),
        P("dp", None),
        P("dp", "expert", None),
        P(everyone, None),
        P(None, everyone),
        P(everyone, None),
        P(everyone, None),
        P(None, everyone),
        P(everyone, None),
        P(None, everyone),
        P("expert", "dp", None),
        P("expert", "dp", None),
        P("expert", None, "dp"),
    )
    out_specs = (
        P("dp", "expert", None),
        P("dp", "expert", None),
        P(everyone, None),
        P(None, everyone),
        P(everyone, None),
        P(everyone, None),
        P(None, everyone),
        P(everyone, None),
        P(None, everyone),
        P("expert", "dp", None),
        P("expert", "dp", None),
        P("expert", None, "dp"),
    )
    return jax.shard_map(local, mesh=mesh, in_specs=in_specs, out_specs=out_specs, check_vma=False)
```

```python
import functools

import jax
import jax.numpy as jnp
from jax import lax
from jax.experimental import pallas as pl
from jax.experimental.pallas import tpu as pltpu
from jax.sharding import PartitionSpec as P

H = 10
HD = 128
TOP = 7
EXP_DEV = 2
EPS = 1e-06
NEG = -1e30
BF = jnp.bfloat16
F32 = jnp.float32
VMEM_LIMIT = 56 * 1024 * 1024
MOE_VMEM = 62 * 1024 * 1024


def params(**kw):
    return pltpu.CompilerParams(vmem_limit_bytes=VMEM_LIMIT, **kw)


def nn(a, b):
    return jnp.dot(a, b, preferred_element_type=F32)


def nt(a, b):
    return lax.dot_general(a, b, (((1,), (1,)), ((), ())), preferred_element_type=F32)


def tn(a, b):
    return lax.dot_general(a, b, (((0,), (0,)), ((), ())), preferred_element_type=F32)


def doc_starts_of(lengths, places):
    doc_ends = jnp.cumsum(lengths)
    doc_starts = doc_ends - lengths
    total = doc_ends[-1]
    doc_index = jnp.sum((places[:, None] >= doc_ends[None, :]).astype(jnp.int32), axis=1)
    live = places < total
    matches = doc_index[:, None] == jnp.arange(lengths.shape[0], dtype=jnp.int32)[None, :]
    first = jnp.sum(jnp.where(matches, doc_starts[None, :], 0), axis=1)
    return jnp.where(live, first, places), places - jnp.where(live, first, total)


def turn_tables(rope_pos):
    half = HD // 2
    frequency = 10000.0 ** (-jnp.arange(half, dtype=F32) / half)
    angles = rope_pos.astype(F32)[:, None] * frequency[None, :]
    cosine = jnp.cos(angles)
    sine = jnp.sin(angles)
    return (
        jnp.concatenate([cosine, cosine], axis=1),
        jnp.concatenate([-sine, sine], axis=1),
    )


def inverse_rms(values):
    return lax.rsqrt(jnp.mean(values * values, axis=-1, keepdims=True) + EPS)


MESH = pl.DeviceIdType.MESH


def sent(src, dst, send_sem, recv_sem, device):
    return pltpu.make_async_remote_copy(
        src_ref=src,
        dst_ref=dst,
        send_sem=send_sem,
        recv_sem=recv_sem,
        device_id=device,
        device_id_type=MESH,
    )


class Place:
    def __init__(self, chips):
        self.d = lax.axis_index("dp")
        self.e = lax.axis_index("expert")
        self.z = self.e // 2
        self.c = self.e % 2
        self.y = self.d // 2
        self.x = self.d % 2
        self.chips = chips
        self.sibling = (self.d, self.e + 1 - 2 * self.c)
        self.across_x = (self.d + 1 - 2 * self.x, self.e)
        self.across_y = (self.d + 2 - 4 * self.y, self.e)
        self.up = (self.d, self.e + 2)
        self.down = (self.d, self.e - 2)


def greet(devices, conditions):
    barrier = pltpu.get_barrier_semaphore()
    count = 0
    for device, condition in zip(devices, conditions):
        if condition is None:
            pl.semaphore_signal(barrier, inc=1, device_id=device, device_id_type=MESH)
            count = count + 1
        else:

            @pl.when(condition)
            def _(device=device):
                pl.semaphore_signal(barrier, inc=1, device_id=device, device_id_type=MESH)

            count = count + condition.astype(jnp.int32)
    pl.semaphore_wait(barrier, count)


def gather_kernel(chips, n_full, n_chain, *refs):
    n = n_full + n_chain
    ins, outs, sems = refs[:n], refs[n : 2 * n], refs[2 * n :]
    at = Place(chips)
    chain = 2 * chips
    z, c = at.z, at.c
    has_up, has_down = z < chips - 1, z > 0
    devices = [at.sibling, at.up, at.down]
    conditions = [None, has_up, has_down]
    if n_full:
        devices += [at.across_x, at.across_y]
        conditions += [None, None]
    greet(devices, conditions)
    x_dp, y_dp = at.across_x[0], at.across_y[0]
    far_dp = 3 - at.d

    class Array:
        pass

    arrays = []
    position = 0
    for i in range(n):
        a = Array()
        a.full = i < n_full
        a.own, a.out = ins[i], outs[i]
        a.local, a.s_chain, a.r_chain, a.s_core, a.r_core = sems[position : position + 5]
        position += 5
        if a.full:
            a.s_side, a.r_side, a.s_half, a.r_half = sems[position : position + 4]
            position += 4
            cut = a.own.shape[-1] // 256 * 128
            a.halves = (pl.ds(0, cut), pl.ds(cut, a.own.shape[-1] - cut))
        arrays.append(a)

    def slot(a, dd, zz, cc):
        return a.out.at[dd * chain + 2 * zz + cc] if a.full else a.out.at[2 * zz + cc]

    def core_index(a, dd, zz):
        return dd * chips + zz if a.full else zz

    def to_core(a, dd, zz, src=None):
        ref = slot(a, dd, zz, c)
        k = core_index(a, dd, zz)
        return sent(ref if src is None else src, ref, a.s_core.at[k], a.r_core.at[k], at.sibling)

    def from_core(a, dd, zz):
        ref = slot(a, dd, zz, 1 - c)
        k = core_index(a, dd, zz)
        return sent(ref, ref, a.s_core.at[k], a.r_core.at[k], at.sibling)

    def along(a, zz, direction, src=None):
        ref = slot(a, at.d, zz, c)
        device = at.up if direction == 0 else at.down
        return sent(ref if src is None else src, ref, a.s_chain.at[direction, zz], a.r_chain.at[zz], device)

    def side(a, dd, zz, axis, src=None):
        ref = slot(a, dd, zz, c)
        device = at.across_x if axis == 0 else at.across_y
        return sent(
            ref if src is None else src, ref, a.s_side.at[axis, zz], a.r_side.at[axis, zz], device
        )

    def half(a, dd, zz, which):
        ref = slot(a, dd, zz, c).at[:, a.halves[which]]
        device = at.across_y if which == 0 else at.across_x
        return sent(ref, ref, a.s_half.at[which, zz], a.r_half.at[which, zz], device)

    def present(zz):
        return (zz >= 0) & (zz < chips)

    def block_here(zz, distance, direction):
        for a in arrays:
            along(a, zz, direction).wait_recv()
            if direction == 0:

                @pl.when(has_up)
                def _(a=a):
                    along(a, zz, 0).start()
            else:

                @pl.when(has_down)
                def _(a=a):
                    along(a, zz, 1).start()

            if a.full:
                side(a, at.d, zz, 0).start()
                side(a, at.d, zz, 1).start()
            to_core(a, at.d, zz).start()

    def side_here(zz):
        for a in arrays[:n_full]:
            side(a, x_dp, zz, 0).wait_recv()
            half(a, x_dp, zz, 0).start()
            to_core(a, x_dp, zz).start()
            side(a, y_dp, zz, 1).wait_recv()
            half(a, y_dp, zz, 1).start()
            to_core(a, y_dp, zz).start()

    def far_here(zz):
        for a in arrays[:n_full]:
            half(a, far_dp, zz, 0).wait_recv()
            half(a, far_dp, zz, 1).wait_recv()
            to_core(a, far_dp, zz).start()

    for a in arrays:

        @pl.when(has_up)
        def _(a=a):
            along(a, z, 0, a.own).start()

        @pl.when(has_down)
        def _(a=a):
            along(a, z, 1, a.own).start()

        if a.full:
            side(a, at.d, z, 0, a.own).start()
            side(a, at.d, z, 1, a.own).start()
        to_core(a, at.d, z, a.own).start()
    for a in arrays:
        pltpu.make_async_copy(a.own, slot(a, at.d, z, c), a.local).start()

    def at_distance(k, fn):
        @pl.when((k >= 0) & present(z - k))
        def _():
            fn(z - k)

        @pl.when((k >= 1) & present(z + k))
        def _():
            fn(z + k)

    def step(k, carry):
        @pl.when(present(z - k))
        def _():
            block_here(z - k, k, 0)

        @pl.when(present(z + k))
        def _():
            block_here(z + k, k, 1)

        if n_full:
            at_distance(k - 1, side_here)
            at_distance(k - 2, far_here)
        return carry

    lax.fori_loop(1, chips + (2 if n_full else 0), step, 0)

    def finish(zz, carry):
        for a in arrays:
            for dd in range(4) if a.full else (0,):
                from_core(a, dd, zz).wait_recv()
                to_core(a, dd, zz).wait_send()

            @pl.when((zz <= z) & has_up)
            def _(a=a):
                along(a, zz, 0).wait_send()

            @pl.when((zz >= z) & has_down)
            def _(a=a):
                along(a, zz, 1).wait_send()

            if a.full:
                for axis in (0, 1):
                    side(a, at.d, zz, axis).wait_send()
                half(a, x_dp, zz, 0).wait_send()
                half(a, y_dp, zz, 1).wait_send()
        return carry

    lax.fori_loop(0, chips, finish, 0)
    for a in arrays:
        pltpu.make_async_copy(a.own, slot(a, at.d, z, c), a.local).wait()


def gather(full, chained, collective_id):
    chain = lax.axis_size("expert")
    chips = chain // 2
    spread = lax.axis_size("dp")
    assert spread == 4 and chain % 2 == 0
    dma = pltpu.SemaphoreType.DMA
    scratch = []
    for array in full:
        scratch += [dma, dma((2, chips)), dma((chips,)), dma((4 * chips,)), dma((4 * chips,))]
        scratch += [dma((2, chips))] * 4
    for array in chained:
        scratch += [dma, dma((2, chips)), dma((chips,)), dma((chips,)), dma((chips,))]
    shapes = [jax.ShapeDtypeStruct((spread * chain,) + a.shape, a.dtype) for a in full]
    shapes += [jax.ShapeDtypeStruct((chain,) + a.shape, a.dtype) for a in chained]
    n = len(full) + len(chained)
    moved = sum(s.size * s.dtype.itemsize for s in shapes)
    return pl.pallas_call(
        functools.partial(gather_kernel, chips, len(full), len(chained)),
        out_shape=shapes,
        in_specs=[pl.BlockSpec(memory_space=pl.ANY)] * n,
        out_specs=[pl.BlockSpec(memory_space=pl.ANY)] * n,
        scratch_shapes=scratch,
        compiler_params=params(collective_id=collective_id, has_side_effects=True),
        cost_estimate=pl.CostEstimate(flops=0, bytes_accessed=16 * moved, transcendentals=0),
    )(*full, *chained)


def to_owner_kernel(chips, wide_ref, thin_ref, out_ref, thin_out, mine, other, came, sems_in, s_core, r_core, s_chain, r_chain, s_thin, r_thin):
    at = Place(chips)
    chain = 2 * chips
    z, c = at.z, at.c
    devices = [(at.d, lax.rem(at.e + k, chain)) for k in range(1, chain)]
    greet(devices, [None] * (chain - 1))

    def load(zz):
        return pltpu.make_async_copy(wide_ref.at[2 * zz + c], mine.at[zz], sems_in.at[zz])

    def to_core(zz):
        return sent(
            wide_ref.at[2 * zz + 1 - c], other.at[zz], s_core.at[zz], r_core.at[zz], at.sibling
        )

    def thin(k):
        target = lax.rem(at.e + k, chain)
        return sent(
            thin_ref.at[target], thin_out.at[at.e], s_thin.at[k], r_thin.at[k], (at.d, target)
        )

    def over(k):
        zz = lax.rem(z + k, chips)
        return sent(
            mine.at[zz], came.at[k], s_chain.at[k], r_chain.at[k], (at.d, 2 * zz + c)
        )

    order = [lax.rem(z + k, chips) for k in range(1, chips)] + [z]
    for zz in order:
        to_core(zz).start()
        load(zz).start()
    for k in range(1, chain):
        thin(k).start()
    own_thin = pltpu.make_async_copy(thin_ref.at[at.e], thin_out.at[at.e], s_thin.at[0])
    own_thin.start()
    for k, zz in enumerate(order):
        to_core(zz).wait_recv()
        load(zz).wait()
        total = mine[zz].astype(F32) + other[zz].astype(F32)
        if k < chips - 1:
            mine[zz] = total.astype(BF)
            over(k + 1).start()
        else:
            out_ref[...] = total
    for k in range(1, chips):
        over(k).wait_recv()
        out_ref[...] += came[k].astype(F32)
    for k in range(1, chips):
        over(k).wait_send()
    for zz in order:
        to_core(zz).wait_send()
    own_thin.wait()
    for k in range(1, chain):
        thin(k).wait()


def to_owner(wide, thin, collective_id):
    chain, rows, width = wide.shape
    chips = chain // 2
    dma = pltpu.SemaphoreType.DMA
    return pl.pallas_call(
        functools.partial(to_owner_kernel, chips),
        out_shape=[
            jax.ShapeDtypeStruct((rows, width), F32),
            jax.ShapeDtypeStruct(thin.shape, thin.dtype),
        ],
        in_specs=[pl.BlockSpec(memory_space=pl.ANY), pl.BlockSpec(memory_space=pltpu.VMEM)],
        out_specs=[pl.BlockSpec(memory_space=pltpu.VMEM), pl.BlockSpec(memory_space=pltpu.VMEM)],
        scratch_shapes=[
            pltpu.VMEM((chips, rows, width), BF),
            pltpu.VMEM((chips, rows, width), BF),
            pltpu.VMEM((chips, rows, width), BF),
            dma((chips,)),
            dma((chips,)),
            dma((chips,)),
            dma((chips,)),
            dma((chips,)),
            dma((chain,)),
            dma((chain,)),
        ],
        compiler_params=params(collective_id=collective_id, has_side_effects=True),
        cost_estimate=pl.CostEstimate(
            flops=0, bytes_accessed=16 * wide.size * 2, transcendentals=0
        ),
    )(wide, thin)


def sum_dense_kernel(chips, chunks, n_in, *refs):
    ins, outs = refs[:n_in], refs[n_in : 2 * n_in]
    n_chunks = len(chunks)
    rest = refs[2 * n_in :]
    sems = rest[:10]
    s_in, s_core, r_core, s_one, r_one, s_two, r_two, s_end, r_end = sems[:9]
    buffers = rest[9:]
    at = Place(chips)
    z, c, x, y = at.z, at.c, at.x, at.y
    others = [(at.d, 2 * lax.rem(z + k, chips) + c) for k in range(1, chips)]
    devices = [at.sibling, at.across_x, at.across_y] + others
    greet(devices, [None] * len(devices))

    class Chunk:
        def __init__(self, q):
            i, first, wide = chunks[q]
            self.i, self.first, self.wide = i, first, wide
            self.q = q
            self.mine, self.other, one_x, one_y, two_x, two_y, self.end = buffers[7 * q : 7 * q + 7]
            self.one, self.two = (one_x, one_y), (two_x, two_y)
            self.cols = pl.ds(first, wide)
            cut = wide // 256 * 128
            self.half = (pl.ds(0, cut), pl.ds(cut, wide - cut))

        def load(self):
            return pltpu.make_async_copy(
                ins[self.i].at[:, :, :, c, :, self.cols], self.mine, s_in.at[self.q]
            )

        def core(self):
            return sent(
                ins[self.i].at[:, :, :, 1 - c, :, self.cols],
                self.other,
                s_core.at[self.q],
                r_core.at[self.q],
                at.sibling,
            )

        def first_x(self):
            return sent(
                self.mine.at[:, 1 - x, :, :, self.half[0]],
                self.one[0],
                s_one.at[self.q, 0],
                r_one.at[self.q, 0],
                at.across_x,
            )

        def first_y(self):
            return sent(
                self.mine.at[1 - y, :, :, :, self.half[1]],
                self.one[1],
                s_one.at[self.q, 1],
                r_one.at[self.q, 1],
                at.across_y,
            )

        def second_y(self):
            return sent(
                self.mine.at[1 - y, x, :, :, self.half[0]],
                self.two[0],
                s_two.at[self.q, 0],
                r_two.at[self.q, 0],
                at.across_y,
            )

        def second_x(self):
            return sent(
                self.mine.at[y, 1 - x, :, :, self.half[1]],
                self.two[1],
                s_two.at[self.q, 1],
                r_two.at[self.q, 1],
                at.across_x,
            )

        def last(self, k):
            zz = lax.rem(z + k, chips)
            return sent(
                self.mine.at[y, x, zz],
                self.end.at[k - 1],
                s_end.at[self.q, k - 1],
                r_end.at[self.q, k - 1],
                (at.d, 2 * zz + c),
            )

    parts = [Chunk(q) for q in range(n_chunks)]

    def add(ref, place, more):
        ref[place] = (ref[place].astype(F32) + more.astype(F32)).astype(BF)

    def stage_one(p):
        p.core().wait_recv()
        p.load().wait()

        def body(k, carry):
            yy, xx, zz = k // (2 * chips), (k // chips) % 2, k % chips
            p.mine[yy, xx, zz] = (
                p.mine[yy, xx, zz].astype(F32) + p.other[yy, xx, zz].astype(F32)
            ).astype(BF)
            return carry

        lax.fori_loop(0, 4 * chips, body, 0)
        p.first_x().start()
        p.first_y().start()

    def stage_two(p):
        p.first_x().wait_recv()
        p.first_y().wait_recv()

        def body(k, carry):
            v, zz = k // chips, k % chips
            a, b = p.half
            p.mine[v, x, zz, :, a] = (
                p.mine[v, x, zz, :, a].astype(F32) + p.one[0][v, zz].astype(F32)
            ).astype(BF)
            p.mine[y, v, zz, :, b] = (
                p.mine[y, v, zz, :, b].astype(F32) + p.one[1][v, zz].astype(F32)
            ).astype(BF)
            return carry

        lax.fori_loop(0, 2 * chips, body, 0)
        p.second_y().start()
        p.second_x().start()

    def stage_three(p):
        p.second_y().wait_recv()
        p.second_x().wait_recv()

        def body(zz, carry):
            for w in (0, 1):
                s = p.half[w]
                p.mine[y, x, zz, :, s] = (
                    p.mine[y, x, zz, :, s].astype(F32) + p.two[w][zz].astype(F32)
                ).astype(BF)
            return carry

        lax.fori_loop(0, chips, body, 0)
        for k in range(1, chips):
            p.last(k).start()

    def stage_four(p):
        total = p.mine[y, x, z].astype(F32)
        for k in range(1, chips):
            p.last(k).wait_recv()
            total = total + p.end[k - 1].astype(F32)
        outs[p.i][:, p.first : p.first + p.wide] = total

    for p in parts:
        p.core().start()
        p.load().start()
    stages = (stage_one, stage_two, stage_three, stage_four)
    for t in range(n_chunks + len(stages) - 1):
        for s, stage in enumerate(stages):
            if 0 <= t - s < n_chunks:
                stage(parts[t - s])
    for p in parts:
        p.core().wait_send()
        p.first_x().wait_send()
        p.first_y().wait_send()
        p.second_x().wait_send()
        p.second_y().wait_send()
        for k in range(1, chips):
            p.last(k).wait_send()


def sum_dense(arrays, chunk_widths, collective_id):
    chain = lax.axis_size("expert")
    chips = chain // 2
    assert lax.axis_size("dp") == 4
    block = arrays[0].shape[0] // (4 * chain)
    dma = pltpu.SemaphoreType.DMA
    chunks = []
    for i, (array, wide) in enumerate(zip(arrays, chunk_widths)):
        assert array.shape[1] % wide == 0 and wide % 128 == 0 and wide >= 256
        chunks += [(i, first, wide) for first in range(0, array.shape[1], wide)]
    q = len(chunks)
    scratch = [dma((q,)), dma((q,)), dma((q,))] + [dma((q, 2))] * 4 + [dma((q, max(1, chips - 1)))] * 2
    for i, first, wide in chunks:
        cut = wide // 256 * 128
        scratch += [
            pltpu.VMEM((2, 2, chips, block, wide), BF),
            pltpu.VMEM((2, 2, chips, block, wide), BF),
            pltpu.VMEM((2, chips, block, cut), BF),
            pltpu.VMEM((2, chips, block, wide - cut), BF),
            pltpu.VMEM((chips, block, cut), BF),
            pltpu.VMEM((chips, block, wide - cut), BF),
            pltpu.VMEM((max(1, chips - 1), block, wide), BF),
        ]
    n = len(arrays)
    return pl.pallas_call(
        functools.partial(sum_dense_kernel, chips, tuple(chunks), n),
        out_shape=[jax.ShapeDtypeStruct((block, a.shape[1]), F32) for a in arrays],
        in_specs=[pl.BlockSpec(memory_space=pl.ANY)] * n,
        out_specs=[pl.BlockSpec(memory_space=pltpu.VMEM)] * n,
        scratch_shapes=scratch,
        compiler_params=params(collective_id=collective_id, has_side_effects=True),
        cost_estimate=pl.CostEstimate(
            flops=0, bytes_accessed=16 * sum(a.size for a in arrays), transcendentals=0
        ),
    )(*[a.reshape(2, 2, chips, 2, block, a.shape[1]) for a in arrays])


def qkv_kernel(per_block, x_ref, w_ref, cos_ref, sin_ref, o_ref):
    column = pl.program_id(1)
    product = nn(x_ref[...], w_ref[...])
    for k in range(per_block):
        part = product[:, k * HD : (k + 1) * HD]
        head = column * per_block + k
        turned = part * cos_ref[...] + pltpu.roll(part, HD // 2, 1) * sin_ref[...]
        o_ref[:, k * HD : (k + 1) * HD] = jnp.where(head < 2 * H, turned, part).astype(BF)


def project_qkv(normed, weight, cosine, sine):
    rows, width = normed.shape
    columns = weight.shape[1]
    per_block = 2
    tile_m = min(rows, 1536)
    return pl.pallas_call(
        functools.partial(qkv_kernel, per_block),
        out_shape=jax.ShapeDtypeStruct((rows, columns), BF),
        grid=(rows // tile_m, columns // (per_block * HD)),
        in_specs=[
            pl.BlockSpec((tile_m, width), lambda m, n: (m, 0)),
            pl.BlockSpec((width, per_block * HD), lambda m, n: (0, n)),
            pl.BlockSpec((tile_m, HD), lambda m, n: (m, 0)),
            pl.BlockSpec((tile_m, HD), lambda m, n: (m, 0)),
        ],
        out_specs=pl.BlockSpec((tile_m, per_block * HD), lambda m, n: (m, n)),
        compiler_params=params(),
        cost_estimate=pl.CostEstimate(
            flops=2 * rows * width * columns,
            bytes_accessed=2 * (rows * width + width * columns + rows * columns),
            transcendentals=0,
        ),
    )(normed, weight, cosine, sine)


def attend_kernel(scale, me_ref, q_ref, k_ref, v_ref, first_ref, o_ref, log_ref, bias):
    rows, keys = bias.shape

    @pl.when(pl.program_id(0) == 0)
    def _():
        key_place = lax.broadcasted_iota(jnp.int32, (rows, keys), 1)
        query_place = me_ref[0] * rows + lax.broadcasted_iota(jnp.int32, (rows, keys), 0)
        allowed = (key_place <= query_place) & (key_place >= first_ref[...])
        bias[...] = jnp.where(allowed, 0.0, NEG)

    scores = nt(q_ref[...], k_ref[...]) * scale + bias[...]
    top = jnp.max(scores, axis=-1, keepdims=True)
    weights = jnp.exp(scores - top)
    total = jnp.sum(weights, axis=-1, keepdims=True)
    o_ref[...] = nn(weights.astype(BF), v_ref[...]) / total
    log_ref[...] = jnp.broadcast_to(top + jnp.log(total), (rows, 8))[None]


def attend(me, qkv, first_own):
    keys = qkv.shape[0]
    rows = first_own.shape[0]
    return pl.pallas_call(
        functools.partial(attend_kernel, HD**-0.5),
        out_shape=[
            jax.ShapeDtypeStruct((rows, H * HD), F32),
            jax.ShapeDtypeStruct((H, rows, 8), F32),
        ],
        grid_spec=pltpu.PrefetchScalarGridSpec(
            num_scalar_prefetch=1,
            grid=(H,),
            in_specs=[
                pl.BlockSpec((rows, HD), lambda h, me: (me[0], h)),
                pl.BlockSpec((keys, HD), lambda h, me: (0, H + h)),
                pl.BlockSpec((keys, HD), lambda h, me: (0, 2 * H + h)),
                pl.BlockSpec((rows, 1), lambda h, me: (0, 0)),
            ],
            out_specs=[
                pl.BlockSpec((rows, HD), lambda h, me: (0, h)),
                pl.BlockSpec((1, rows, 8), lambda h, me: (h, 0, 0)),
            ],
            scratch_shapes=[pltpu.VMEM((rows, keys), F32)],
        ),
        compiler_params=params(),
        cost_estimate=pl.CostEstimate(
            flops=4 * rows * keys * H * HD,
            bytes_accessed=4 * keys * H * HD,
            transcendentals=H * rows * keys,
        ),
    )(me, qkv, qkv, qkv, first_own[:, None])


def attend_back_kernel(
    scale,
    me_ref,
    q_ref,
    k_ref,
    v_ref,
    qa_ref,
    ko_ref,
    vo_ref,
    do_ref,
    da_ref,
    log_ref,
    delta_ref,
    loga_ref,
    deltaa_ref,
    first_ref,
    firsta_ref,
    cos_ref,
    sin_ref,
    o_ref,
    bias,
    biast,
):
    rows, keys = bias.shape

    @pl.when(pl.program_id(0) == 0)
    def _():
        place = lax.broadcasted_iota(jnp.int32, (rows, keys), 1)
        own = me_ref[0] * rows + lax.broadcasted_iota(jnp.int32, (rows, keys), 0)
        bias[...] = jnp.where((place <= own) & (place >= first_ref[...]), 0.0, NEG)
        biast[...] = jnp.where((own <= place) & (own >= firsta_ref[...]), 0.0, NEG)

    def unturn(value):
        return value * cos_ref[...] - pltpu.roll(value, HD // 2, 1) * sin_ref[...]

    log_own = log_ref[0][:, :1]
    delta_own = delta_ref[0][:, :1]
    weights = jnp.exp(nt(q_ref[...], k_ref[...]) * scale + bias[...] - log_own)
    back = nt(do_ref[...], v_ref[...])
    grad = (weights * (back - delta_own) * scale).astype(BF)
    o_ref[0] = unturn(nn(grad, k_ref[...])).astype(BF)

    weights = jnp.exp(nt(ko_ref[...], qa_ref[...]) * scale + biast[...] - loga_ref[0])
    o_ref[2] = nn(weights.astype(BF), da_ref[...]).astype(BF)
    back = nt(vo_ref[...], da_ref[...])
    grad = (weights * (back - deltaa_ref[0]) * scale).astype(BF)
    o_ref[1] = unturn(nn(grad, qa_ref[...])).astype(BF)


def attend_back(me, qkv, grad_own, grad_all, log_own, delta_own, log_all, delta_all, first, cosine, sine):
    keys = qkv.shape[0]
    rows = grad_own.shape[0]
    first_own, first_all = first
    return pl.pallas_call(
        functools.partial(attend_back_kernel, HD**-0.5),
        out_shape=jax.ShapeDtypeStruct((3, rows, H * HD), BF),
        grid_spec=pltpu.PrefetchScalarGridSpec(
            num_scalar_prefetch=1,
            grid=(H,),
            in_specs=[
                pl.BlockSpec((rows, HD), lambda h, me: (me[0], h)),
                pl.BlockSpec((keys, HD), lambda h, me: (0, H + h)),
                pl.BlockSpec((keys, HD), lambda h, me: (0, 2 * H + h)),
                pl.BlockSpec((keys, HD), lambda h, me: (0, h)),
                pl.BlockSpec((rows, HD), lambda h, me: (me[0], H + h)),
                pl.BlockSpec((rows, HD), lambda h, me: (me[0], 2 * H + h)),
                pl.BlockSpec((rows, HD), lambda h, me: (0, h)),
                pl.BlockSpec((keys, HD), lambda h, me: (0, h)),
                pl.BlockSpec((1, rows, 8), lambda h, me: (h, 0, 0)),
                pl.BlockSpec((1, rows, 8), lambda h, me: (h, 0, 0)),
                pl.BlockSpec((1, 1, keys), lambda h, me: (h, 0, 0)),
                pl.BlockSpec((1, 1, keys), lambda h, me: (h, 0, 0)),
                pl.BlockSpec((rows, 1), lambda h, me: (0, 0)),
                pl.BlockSpec((1, keys), lambda h, me: (0, 0)),
                pl.BlockSpec((rows, HD), lambda h, me: (0, 0)),
                pl.BlockSpec((rows, HD), lambda h, me: (0, 0)),
            ],
            out_specs=pl.BlockSpec((3, rows, HD), lambda h, me: (0, 0, h)),
            scratch_shapes=[pltpu.VMEM((rows, keys), F32)] * 2,
        ),
        compiler_params=params(),
        cost_estimate=pl.CostEstimate(
            flops=14 * rows * keys * H * HD,
            bytes_accessed=8 * keys * H * HD,
            transcendentals=2 * H * rows * keys,
        ),
    )(
        me,
        qkv,
        qkv,
        qkv,
        qkv,
        qkv,
        qkv,
        grad_own,
        grad_all,
        log_own,
        delta_own,
        log_all,
        delta_all,
        first_own[:, None],
        first_all[None, :],
        cosine,
        sine,
    )


def moe_kernel(
    chips,
    experts,
    x_own,
    routes,
    grads,
    misc,
    weights,
    row_out,
    thin_out,
    mid_out,
    grad_out,
    x_all,
    g_all,
    w,
    hid,
    part,
    other,
    came,
    thin,
    dots,
    s_load,
    s_x,
    r_x,
    s_fwd,
    r_fwd,
    s_part,
    r_part,
    s_came,
    r_came,
    s_thin,
    r_thin,
):
    at = Place(chips)
    z, c = at.z, at.c
    chain = 2 * chips
    rows, width = x_own.shape
    both = w.shape[2]
    tiles = both // 256
    per_expert = both // 256
    greet([(at.d, lax.rem(at.e + k, chain)) for k in range(1, chain)], [None] * (chain - 1))

    near = jnp.minimum(z, chips - 1 - z)

    def order(j):
        step = (j + 1) // 2
        around = jnp.where(j % 2 == 1, z - step, z + step)
        return jnp.where(j <= 2 * near, around, jnp.where(2 * z < chips, j, chips - 1 - j))

    def own_load():
        return pltpu.make_async_copy(x_own, x_all.at[z, c], s_load.at[0])

    hidden = both // EXP_DEV

    def weight_load(k, e):
        return pltpu.make_async_copy(
            weights.at[k, e], w.at[k, :, pl.ds(e * hidden, hidden)], s_load.at[2 + 2 * k + e]
        )

    def grad_store(k, e):
        return pltpu.make_async_copy(
            w.at[k, :, pl.ds(e * hidden, hidden)], grad_out.at[k, e], s_load.at[2 + 2 * k + e]
        )

    def grads_load():
        return pltpu.make_async_copy(grads, g_all, s_load.at[1])

    def x_send(zz):
        return sent(x_own, x_all.at[z, c], s_x.at[zz], r_x.at[z], (at.d, 2 * zz + c))

    def x_came(zz):
        ref = x_all.at[zz, c]
        return sent(ref, ref, s_x.at[zz], r_x.at[zz], (at.d, 2 * zz + c))

    def forward(zz):
        ref = x_all.at[zz, c]
        return sent(ref, ref, s_fwd.at[zz], r_fwd.at[zz], at.sibling)

    def forwarded(zz):
        ref = x_all.at[zz, 1 - c]
        return sent(ref, ref, s_fwd.at[zz], r_fwd.at[zz], at.sibling)

    def part_send(zz):
        return sent(part.at[zz, 1 - c], other.at[zz], s_part.at[zz], r_part.at[zz], at.sibling)

    def came_send(zz):
        return sent(part.at[zz, c], came.at[z], s_came.at[zz], r_came.at[z], (at.d, 2 * zz + c))

    def came_here(zz):
        return sent(part.at[zz, c], came.at[zz], s_came.at[zz], r_came.at[zz], (at.d, 2 * zz + c))

    def thin_send(zz, cc):
        return sent(
            thin.at[zz], thin_out.at[at.e], s_thin.at[2 * zz + cc], r_thin.at[at.e], (at.d, 2 * zz + cc)
        )

    def thin_here(e):
        return sent(thin.at[0], thin_out.at[e], s_thin.at[e], r_thin.at[e], (at.d, e))

    own_load().start()
    sent(x_own, x_all.at[z, c], s_fwd.at[z], r_fwd.at[z], at.sibling).start()
    for j in range(1, chips):
        x_send(order(j)).start()
    for k in range(3):
        for e in range(EXP_DEV):
            weight_load(k, e).start()
    grads_load().start()
    own_load().wait()

    lanes = lax.broadcasted_iota(jnp.int32, (2 * rows, 128), 1)

    def gates_of(zz, x):
        logits = jnp.where(lanes < experts, nn(x, misc[...]), NEG)
        powers = jnp.exp(logits - jnp.max(logits, axis=1, keepdims=True))
        probs = powers / jnp.sum(powers, axis=1, keepdims=True)
        named = routes[zz][:, 0:1] == lanes
        for j in range(1, TOP):
            named = named | (routes[zz][:, j : j + 1] == lanes)
        chosen = jnp.where(named, probs, 0.0)
        gates = chosen / jnp.sum(chosen, axis=1, keepdims=True)
        return [
            jnp.sum(jnp.where(lanes == EXP_DEV * at.e + k, gates, 0.0), axis=1, keepdims=True)
            for k in range(EXP_DEV)
        ]

    def settle(zz):
        part_send(zz).wait_recv()
        total = part[zz, c].astype(F32) + other[zz].astype(F32)

        @pl.when(zz == z)
        def _():
            row_out[...] = total

        @pl.when(zz != z)
        def _():
            part[zz, c] = total.astype(BF)
            came_send(zz).start()

    def block(j, carry):
        zz = order(j)
        forwarded(zz).wait_recv()
        here = pl.ds(pl.multiple_of(zz * 2 * rows, 2 * rows), 2 * rows)
        x = x_all[zz].reshape(2 * rows, width)
        first, second = gates_of(zz, x)
        dots[...] = jnp.zeros_like(dots)

        @pl.when(j == 0)
        def _():
            for k in range(3):
                for e in range(EXP_DEV):
                    weight_load(k, e).wait()
            grads_load().wait()

        def tile(n, carry):
            cols = pl.ds(pl.multiple_of(n * 256, 256), 256)
            x = x_all[zz].reshape(2 * rows, width)
            g = g_all[zz].reshape(2 * rows, width)
            gate_v = nn(x, w[0, :, cols])
            up_v = nn(x, w[1, :, cols])
            back = nn(g, w[2, :, cols])
            for half in (0, 1):
                s = slice(half * 128, half * 128 + 128)
                is_first = 2 * n + half < per_expert
                gate = jnp.where(is_first, first, second)
                v, u, b = gate_v[:, s], up_v[:, s], back[:, s]
                sig = jax.nn.sigmoid(v)
                act = v * sig
                mid = act * u
                dots[0] += mid * b * is_first.astype(F32)
                dots[1] += mid * b * (1.0 - is_first.astype(F32))
                b = gate * b
                to = pl.ds(pl.multiple_of(n * 256 + half * 128, 128), 128)
                hid[2, here, to] = (gate * mid).astype(BF)
                hid[0, here, to] = (b * u * (sig * (1.0 + v * (1.0 - sig)))).astype(BF)
                hid[1, here, to] = (b * act).astype(BF)
            return carry

        early = (tiles + 1) // 2
        lax.fori_loop(0, early, tile, 0, unroll=True)

        @pl.when(j + 1 < chips)
        def _():
            x_came(order(j + 1)).wait_recv()
            forward(order(j + 1)).start()

        @pl.when(j > 0)
        def _():
            settle(order(j - 1))

        lax.fori_loop(early, tiles, tile, 0, unroll=True)

        def row_tile(n, carry):
            cols = pl.ds(pl.multiple_of(n * 256, 256), 256)
            row = nt(hid[0, here, :], w[0, cols, :]) + nt(hid[1, here, :], w[1, cols, :])
            part[zz, 0, :, cols] = row[:rows].astype(BF)
            part[zz, 1, :, cols] = row[rows:].astype(BF)
            return carry

        lax.fori_loop(0, width // 256, row_tile, 0, unroll=True)
        part_send(zz).start()
        column = jnp.where(
            lanes == 0,
            jnp.sum(dots[0], axis=1, keepdims=True),
            jnp.sum(dots[1], axis=1, keepdims=True),
        )
        thin[zz] = column.T[:8]

        @pl.when(zz == z)
        def _():
            thin_out[at.e] = thin[zz]

        for cc in (0, 1):

            @pl.when(2 * zz + cc != at.e)
            def _(cc=cc):
                thin_send(zz, cc).start()

        return carry

    lax.fori_loop(0, chips, block, 0)
    settle(order(chips - 1))
    mid_store = pltpu.make_async_copy(hid.at[2], mid_out, s_load.at[0])
    mid_store.start()
    for k in (2, 0, 1):

        def grad_tile(n, carry, k=k):
            cols = pl.ds(pl.multiple_of(n * 256, 256), 256)
            left = g_all if k == 2 else x_all
            left = left[...].reshape(chain * rows, width)
            w[k, :, cols] = tn(left, hid[k, :, cols]).astype(BF)
            return carry

        lax.fori_loop(0, tiles, grad_tile, 0, unroll=True)
        for e in range(EXP_DEV):
            grad_store(k, e).start()

    for zz in range(chips):

        @pl.when(zz != z)
        def _(zz=zz):
            came_here(zz).wait_recv()
            row_out[...] += came[zz].astype(F32)
            came_send(zz).wait_send()
            x_send(zz).wait_send()

        part_send(zz).wait_send()
        forward(zz).wait_send()
        for cc in (0, 1):

            @pl.when(2 * zz + cc != at.e)
            def _(zz=zz, cc=cc):
                thin_here(2 * zz + cc).wait_recv()
                thin_send(zz, cc).wait_send()

    mid_store.wait()
    for k in range(3):
        for e in range(EXP_DEV):
            grad_store(k, e).wait()


def moe_fused(normed, routes_all, grads_all, misc, weights, experts, collective_id):
    rows, width = normed.shape
    chain = routes_all.shape[0] // rows
    chips = chain // 2
    both = EXP_DEV * weights.shape[3]
    dma = pltpu.SemaphoreType.DMA
    blocks = (chips, 2, rows, width)
    anywhere = pl.BlockSpec(memory_space=pl.ANY)
    vmem = pl.BlockSpec(memory_space=pltpu.VMEM)
    return pl.pallas_call(
        functools.partial(moe_kernel, chips, experts),
        out_shape=[
            jax.ShapeDtypeStruct((rows, width), F32),
            jax.ShapeDtypeStruct((chain, 8, 2 * rows), F32),
            jax.ShapeDtypeStruct((chain * rows, both), BF),
            jax.ShapeDtypeStruct(weights.shape, BF),
        ],
        in_specs=[anywhere, vmem, anywhere, vmem, anywhere],
        out_specs=[vmem, vmem, anywhere, anywhere],
        scratch_shapes=[
            pltpu.VMEM(blocks, BF),
            pltpu.VMEM(blocks, BF),
            pltpu.VMEM((3, width, both), BF),
            pltpu.VMEM((3, chain * rows, both), BF),
            pltpu.VMEM(blocks, BF),
            pltpu.VMEM((chips, rows, width), BF),
            pltpu.VMEM((chips, rows, width), BF),
            pltpu.VMEM((chips, 8, 2 * rows), F32),
            pltpu.VMEM((2, 2 * rows, 128), F32),
            dma((8,)),
        ]
        + [dma((chips,))] * 8
        + [dma((chain,))] * 2,
        compiler_params=pltpu.CompilerParams(
            vmem_limit_bytes=MOE_VMEM, collective_id=collective_id, has_side_effects=True
        ),
        cost_estimate=pl.CostEstimate(
            flops=16 * chain * rows * width * both,
            bytes_accessed=4 * weights.size + 4 * chain * rows * both,
            transcendentals=chain * rows * both,
        ),
    )(
        normed,
        routes_all.reshape(chips, 2 * rows, TOP),
        grads_all.reshape(blocks),
        misc,
        weights,
    )


def moe_plain(moe_all, gates_here, grads_all, weights):
    keys, width = moe_all.shape
    hidden = weights.shape[3]
    at_once = 768 if keys % 768 == 0 else keys

    def some(rows):
        x, gates, g = rows
        row = jnp.zeros(x.shape, F32)
        dots, mids, gate_vs, up_vs = [], [], [], []
        for e in range(EXP_DEV):
            scale = gates[:, e : e + 1]
            gate_v = nn(x, weights[0, e])
            up_v = nn(x, weights[1, e])
            back = nn(g, weights[2, e])
            act, slope = silu_parts(gate_v)
            mid = act * up_v
            dots.append(jnp.sum(mid * back, axis=1))
            back = back * scale
            gate_vs.append((back * up_v * slope).astype(BF))
            up_vs.append((back * act).astype(BF))
            mids.append((mid * scale).astype(BF))
            row = row + nt(gate_vs[e], weights[0, e]) + nt(up_vs[e], weights[1, e])
        return (
            row.astype(BF),
            jnp.stack(dots, axis=1),
            jnp.concatenate(mids, axis=1),
            jnp.concatenate(gate_vs, axis=1),
            jnp.concatenate(up_vs, axis=1),
        )

    cut = jax.tree.map(
        lambda a: a.reshape((keys // at_once, at_once) + a.shape[1:]), (moe_all, gates_here, grads_all)
    )
    row, dots, mid, gate_v, up_v = jax.tree.map(
        lambda a: a.reshape((keys,) + a.shape[2:]), lax.map(some, cut)
    )

    def grad_of(x, h):
        grad = tn(x, h).astype(BF).reshape(width, EXP_DEV, hidden)
        return jnp.swapaxes(grad, 0, 1)

    weight_grads = jnp.stack(
        [grad_of(moe_all, gate_v), grad_of(moe_all, up_v), grad_of(grads_all, mid)]
    )
    return row, dots, mid, weight_grads


def spread_kernel(
    chips,
    own,
    side,
    mid,
    weights,
    rows_in,
    gate_in,
    up_in,
    cot_in,
    shared_in,
    attn_in,
    attended_in,
    all_out,
    side_out,
    mix_out,
    gate_out,
    up_out,
    down_out,
    out_out,
    mids,
    w,
    mix,
    dense,
    wide,
    s_load,
    s_dense,
    s_chain,
    r_chain,
    s_core,
    r_core,
    s_side,
    r_side,
    s_score,
    r_score,
):
    at = Place(chips)
    z, c = at.z, at.c
    hidden = gate_in.shape[1]
    rows = own.shape[0]
    others = [(at.d, 2 * lax.rem(z + k, chips) + c) for k in range(1, chips)]
    greet([at.sibling] + others, [None] * chips)

    pairs = ((own, all_out, s_chain, r_chain, s_core, r_core), (side, side_out, s_side, r_side, s_score, r_score))

    def along(p, k, src=None):
        source, out, ss, rs = pairs[p][:4]
        zz = lax.rem(z + k, chips)
        ref = out.at[2 * z + c]
        return sent(source if src is None else src, ref, ss.at[zz], rs.at[z], (at.d, 2 * zz + c))

    def along_here(p, zz):
        source, out, ss, rs = pairs[p][:4]
        ref = out.at[2 * zz + c]
        return sent(ref, ref, ss.at[zz], rs.at[zz], (at.d, 2 * zz + c))

    def over(p, zz, core, src=None):
        out, ss, rs = pairs[p][1], pairs[p][4], pairs[p][5]
        ref = out.at[2 * zz + core]
        return sent(ref if src is None else src, ref, ss.at[zz], rs.at[zz], at.sibling)

    near = jnp.minimum(z, chips - 1 - z)

    def order(j):
        step = (j + 1) // 2
        around = jnp.where(j % 2 == 1, z - step, z + step)
        return jnp.where(j <= 2 * near, around, jnp.where(2 * z < chips, j, chips - 1 - j))

    for j in range(1, chips):
        for p in (1, 0):
            along(p, lax.rem(order(j) - z + chips, chips)).start()
    locals_ = []
    for p in (1, 0):
        over(p, z, c, pairs[p][0]).start()
        copy = pltpu.make_async_copy(pairs[p][0], pairs[p][1].at[2 * z + c], s_load.at[p])
        copy.start()
        locals_.append(copy)
    loads = [
        pltpu.make_async_copy(weights.at[2, e], w.at[:, pl.ds(e * hidden, hidden)], s_load.at[2 + e])
        for e in range(EXP_DEV)
    ]
    loads.append(pltpu.make_async_copy(mid, mids, s_load.at[2 + EXP_DEV]))
    for copy in loads:
        copy.start()

    stores = []
    dense[0] = tn(rows_in[...], gate_in[...]).astype(BF)
    dense[1] = tn(rows_in[...], up_in[...]).astype(BF)
    dense[2] = tn(cot_in[...], shared_in[...]).astype(BF)
    wide[...] = tn(attn_in[...], attended_in[...]).astype(BF)
    for k, (src, dst) in enumerate(
        ((dense.at[0], gate_out), (dense.at[1], up_out), (dense.at[2], down_out), (wide, out_out))
    ):
        copy = pltpu.make_async_copy(src, dst, s_dense.at[k])
        copy.start()
        stores.append(copy)
    for copy in loads:
        copy.wait()

    def mix_chip(zz):
        here = pl.ds(zz * 2 * rows, 2 * rows)
        for n in range(0, own.shape[1], 256):
            tile = nt(mids[here, :], w[n : n + 256, :]).astype(BF)
            mix[zz, 0, :, n : n + 256] = tile[:rows]
            mix[zz, 1, :, n : n + 256] = tile[rows:]
        copy = pltpu.make_async_copy(mix.at[zz], mix_out.at[zz], s_dense.at[4 + zz])
        copy.start()
        stores.append(copy)

    for j in range(chips):
        mix_chip(j)
        if j >= 1:
            zz = order(j)
            for p in (1, 0):
                along_here(p, zz).wait_recv()
                over(p, zz, c).start()
    for p in (1, 0):
        for zz in range(chips):
            over(p, zz, 1 - c).wait_recv()
            over(p, zz, c).wait_send()

            @pl.when(zz != z)
            def _(p=p, zz=zz):
                along_here(p, zz).wait_send()

    for copy in locals_ + stores:
        copy.wait()


def spread(own, side, mid, weights, normed, gate_grad, up_grad, cot, shared_mid, attn, attended, collective_id):
    rows, width = own.shape
    keys, both = mid.shape
    chain = keys // rows
    chips = chain // 2
    hidden = gate_grad.shape[1]
    dma = pltpu.SemaphoreType.DMA
    anywhere = pl.BlockSpec(memory_space=pl.ANY)
    vmem = pl.BlockSpec(memory_space=pltpu.VMEM)
    return pl.pallas_call(
        functools.partial(spread_kernel, chips),
        out_shape=[
            jax.ShapeDtypeStruct((chain,) + own.shape, BF),
            jax.ShapeDtypeStruct((chain,) + side.shape, F32),
            jax.ShapeDtypeStruct((chips, 2, rows, width), BF),
            jax.ShapeDtypeStruct((width, hidden), BF),
            jax.ShapeDtypeStruct((width, hidden), BF),
            jax.ShapeDtypeStruct((width, hidden), BF),
            jax.ShapeDtypeStruct((width, width), BF),
        ],
        in_specs=[anywhere] * 4 + [vmem] * 7,
        out_specs=[anywhere] * 7,
        scratch_shapes=[
            pltpu.VMEM((keys, both), BF),
            pltpu.VMEM((width, both), BF),
            pltpu.VMEM((chips, 2, rows, width), BF),
            pltpu.VMEM((3, width, hidden), BF),
            pltpu.VMEM((width, width), BF),
            dma((3 + EXP_DEV,)),
            dma((4 + chips,)),
        ]
        + [dma((chips,))] * 8,
        compiler_params=params(collective_id=collective_id, has_side_effects=True),
        cost_estimate=pl.CostEstimate(
            flops=2 * keys * both * width, bytes_accessed=64 * keys * width, transcendentals=0
        ),
    )(own, side, mid, weights, normed, gate_grad, up_grad, cot, shared_mid, attn, attended)


def finish_kernel(chips, chunks, n_in, experts, *refs):
    ins = refs[:n_in]
    normed, projected, weight_in, misc_in, unit, inverse, gain, grad_middle, mix_in, base = refs[
        n_in : n_in + 10
    ]
    n_out = n_in + 2
    outs = refs[n_in + 10 : n_in + 10 + n_out]
    input_out, output_out = refs[n_in + 10 + n_out : n_in + 12 + n_out]
    rest = refs[n_in + 12 + n_out :]
    s_in, s_core, r_core, s_one, r_one, s_two, r_two, s_end, r_end = rest[:9]
    s_mix, s_mcore, r_mcore, s_mchain, r_mchain, s_weight = rest[9:15]
    weight, grad_ref, tile_ref, mix_mine, mix_other, mix_came = rest[15:21]
    buffers = rest[21:]
    n_chunks = len(chunks)
    at = Place(chips)
    z, c, x, y = at.z, at.c, at.x, at.y
    chain = 2 * chips
    others = [(at.d, 2 * lax.rem(z + k, chips) + c) for k in range(1, chips)]
    devices = [at.sibling, at.across_x, at.across_y] + others
    greet(devices, [None] * len(devices))

    class Chunk:
        def __init__(self, q):
            self.i, self.first, self.wide = chunks[q]
            self.q = q
            self.made = self.i >= n_in
            self.mine, self.other, one_x, one_y, two_x, two_y, self.end, self.give = buffers[
                8 * q : 8 * q + 8
            ]
            self.one, self.two = (one_x, one_y), (two_x, two_y)
            self.cols = pl.ds(self.first, self.wide)
            cut = self.wide // 256 * 128
            self.half = (pl.ds(0, cut), pl.ds(cut, self.wide - cut))

        def load(self):
            return pltpu.make_async_copy(
                ins[self.i].at[:, :, :, c, :, self.cols], self.mine, s_in.at[self.q]
            )

        def core(self):
            source = self.give if self.made else ins[self.i].at[:, :, :, 1 - c, :, self.cols]
            return sent(source, self.other, s_core.at[self.q], r_core.at[self.q], at.sibling)

        def first_x(self):
            return sent(
                self.mine.at[:, 1 - x, :, :, self.half[0]],
                self.one[0],
                s_one.at[self.q, 0],
                r_one.at[self.q, 0],
                at.across_x,
            )

        def first_y(self):
            return sent(
                self.mine.at[1 - y, :, :, :, self.half[1]],
                self.one[1],
                s_one.at[self.q, 1],
                r_one.at[self.q, 1],
                at.across_y,
            )

        def second_y(self):
            return sent(
                self.mine.at[1 - y, x, :, :, self.half[0]],
                self.two[0],
                s_two.at[self.q, 0],
                r_two.at[self.q, 0],
                at.across_y,
            )

        def second_x(self):
            return sent(
                self.mine.at[y, 1 - x, :, :, self.half[1]],
                self.two[1],
                s_two.at[self.q, 1],
                r_two.at[self.q, 1],
                at.across_x,
            )

        def last(self, k):
            zz = lax.rem(z + k, chips)
            return sent(
                self.mine.at[y, x, zz],
                self.end.at[k - 1],
                s_end.at[self.q, k - 1],
                r_end.at[self.q, k - 1],
                (at.d, 2 * zz + c),
            )

        def take(self):
            block = self.mine.shape[3]

            def body(k, carry):
                yy, xx, zz = k // (2 * chips), (k // chips) % 2, k % chips
                row = (2 * yy + xx) * chain + 2 * zz
                keep = pl.ds(pl.multiple_of((row + c) * block, block), block)
                away = pl.ds(pl.multiple_of((row + 1 - c) * block, block), block)
                self.mine[yy, xx, zz] = tile_ref[keep, : self.wide].astype(BF)
                self.give[yy, xx, zz] = tile_ref[away, : self.wide].astype(BF)
                return carry

            lax.fori_loop(0, 4 * chips, body, 0)
            self.core().start()

    parts = [Chunk(q) for q in range(n_chunks)]

    def stage_one(p):
        p.core().wait_recv()
        if not p.made:
            p.load().wait()

        def body(k, carry):
            yy, xx, zz = k // (2 * chips), (k // chips) % 2, k % chips
            p.mine[yy, xx, zz] = (
                p.mine[yy, xx, zz].astype(F32) + p.other[yy, xx, zz].astype(F32)
            ).astype(BF)
            return carry

        lax.fori_loop(0, 4 * chips, body, 0)
        p.first_x().start()
        p.first_y().start()

    def stage_two(p):
        p.first_x().wait_recv()
        p.first_y().wait_recv()

        def body(k, carry):
            v, zz = k // chips, k % chips
            a, b = p.half
            p.mine[v, x, zz, :, a] = (
                p.mine[v, x, zz, :, a].astype(F32) + p.one[0][v, zz].astype(F32)
            ).astype(BF)
            p.mine[y, v, zz, :, b] = (
                p.mine[y, v, zz, :, b].astype(F32) + p.one[1][v, zz].astype(F32)
            ).astype(BF)
            return carry

        lax.fori_loop(0, 2 * chips, body, 0)
        p.second_y().start()
        p.second_x().start()

    def stage_three(p):
        p.second_y().wait_recv()
        p.second_x().wait_recv()

        def body(zz, carry):
            for w in (0, 1):
                s = p.half[w]
                p.mine[y, x, zz, :, s] = (
                    p.mine[y, x, zz, :, s].astype(F32) + p.two[w][zz].astype(F32)
                ).astype(BF)
            return carry

        lax.fori_loop(0, chips, body, 0)
        for k in range(1, chips):
            p.last(k).start()

    def stage_four(p):
        total = p.mine[y, x, z].astype(F32)
        for k in range(1, chips):
            p.last(k).wait_recv()
            total = total + p.end[k - 1].astype(F32)
        outs[p.i][:, p.first : p.first + p.wide] = total

    def mix_load(zz):
        return pltpu.make_async_copy(mix_in.at[zz, c], mix_mine.at[zz], s_mix.at[zz])

    def mix_core(zz):
        return sent(
            mix_in.at[zz, 1 - c], mix_other.at[zz], s_mcore.at[zz], r_mcore.at[zz], at.sibling
        )

    def mix_over(k):
        zz = lax.rem(z + k, chips)
        return sent(
            mix_mine.at[zz], mix_came.at[k], s_mchain.at[k], r_mchain.at[k], (at.d, 2 * zz + c)
        )

    def mix_settle():
        for k in range(1, chips):
            zz = lax.rem(z + k, chips)
            mix_core(zz).wait_recv()
            mix_load(zz).wait()
            mix_mine[zz] = (mix_mine[zz].astype(F32) + mix_other[zz].astype(F32)).astype(BF)
            mix_over(k).start()
        mix_core(z).wait_recv()
        mix_load(z).wait()

    part = projected.shape[2]

    def weight_load(k):
        return pltpu.make_async_copy(
            weight_in.at[:, pl.ds(k * part, part)], weight, s_weight.at[0]
        )

    def input_grads(k):
        weight_load(k).wait()
        if k == 0:
            grad_ref[...] = nt(projected[0], weight[...])
        else:
            grad_ref[...] += nt(projected[k], weight[...])
        if k < 2:
            weight_load(k + 1).start()
            return
        grad = grad_ref[...]
        gains = jnp.sum(grad * unit[...], axis=0, keepdims=True)
        column = jnp.broadcast_to(gains, (8, part)).T[:, :1]
        lanes = lax.broadcasted_iota(jnp.int32, misc_in.shape, 1)
        tile_ref[:, : misc_in.shape[1]] = jnp.where(lanes == experts, column, misc_in[...])
        scaled = grad * gain[...]
        mean = jnp.mean(scaled * unit[...], axis=1, keepdims=True)
        input_out[...] = (grad_middle[...] + inverse[...] * (scaled - unit[...] * mean)).astype(BF)

    for p in parts:
        if not p.made:
            p.core().start()
            p.load().start()
    weight_load(0).start()
    for zz in range(chips):
        mix_core(zz).start()
        mix_load(zz).start()
    n_known = sum(not p.made for p in parts)
    for p in parts[n_known:-1]:
        k, first = p.first // projected.shape[2], p.first % projected.shape[2]
        tile_ref[:, : p.wide] = tn(normed[...], projected[k, :, first : first + p.wide])
        p.take()
    stages = (stage_one, stage_two, stage_three, stage_four)
    for t in range(n_chunks + len(stages) - 1):
        for s, stage in enumerate(stages):
            if 0 <= t - s < n_chunks:
                stage(parts[t - s])
        if t == 1:
            mix_settle()
        if t < 3:
            input_grads(t)
        if t == 2:
            parts[-1].take()
    total = base[...] + mix_mine[z].astype(F32) + mix_other[z].astype(F32)
    for k in range(1, chips):
        mix_over(k).wait_recv()
        total = total + mix_came[k].astype(F32)
    output_out[...] = total.astype(BF)
    for p in parts:
        p.core().wait_send()
        p.first_x().wait_send()
        p.first_y().wait_send()
        p.second_x().wait_send()
        p.second_y().wait_send()
        for k in range(1, chips):
            p.last(k).wait_send()
    for k in range(1, chips):
        mix_over(k).wait_send()
    for zz in range(chips):
        mix_core(zz).wait_send()


def finish(
    arrays,
    chunk_widths,
    experts,
    normed,
    projected,
    qkv_weight,
    misc,
    unit,
    inverse,
    gain,
    grad_middle,
    mix,
    base,
    collective_id,
):
    chain = lax.axis_size("expert")
    chips = chain // 2
    width = arrays[0].shape[0]
    block = width // (4 * chain)
    rows = normed.shape[0]
    columns = qkv_weight.shape[1]
    n = len(arrays)
    dma = pltpu.SemaphoreType.DMA
    sizes = [a.shape[1] for a in arrays] + [columns, misc.shape[1]]
    chunks = []
    for i, (size, wide) in enumerate(zip(sizes, chunk_widths)):
        assert size % wide == 0 and wide % 128 == 0 and wide >= 256
        chunks += [(i, first, wide) for first in range(0, size, wide)]
    q = len(chunks)
    scratch = [dma((q,)), dma((q,)), dma((q,))] + [dma((q, 2))] * 4 + [dma((q, chips - 1))] * 2
    scratch += [dma((chips,))] * 5 + [dma((1,))]
    scratch += [
        pltpu.VMEM((width, columns // 3), BF),
        pltpu.VMEM((rows, width), F32),
        pltpu.VMEM((width, max(chunk_widths[n:])), F32),
        pltpu.VMEM((chips, rows, width), BF),
        pltpu.VMEM((chips, rows, width), BF),
        pltpu.VMEM((chips, rows, width), BF),
    ]
    for i, first, wide in chunks:
        cut = wide // 256 * 128
        scratch += [
            pltpu.VMEM((2, 2, chips, block, wide), BF),
            pltpu.VMEM((2, 2, chips, block, wide), BF),
            pltpu.VMEM((2, chips, block, cut), BF),
            pltpu.VMEM((2, chips, block, wide - cut), BF),
            pltpu.VMEM((chips, block, cut), BF),
            pltpu.VMEM((chips, block, wide - cut), BF),
            pltpu.VMEM((chips - 1, block, wide), BF),
            pltpu.VMEM((2, 2, chips, block, wide) if i >= n else (16, 128), BF),
        ]
    anywhere = pl.BlockSpec(memory_space=pl.ANY)
    vmem = pl.BlockSpec(memory_space=pltpu.VMEM)
    return pl.pallas_call(
        functools.partial(finish_kernel, chips, tuple(chunks), n, experts),
        out_shape=[jax.ShapeDtypeStruct((block, size), F32) for size in sizes]
        + [jax.ShapeDtypeStruct((rows, width), BF)] * 2,
        in_specs=[anywhere] * n
        + [vmem, vmem, anywhere, vmem, vmem, vmem, vmem, vmem, anywhere, vmem],
        out_specs=[vmem] * (n + 4),
        scratch_shapes=scratch,
        compiler_params=pltpu.CompilerParams(
            vmem_limit_bytes=MOE_VMEM, collective_id=collective_id, has_side_effects=True
        ),
        cost_estimate=pl.CostEstimate(
            flops=4 * rows * width * columns, bytes_accessed=64 * width * columns, transcendentals=0
        ),
    )(
        *[a.reshape(2, 2, chips, 2, block, a.shape[1]) for a in arrays],
        normed,
        projected,
        qkv_weight,
        misc,
        unit,
        inverse,
        gain,
        grad_middle,
        mix,
        base,
    )


def silu_parts(values):
    s = jax.nn.sigmoid(values)
    return values * s, s * (1.0 + values * (1.0 - s))


def local(
    tokens,
    cotangent,
    lengths,
    routes,
    attn_qkv,
    attn_out,
    shared_gate,
    shared_up,
    shared_down,
    router,
    gains,
    expert_gate,
    expert_up,
    expert_down,
):
    rows = tokens.shape[1]
    width = tokens.shape[2]
    hidden = shared_gate.shape[1]
    chain = lax.axis_size("expert")
    index = lax.axis_index("expert")
    experts = EXP_DEV * chain
    everyone = ("dp", "expert")
    keys = rows * chain
    own_first = index * rows
    me = index.reshape(1).astype(jnp.int32)

    route_pad = 128 * (-(-(experts + 2) // 128))
    misc = jnp.concatenate([router.astype(BF), gains.astype(BF).T], axis=1)
    misc = jnp.pad(misc, ((0, 0), (0, route_pad - experts - 2)))
    near = jnp.concatenate([misc, attn_out.astype(BF).T], axis=1)
    expert_shard = jnp.stack(
        [expert_gate.astype(BF), expert_up.astype(BF), jnp.swapaxes(expert_down.astype(BF), 1, 2)]
    )
    expert_weight = lax.all_gather(expert_shard, "dp", axis=2, tiled=True)
    qkv_weight, near, tokens_all, routes_all, grads_all = gather(
        [attn_qkv.astype(BF), near], [tokens[0], routes[0], cotangent[0]], 0
    )
    grads_all = grads_all.reshape(keys, width)
    qkv_weight = qkv_weight.reshape(width, 3 * H * HD)
    near = near.reshape(width, near.shape[-1])
    tokens_all = tokens_all.reshape(keys, width)
    routes_all = routes_all.reshape(keys, TOP)
    cuts = [route_pad, route_pad + width]
    cuts += [cuts[-1] + hidden, cuts[-1] + 2 * hidden]
    misc, out_t = jnp.split(near, cuts[:1], axis=1)
    route_weight = misc[:, :experts]
    gain_attn = misc[:, experts].astype(F32)
    gain_moe = misc[:, experts + 1].astype(F32)
    shared = jnp.concatenate(
        [shared_gate.astype(BF), shared_up.astype(BF), shared_down.astype(BF).T], axis=1
    )
    first_all, rope_all = doc_starts_of(lengths[0], jnp.arange(keys, dtype=jnp.int32))
    first_own = lax.dynamic_slice_in_dim(first_all, own_first, rows, 0)
    cosine, sine = turn_tables(rope_all)
    cosine_own = lax.dynamic_slice_in_dim(cosine, own_first, rows, 0)
    sine_own = lax.dynamic_slice_in_dim(sine, own_first, rows, 0)
    wide = tokens_all.astype(F32)
    normed_all = (wide * inverse_rms(wide) * gain_attn).astype(BF)
    inputs = tokens[0].astype(F32)
    inverse_one = inverse_rms(inputs)
    unit_one = inputs * inverse_one
    normed = (unit_one * gain_attn).astype(BF)
    qkv = project_qkv(normed_all, qkv_weight, cosine, sine)
    attended_full, log_own = attend(me, qkv, first_own)
    attended = attended_full.astype(BF)
    middle = inputs + nt(attended, out_t)
    inverse_two = inverse_rms(middle)
    unit_two = middle * inverse_two
    normed_moe = (unit_two * gain_moe).astype(BF)
    shared, expert_weight, normed_moe = lax.optimization_barrier((shared, expert_weight, normed_moe))
    shared = lax.all_gather(shared, everyone, axis=0, tiled=True)
    gate_shared, up_shared, down_t = jnp.split(shared, [hidden, 2 * hidden], axis=1)

    def routing(activations, route_ids):
        logits = nn(activations, route_weight)
        probs = jax.nn.softmax(logits, axis=-1)
        named = route_ids[:, :, None] == jnp.arange(experts, dtype=jnp.int32)[None, None, :]
        named = jnp.any(named, axis=1)
        chosen = jnp.where(named, probs, 0.0)
        total = jnp.sum(chosen, axis=1, keepdims=True)
        return probs, named, chosen / total, total

    probs, named, gates, chosen_total = routing(normed_moe, routes[0])

    shared_gate_v = nn(normed_moe, gate_shared)
    shared_up_v = nn(normed_moe, up_shared)
    shared_act, shared_slope = silu_parts(shared_gate_v)
    shared_mid = (shared_act * shared_up_v).astype(BF)
    shared_out = nt(shared_mid, down_t)
    grad_out = cotangent[0].astype(F32)
    grad_bf = cotangent[0]
    grad_shared_mid = nn(grad_bf, down_t)
    grad_shared_gate_v = (grad_shared_mid * shared_up_v * shared_slope).astype(BF)
    grad_shared_up_v = (grad_shared_mid * shared_act).astype(BF)
    grad_normed_moe = nt(grad_shared_gate_v, gate_shared) + nt(grad_shared_up_v, up_shared)

    fits = 2 * (2 * expert_weight.size // 2 + 3 * keys * EXP_DEV * hidden + 5 * keys * width) < MOE_VMEM
    if fits:
        row_sum, gate_grads, expert_mid, expert_grads = moe_fused(
            normed_moe, routes_all, grads_all, misc, expert_weight, experts, 1
        )
        core = index % 2
        gate_grads = gate_grads[:, :EXP_DEV].reshape(chain, EXP_DEV, 2, rows)
        gate_grads = jnp.where(core == 0, gate_grads[:, :, 0], gate_grads[:, :, 1])
    else:
        moe_all = gather([], [normed_moe], 1)[0].reshape(keys, width)
        unused, unused, gates_all, unused = routing(moe_all, routes_all)
        gates_here = lax.dynamic_slice_in_dim(gates_all, index * EXP_DEV, EXP_DEV, 1)
        row_part, gate_grads, expert_mid, expert_grads = moe_plain(
            moe_all, gates_here, grads_all, expert_weight
        )
        gate_grads = jnp.transpose(gate_grads.T.reshape(EXP_DEV, chain, rows), (1, 0, 2))
        row_sum, gate_grads = to_owner(row_part.reshape(chain, rows, width), gate_grads, 2)
    gate_grads = gate_grads.reshape(experts, rows).T
    expert_sum = lax.psum_scatter(expert_grads, "dp", scatter_dimension=2, tiled=True)
    grad_chosen = (gate_grads - jnp.sum(gates * gate_grads, axis=1, keepdims=True)) / chosen_total
    grad_probs = jnp.where(named, grad_chosen, 0.0)
    grad_logits = (
        probs * (grad_probs - jnp.sum(probs * grad_probs, axis=1, keepdims=True))
    ).astype(BF)
    grad_route = tn(normed_moe, grad_logits)
    grad_normed_moe = grad_normed_moe + row_sum + nt(grad_logits, route_weight)
    grad_gain_moe = jnp.sum(grad_normed_moe * unit_two, axis=0)
    scaled_two = grad_normed_moe * gain_moe
    grad_middle = grad_out + inverse_two * (
        scaled_two - unit_two * jnp.mean(scaled_two * unit_two, axis=-1, keepdims=True)
    )
    grad_attn = grad_middle.astype(BF)
    grad_attended = nn(grad_attn, out_t).astype(BF)

    delta = jnp.sum((grad_attended.astype(F32) * attended_full).reshape(rows, H, HD), axis=-1).T
    side = jnp.concatenate([log_own[:, :, 0], delta], axis=0)
    if fits:
        grad_all, side_all, mixture, grad_gate_shared, grad_up_shared, grad_down_t, grad_out_t = spread(
            grad_attended,
            side,
            expert_mid,
            expert_weight,
            normed_moe,
            grad_shared_gate_v,
            grad_shared_up_v,
            grad_bf,
            shared_mid,
            grad_attn,
            attended,
            3,
        )
    else:
        grad_all, side_all = gather([], [grad_attended, side], 3)
    grad_all = grad_all.reshape(keys, H * HD)
    side_all = jnp.transpose(side_all, (1, 0, 2)).reshape(2, H, 1, keys)
    grads = attend_back(
        me,
        qkv,
        grad_attended,
        grad_all,
        log_own,
        jnp.broadcast_to(delta[:, :, None], (H, rows, 8)),
        side_all[0],
        side_all[1],
        (first_own, first_all),
        cosine_own,
        sine_own,
    )
    grad_misc = jnp.concatenate(
        [grad_route, jnp.zeros((width, 1), F32), grad_gain_moe[:, None]], axis=1
    )
    grad_misc = jnp.pad(grad_misc, ((0, 0), (0, 256 - experts - 2)))
    if fits:
        out_sum, gate_sum, up_sum, down_sum, qkv_sum, misc_sum, grad_inputs, output = finish(
            [grad_out_t, grad_gate_shared, grad_up_shared, grad_down_t],
            (640, hidden, hidden, hidden, 640, 256),
            experts,
            normed,
            grads,
            qkv_weight,
            grad_misc,
            unit_one,
            inverse_one,
            gain_attn[None, :],
            grad_middle,
            mixture,
            middle + shared_out,
            4,
        )
    else:
        down = expert_weight[2]
        mixture = nt(expert_mid[:, :hidden], down[0])
        for e in range(1, EXP_DEV):
            mixture = mixture + nt(expert_mid[:, e * hidden : (e + 1) * hidden], down[e])
        mixture = lax.psum_scatter(mixture.astype(BF), "expert", scatter_dimension=0, tiled=True)
        output = (middle + shared_out + mixture.astype(F32)).astype(BF)
        grad_projected = jnp.concatenate([grads[0], grads[1], grads[2]], axis=1)
        grad_normed_one = nt(grad_projected, qkv_weight)
        grad_gain_attn = jnp.sum(grad_normed_one * unit_one, axis=0)
        scaled_one = grad_normed_one * gain_attn
        grad_inputs = grad_middle + inverse_one * (
            scaled_one - unit_one * jnp.mean(scaled_one * unit_one, axis=-1, keepdims=True)
        )
        grad_inputs = grad_inputs.astype(BF)
        out_sum, gate_sum, up_sum, down_sum, qkv_sum, misc_sum = sum_dense(
            [
                tn(grad_attn, attended).astype(BF),
                tn(normed_moe, grad_shared_gate_v).astype(BF),
                tn(normed_moe, grad_shared_up_v).astype(BF),
                tn(grad_bf, shared_mid).astype(BF),
                tn(normed, grad_projected).astype(BF),
                grad_misc.at[:, experts].set(grad_gain_attn).astype(BF),
            ],
            (640, hidden, hidden, hidden, 768, 256),
            4,
        )
    expert_sum = expert_sum.astype(F32)
    return (
        output[None],
        grad_inputs[None],
        qkv_sum,
        out_sum.T,
        gate_sum,
        up_sum,
        down_sum.T,
        misc_sum[:, :experts],
        misc_sum[:, experts : experts + 2].T,
        expert_sum[0],
        expert_sum[1],
        jnp.swapaxes(expert_sum[2], 1, 2),
    )


def solution(mesh):
    everyone = ("dp", "expert")
    in_specs = (
        P("dp", "expert", None),
        P("dp", "expert", None),
        P("dp", None),
        P("dp", "expert", None),
        P(everyone, None),
        P(None, everyone),
        P(everyone, None),
        P(everyone, None),
        P(None, everyone),
        P(everyone, None),
        P(None, everyone),
        P("expert", "dp", None),
        P("expert", "dp", None),
        P("expert", None, "dp"),
    )
    out_specs = (
        P("dp", "expert", None),
        P("dp", "expert", None),
        P(everyone, None),
        P(None, everyone),
        P(everyone, None),
        P(everyone, None),
        P(None, everyone),
        P(everyone, None),
        P(None, everyone),
        P("expert", "dp", None),
        P("expert", "dp", None),
        P("expert", None, "dp"),
    )
    return jax.shard_map(local, mesh=mesh, in_specs=in_specs, out_specs=out_specs, check_vma=False)
```

```python
import functools

import jax
import jax.numpy as jnp
from jax import lax
from jax.experimental import pallas as pl
from jax.experimental.pallas import tpu as pltpu
from jax.sharding import PartitionSpec as P

H = 10
HD = 128
TOP = 7
EXP_DEV = 2
EPS = 1e-06
NEG = -1e30
BF = jnp.bfloat16
F32 = jnp.float32
VMEM_LIMIT = 56 * 1024 * 1024
MOE_VMEM = 62 * 1024 * 1024


def params(**kw):
    return pltpu.CompilerParams(vmem_limit_bytes=VMEM_LIMIT, **kw)


def nn(a, b):
    return jnp.dot(a, b, preferred_element_type=F32)


def nt(a, b):
    return lax.dot_general(a, b, (((1,), (1,)), ((), ())), preferred_element_type=F32)


def tn(a, b):
    return lax.dot_general(a, b, (((0,), (0,)), ((), ())), preferred_element_type=F32)


def doc_starts_of(lengths, places):
    doc_ends = jnp.cumsum(lengths)
    doc_starts = doc_ends - lengths
    total = doc_ends[-1]
    doc_index = jnp.sum((places[:, None] >= doc_ends[None, :]).astype(jnp.int32), axis=1)
    live = places < total
    matches = doc_index[:, None] == jnp.arange(lengths.shape[0], dtype=jnp.int32)[None, :]
    first = jnp.sum(jnp.where(matches, doc_starts[None, :], 0), axis=1)
    return jnp.where(live, first, places), places - jnp.where(live, first, total)


def turn_tables(rope_pos):
    half = HD // 2
    frequency = 10000.0 ** (-jnp.arange(half, dtype=F32) / half)
    angles = rope_pos.astype(F32)[:, None] * frequency[None, :]
    cosine = jnp.cos(angles)
    sine = jnp.sin(angles)
    return (
        jnp.concatenate([cosine, cosine], axis=1),
        jnp.concatenate([-sine, sine], axis=1),
    )


def inverse_rms(values):
    return lax.rsqrt(jnp.mean(values * values, axis=-1, keepdims=True) + EPS)


MESH = pl.DeviceIdType.MESH


def sent(src, dst, send_sem, recv_sem, device):
    return pltpu.make_async_remote_copy(
        src_ref=src,
        dst_ref=dst,
        send_sem=send_sem,
        recv_sem=recv_sem,
        device_id=device,
        device_id_type=MESH,
    )


class Place:
    def __init__(self, chips):
        self.d = lax.axis_index("dp")
        self.e = lax.axis_index("expert")
        self.z = self.e // 2
        self.c = self.e % 2
        self.y = self.d // 2
        self.x = self.d % 2
        self.chips = chips
        self.sibling = (self.d, self.e + 1 - 2 * self.c)
        self.across_x = (self.d + 1 - 2 * self.x, self.e)
        self.across_y = (self.d + 2 - 4 * self.y, self.e)
        self.up = (self.d, self.e + 2)
        self.down = (self.d, self.e - 2)


def greet(devices, conditions):
    barrier = pltpu.get_barrier_semaphore()
    count = 0
    for device, condition in zip(devices, conditions):
        if condition is None:
            pl.semaphore_signal(barrier, inc=1, device_id=device, device_id_type=MESH)
            count = count + 1
        else:

            @pl.when(condition)
            def _(device=device):
                pl.semaphore_signal(barrier, inc=1, device_id=device, device_id_type=MESH)

            count = count + condition.astype(jnp.int32)
    pl.semaphore_wait(barrier, count)


def gather_kernel(chips, n_full, n_chain, *refs):
    n = n_full + n_chain
    ins, outs, sems = refs[:n], refs[n : 2 * n], refs[2 * n :]
    at = Place(chips)
    chain = 2 * chips
    z, c = at.z, at.c
    has_up, has_down = z < chips - 1, z > 0
    devices = [at.sibling, at.up, at.down]
    conditions = [None, has_up, has_down]
    if n_full:
        devices += [at.across_x, at.across_y]
        conditions += [None, None]
    greet(devices, conditions)
    x_dp, y_dp = at.across_x[0], at.across_y[0]
    far_dp = 3 - at.d

    class Array:
        pass

    arrays = []
    position = 0
    for i in range(n):
        a = Array()
        a.full = i < n_full
        a.own, a.out = ins[i], outs[i]
        a.local, a.s_chain, a.r_chain, a.s_core, a.r_core = sems[position : position + 5]
        position += 5
        if a.full:
            a.s_side, a.r_side, a.s_half, a.r_half = sems[position : position + 4]
            position += 4
            cut = a.own.shape[-1] // 256 * 128
            a.halves = (pl.ds(0, cut), pl.ds(cut, a.own.shape[-1] - cut))
        arrays.append(a)

    def slot(a, dd, zz, cc):
        return a.out.at[dd * chain + 2 * zz + cc] if a.full else a.out.at[2 * zz + cc]

    def core_index(a, dd, zz):
        return dd * chips + zz if a.full else zz

    def to_core(a, dd, zz, src=None):
        ref = slot(a, dd, zz, c)
        k = core_index(a, dd, zz)
        return sent(ref if src is None else src, ref, a.s_core.at[k], a.r_core.at[k], at.sibling)

    def from_core(a, dd, zz):
        ref = slot(a, dd, zz, 1 - c)
        k = core_index(a, dd, zz)
        return sent(ref, ref, a.s_core.at[k], a.r_core.at[k], at.sibling)

    def along(a, zz, direction, src=None):
        ref = slot(a, at.d, zz, c)
        device = at.up if direction == 0 else at.down
        return sent(ref if src is None else src, ref, a.s_chain.at[direction, zz], a.r_chain.at[zz], device)

    def side(a, dd, zz, axis, src=None):
        ref = slot(a, dd, zz, c)
        device = at.across_x if axis == 0 else at.across_y
        return sent(
            ref if src is None else src, ref, a.s_side.at[axis, zz], a.r_side.at[axis, zz], device
        )

    def half(a, dd, zz, which):
        ref = slot(a, dd, zz, c).at[:, a.halves[which]]
        device = at.across_y if which == 0 else at.across_x
        return sent(ref, ref, a.s_half.at[which, zz], a.r_half.at[which, zz], device)

    def present(zz):
        return (zz >= 0) & (zz < chips)

    def block_here(some, zz, direction):
        for a in some:
            along(a, zz, direction).wait_recv()
            if direction == 0:

                @pl.when(has_up)
                def _(a=a):
                    along(a, zz, 0).start()
            else:

                @pl.when(has_down)
                def _(a=a):
                    along(a, zz, 1).start()

            if a.full:
                side(a, at.d, zz, 0).start()
                side(a, at.d, zz, 1).start()
            to_core(a, at.d, zz).start()

    def side_here(zz):
        for a in arrays[:n_full]:
            side(a, x_dp, zz, 0).wait_recv()
            half(a, x_dp, zz, 0).start()
            to_core(a, x_dp, zz).start()
            side(a, y_dp, zz, 1).wait_recv()
            half(a, y_dp, zz, 1).start()
            to_core(a, y_dp, zz).start()

    def far_here(zz):
        for a in arrays[:n_full]:
            half(a, far_dp, zz, 0).wait_recv()
            half(a, far_dp, zz, 1).wait_recv()
            to_core(a, far_dp, zz).start()

    def own_here(some):
        for a in some:

            @pl.when(has_up)
            def _(a=a):
                along(a, z, 0, a.own).start()

            @pl.when(has_down)
            def _(a=a):
                along(a, z, 1, a.own).start()

            if a.full:
                side(a, at.d, z, 0, a.own).start()
                side(a, at.d, z, 1, a.own).start()
            to_core(a, at.d, z, a.own).start()
            pltpu.make_async_copy(a.own, slot(a, at.d, z, c), a.local).start()

    def at_distance(k, fn):
        @pl.when((k >= 0) & present(z - k))
        def _():
            fn(z - k)

        @pl.when((k >= 1) & present(z + k))
        def _():
            fn(z + k)

    def chain_step(some, k):
        @pl.when(present(z - k))
        def _():
            block_here(some, z - k, 0)

        @pl.when(present(z + k))
        def _():
            block_here(some, z + k, 1)

    full, chained = arrays[:n_full], arrays[n_full:]
    if n_full:
        own_here(full)

        def first_step(k, carry):
            chain_step(full, k)
            return carry

        lax.fori_loop(1, chips, first_step, 0)
    own_here(chained)

    def step(k, carry):
        if n_full:
            at_distance(k - 1, side_here)
        chain_step(chained, k)
        if n_full:
            at_distance(k - 2, far_here)
        return carry

    lax.fori_loop(1, chips + (2 if n_full else 0), step, 0)

    def finish(zz, carry):
        for a in arrays:
            for dd in range(4) if a.full else (0,):
                from_core(a, dd, zz).wait_recv()
                to_core(a, dd, zz).wait_send()

            @pl.when((zz <= z) & has_up)
            def _(a=a):
                along(a, zz, 0).wait_send()

            @pl.when((zz >= z) & has_down)
            def _(a=a):
                along(a, zz, 1).wait_send()

            if a.full:
                for axis in (0, 1):
                    side(a, at.d, zz, axis).wait_send()
                half(a, x_dp, zz, 0).wait_send()
                half(a, y_dp, zz, 1).wait_send()
        return carry

    lax.fori_loop(0, chips, finish, 0)
    for a in arrays:
        pltpu.make_async_copy(a.own, slot(a, at.d, z, c), a.local).wait()


def gather(full, chained, collective_id):
    chain = lax.axis_size("expert")
    chips = chain // 2
    spread = lax.axis_size("dp")
    assert spread == 4 and chain % 2 == 0
    dma = pltpu.SemaphoreType.DMA
    scratch = []
    for array in full:
        scratch += [dma, dma((2, chips)), dma((chips,)), dma((4 * chips,)), dma((4 * chips,))]
        scratch += [dma((2, chips))] * 4
    for array in chained:
        scratch += [dma, dma((2, chips)), dma((chips,)), dma((chips,)), dma((chips,))]
    shapes = [jax.ShapeDtypeStruct((spread * chain,) + a.shape, a.dtype) for a in full]
    shapes += [jax.ShapeDtypeStruct((chain,) + a.shape, a.dtype) for a in chained]
    n = len(full) + len(chained)
    moved = sum(s.size * s.dtype.itemsize for s in shapes)
    return pl.pallas_call(
        functools.partial(gather_kernel, chips, len(full), len(chained)),
        out_shape=shapes,
        in_specs=[pl.BlockSpec(memory_space=pl.ANY)] * n,
        out_specs=[pl.BlockSpec(memory_space=pl.ANY)] * n,
        scratch_shapes=scratch,
        compiler_params=params(collective_id=collective_id, has_side_effects=True),
        cost_estimate=pl.CostEstimate(flops=0, bytes_accessed=16 * moved, transcendentals=0),
    )(*full, *chained)


def to_owner_kernel(chips, wide_ref, thin_ref, out_ref, thin_out, mine, other, came, sems_in, s_core, r_core, s_chain, r_chain, s_thin, r_thin):
    at = Place(chips)
    chain = 2 * chips
    z, c = at.z, at.c
    devices = [(at.d, lax.rem(at.e + k, chain)) for k in range(1, chain)]
    greet(devices, [None] * (chain - 1))

    def load(zz):
        return pltpu.make_async_copy(wide_ref.at[2 * zz + c], mine.at[zz], sems_in.at[zz])

    def to_core(zz):
        return sent(
            wide_ref.at[2 * zz + 1 - c], other.at[zz], s_core.at[zz], r_core.at[zz], at.sibling
        )

    def thin(k):
        target = lax.rem(at.e + k, chain)
        return sent(
            thin_ref.at[target], thin_out.at[at.e], s_thin.at[k], r_thin.at[k], (at.d, target)
        )

    def over(k):
        zz = lax.rem(z + k, chips)
        return sent(
            mine.at[zz], came.at[k], s_chain.at[k], r_chain.at[k], (at.d, 2 * zz + c)
        )

    order = [lax.rem(z + k, chips) for k in range(1, chips)] + [z]
    for zz in order:
        to_core(zz).start()
        load(zz).start()
    for k in range(1, chain):
        thin(k).start()
    own_thin = pltpu.make_async_copy(thin_ref.at[at.e], thin_out.at[at.e], s_thin.at[0])
    own_thin.start()
    for k, zz in enumerate(order):
        to_core(zz).wait_recv()
        load(zz).wait()
        total = mine[zz].astype(F32) + other[zz].astype(F32)
        if k < chips - 1:
            mine[zz] = total.astype(BF)
            over(k + 1).start()
        else:
            out_ref[...] = total
    for k in range(1, chips):
        over(k).wait_recv()
        out_ref[...] += came[k].astype(F32)
    for k in range(1, chips):
        over(k).wait_send()
    for zz in order:
        to_core(zz).wait_send()
    own_thin.wait()
    for k in range(1, chain):
        thin(k).wait()


def to_owner(wide, thin, collective_id):
    chain, rows, width = wide.shape
    chips = chain // 2
    dma = pltpu.SemaphoreType.DMA
    return pl.pallas_call(
        functools.partial(to_owner_kernel, chips),
        out_shape=[
            jax.ShapeDtypeStruct((rows, width), F32),
            jax.ShapeDtypeStruct(thin.shape, thin.dtype),
        ],
        in_specs=[pl.BlockSpec(memory_space=pl.ANY), pl.BlockSpec(memory_space=pltpu.VMEM)],
        out_specs=[pl.BlockSpec(memory_space=pltpu.VMEM), pl.BlockSpec(memory_space=pltpu.VMEM)],
        scratch_shapes=[
            pltpu.VMEM((chips, rows, width), BF),
            pltpu.VMEM((chips, rows, width), BF),
            pltpu.VMEM((chips, rows, width), BF),
            dma((chips,)),
            dma((chips,)),
            dma((chips,)),
            dma((chips,)),
            dma((chips,)),
            dma((chain,)),
            dma((chain,)),
        ],
        compiler_params=params(collective_id=collective_id, has_side_effects=True),
        cost_estimate=pl.CostEstimate(
            flops=0, bytes_accessed=16 * wide.size * 2, transcendentals=0
        ),
    )(wide, thin)


def sum_dense_kernel(chips, chunks, n_in, *refs):
    ins, outs = refs[:n_in], refs[n_in : 2 * n_in]
    n_chunks = len(chunks)
    rest = refs[2 * n_in :]
    sems = rest[:10]
    s_in, s_core, r_core, s_one, r_one, s_two, r_two, s_end, r_end = sems[:9]
    buffers = rest[9:]
    at = Place(chips)
    z, c, x, y = at.z, at.c, at.x, at.y
    others = [(at.d, 2 * lax.rem(z + k, chips) + c) for k in range(1, chips)]
    devices = [at.sibling, at.across_x, at.across_y] + others
    greet(devices, [None] * len(devices))

    class Chunk:
        def __init__(self, q):
            i, first, wide = chunks[q]
            self.i, self.first, self.wide = i, first, wide
            self.q = q
            self.mine, self.other, one_x, one_y, two_x, two_y, self.end = buffers[7 * q : 7 * q + 7]
            self.one, self.two = (one_x, one_y), (two_x, two_y)
            self.cols = pl.ds(first, wide)
            cut = wide // 256 * 128
            self.half = (pl.ds(0, cut), pl.ds(cut, wide - cut))

        def load(self):
            return pltpu.make_async_copy(
                ins[self.i].at[:, :, :, c, :, self.cols], self.mine, s_in.at[self.q]
            )

        def core(self):
            return sent(
                ins[self.i].at[:, :, :, 1 - c, :, self.cols],
                self.other,
                s_core.at[self.q],
                r_core.at[self.q],
                at.sibling,
            )

        def first_x(self):
            return sent(
                self.mine.at[:, 1 - x, :, :, self.half[0]],
                self.one[0],
                s_one.at[self.q, 0],
                r_one.at[self.q, 0],
                at.across_x,
            )

        def first_y(self):
            return sent(
                self.mine.at[1 - y, :, :, :, self.half[1]],
                self.one[1],
                s_one.at[self.q, 1],
                r_one.at[self.q, 1],
                at.across_y,
            )

        def second_y(self):
            return sent(
                self.mine.at[1 - y, x, :, :, self.half[0]],
                self.two[0],
                s_two.at[self.q, 0],
                r_two.at[self.q, 0],
                at.across_y,
            )

        def second_x(self):
            return sent(
                self.mine.at[y, 1 - x, :, :, self.half[1]],
                self.two[1],
                s_two.at[self.q, 1],
                r_two.at[self.q, 1],
                at.across_x,
            )

        def last(self, k):
            zz = lax.rem(z + k, chips)
            return sent(
                self.mine.at[y, x, zz],
                self.end.at[k - 1],
                s_end.at[self.q, k - 1],
                r_end.at[self.q, k - 1],
                (at.d, 2 * zz + c),
            )

    parts = [Chunk(q) for q in range(n_chunks)]

    def add(ref, place, more):
        ref[place] = (ref[place].astype(F32) + more.astype(F32)).astype(BF)

    def stage_one(p):
        p.core().wait_recv()
        p.load().wait()

        def body(k, carry):
            yy, xx, zz = k // (2 * chips), (k // chips) % 2, k % chips
            p.mine[yy, xx, zz] = (
                p.mine[yy, xx, zz].astype(F32) + p.other[yy, xx, zz].astype(F32)
            ).astype(BF)
            return carry

        lax.fori_loop(0, 4 * chips, body, 0)
        p.first_x().start()
        p.first_y().start()

    def stage_two(p):
        p.first_x().wait_recv()
        p.first_y().wait_recv()

        def body(k, carry):
            v, zz = k // chips, k % chips
            a, b = p.half
            p.mine[v, x, zz, :, a] = (
                p.mine[v, x, zz, :, a].astype(F32) + p.one[0][v, zz].astype(F32)
            ).astype(BF)
            p.mine[y, v, zz, :, b] = (
                p.mine[y, v, zz, :, b].astype(F32) + p.one[1][v, zz].astype(F32)
            ).astype(BF)
            return carry

        lax.fori_loop(0, 2 * chips, body, 0)
        p.second_y().start()
        p.second_x().start()

    def stage_three(p):
        p.second_y().wait_recv()
        p.second_x().wait_recv()

        def body(zz, carry):
            for w in (0, 1):
                s = p.half[w]
                p.mine[y, x, zz, :, s] = (
                    p.mine[y, x, zz, :, s].astype(F32) + p.two[w][zz].astype(F32)
                ).astype(BF)
            return carry

        lax.fori_loop(0, chips, body, 0)
        for k in range(1, chips):
            p.last(k).start()

    def stage_four(p):
        total = p.mine[y, x, z].astype(F32)
        for k in range(1, chips):
            p.last(k).wait_recv()
            total = total + p.end[k - 1].astype(F32)
        outs[p.i][:, p.first : p.first + p.wide] = total

    for p in parts:
        p.core().start()
        p.load().start()
    stages = (stage_one, stage_two, stage_three, stage_four)
    for t in range(n_chunks + len(stages) - 1):
        for s, stage in enumerate(stages):
            if 0 <= t - s < n_chunks:
                stage(parts[t - s])
    for p in parts:
        p.core().wait_send()
        p.first_x().wait_send()
        p.first_y().wait_send()
        p.second_x().wait_send()
        p.second_y().wait_send()
        for k in range(1, chips):
            p.last(k).wait_send()


def sum_dense(arrays, chunk_widths, collective_id):
    chain = lax.axis_size("expert")
    chips = chain // 2
    assert lax.axis_size("dp") == 4
    block = arrays[0].shape[0] // (4 * chain)
    dma = pltpu.SemaphoreType.DMA
    chunks = []
    for i, (array, wide) in enumerate(zip(arrays, chunk_widths)):
        assert array.shape[1] % wide == 0 and wide % 128 == 0 and wide >= 256
        chunks += [(i, first, wide) for first in range(0, array.shape[1], wide)]
    q = len(chunks)
    scratch = [dma((q,)), dma((q,)), dma((q,))] + [dma((q, 2))] * 4 + [dma((q, max(1, chips - 1)))] * 2
    for i, first, wide in chunks:
        cut = wide // 256 * 128
        scratch += [
            pltpu.VMEM((2, 2, chips, block, wide), BF),
            pltpu.VMEM((2, 2, chips, block, wide), BF),
            pltpu.VMEM((2, chips, block, cut), BF),
            pltpu.VMEM((2, chips, block, wide - cut), BF),
            pltpu.VMEM((chips, block, cut), BF),
            pltpu.VMEM((chips, block, wide - cut), BF),
            pltpu.VMEM((max(1, chips - 1), block, wide), BF),
        ]
    n = len(arrays)
    return pl.pallas_call(
        functools.partial(sum_dense_kernel, chips, tuple(chunks), n),
        out_shape=[jax.ShapeDtypeStruct((block, a.shape[1]), F32) for a in arrays],
        in_specs=[pl.BlockSpec(memory_space=pl.ANY)] * n,
        out_specs=[pl.BlockSpec(memory_space=pltpu.VMEM)] * n,
        scratch_shapes=scratch,
        compiler_params=params(collective_id=collective_id, has_side_effects=True),
        cost_estimate=pl.CostEstimate(
            flops=0, bytes_accessed=16 * sum(a.size for a in arrays), transcendentals=0
        ),
    )(*[a.reshape(2, 2, chips, 2, block, a.shape[1]) for a in arrays])


def qkv_kernel(per_block, x_ref, w_ref, cos_ref, sin_ref, o_ref):
    column = pl.program_id(1)
    rows = x_ref.shape[0]
    step = 384 if rows % 384 == 0 else rows
    for first in range(0, per_block, 2):
        for r in range(0, rows, step):
            product = nn(x_ref[r : r + step, :], w_ref[:, first * HD : (first + 2) * HD])
            for k in (0, 1):
                part = product[:, k * HD : (k + 1) * HD]
                head = column * per_block + first + k
                turned = (
                    part * cos_ref[r : r + step, :]
                    + pltpu.roll(part, HD // 2, 1) * sin_ref[r : r + step, :]
                )
                o_ref[r : r + step, (first + k) * HD : (first + k + 1) * HD] = jnp.where(
                    head < 2 * H, turned, part
                ).astype(BF)


def project_qkv(normed, weight, cosine, sine):
    rows, width = normed.shape
    columns = weight.shape[1]
    per_block = 6
    tile_m = min(rows, 1536)
    return pl.pallas_call(
        functools.partial(qkv_kernel, per_block),
        out_shape=jax.ShapeDtypeStruct((rows, columns), BF),
        grid=(rows // tile_m, columns // (per_block * HD)),
        in_specs=[
            pl.BlockSpec((tile_m, width), lambda m, n: (m, 0)),
            pl.BlockSpec((width, per_block * HD), lambda m, n: (0, n)),
            pl.BlockSpec((tile_m, HD), lambda m, n: (m, 0)),
            pl.BlockSpec((tile_m, HD), lambda m, n: (m, 0)),
        ],
        out_specs=pl.BlockSpec((tile_m, per_block * HD), lambda m, n: (m, n)),
        compiler_params=params(),
        cost_estimate=pl.CostEstimate(
            flops=2 * rows * width * columns,
            bytes_accessed=2 * (rows * width + width * columns + rows * columns),
            transcendentals=0,
        ),
    )(normed, weight, cosine, sine)


def attend_kernel(scale, me_ref, q_ref, k_ref, v_ref, first_ref, o_ref, log_ref, bias):
    rows, keys = bias.shape

    @pl.when(pl.program_id(0) == 0)
    def _():
        key_place = lax.broadcasted_iota(jnp.int32, (rows, keys), 1)
        query_place = me_ref[0] * rows + lax.broadcasted_iota(jnp.int32, (rows, keys), 0)
        allowed = (key_place <= query_place) & (key_place >= first_ref[...])
        bias[...] = jnp.where(allowed, 0.0, NEG)

    scores = nt(q_ref[...], k_ref[...]) * scale + bias[...]
    top = jnp.max(scores, axis=-1, keepdims=True)
    weights = jnp.exp(scores - top)
    total = jnp.sum(weights, axis=-1, keepdims=True)
    o_ref[...] = nn(weights.astype(BF), v_ref[...]) / total
    log_ref[...] = jnp.broadcast_to(top + jnp.log(total), (rows, 8))[None]


def attend(me, qkv, first_own):
    keys = qkv.shape[0]
    rows = first_own.shape[0]
    return pl.pallas_call(
        functools.partial(attend_kernel, HD**-0.5),
        out_shape=[
            jax.ShapeDtypeStruct((rows, H * HD), F32),
            jax.ShapeDtypeStruct((H, rows, 8), F32),
        ],
        grid_spec=pltpu.PrefetchScalarGridSpec(
            num_scalar_prefetch=1,
            grid=(H,),
            in_specs=[
                pl.BlockSpec((rows, HD), lambda h, me: (me[0], h)),
                pl.BlockSpec((keys, HD), lambda h, me: (0, H + h)),
                pl.BlockSpec((keys, HD), lambda h, me: (0, 2 * H + h)),
                pl.BlockSpec((rows, 1), lambda h, me: (0, 0)),
            ],
            out_specs=[
                pl.BlockSpec((rows, HD), lambda h, me: (0, h)),
                pl.BlockSpec((1, rows, 8), lambda h, me: (h, 0, 0)),
            ],
            scratch_shapes=[pltpu.VMEM((rows, keys), F32)],
        ),
        compiler_params=params(),
        cost_estimate=pl.CostEstimate(
            flops=4 * rows * keys * H * HD,
            bytes_accessed=4 * keys * H * HD,
            transcendentals=H * rows * keys,
        ),
    )(me, qkv, qkv, qkv, first_own[:, None])


def attend_back_kernel(
    scale,
    me_ref,
    q_ref,
    k_ref,
    v_ref,
    qa_ref,
    ko_ref,
    vo_ref,
    do_ref,
    da_ref,
    log_ref,
    delta_ref,
    loga_ref,
    deltaa_ref,
    first_ref,
    firsta_ref,
    cos_ref,
    sin_ref,
    o_ref,
    bias,
    biast,
):
    rows, keys = bias.shape

    @pl.when(pl.program_id(0) == 0)
    def _():
        place = lax.broadcasted_iota(jnp.int32, (rows, keys), 1)
        own = me_ref[0] * rows + lax.broadcasted_iota(jnp.int32, (rows, keys), 0)
        bias[...] = jnp.where((place <= own) & (place >= first_ref[...]), 0.0, NEG)
        biast[...] = jnp.where((own <= place) & (own >= firsta_ref[...]), 0.0, NEG)

    def unturn(value):
        return value * cos_ref[...] - pltpu.roll(value, HD // 2, 1) * sin_ref[...]

    log_own = log_ref[0][:, :1]
    delta_own = delta_ref[0][:, :1]
    weights = jnp.exp(nt(q_ref[...], k_ref[...]) * scale + bias[...] - log_own)
    back = nt(do_ref[...], v_ref[...])
    grad = (weights * (back - delta_own) * scale).astype(BF)
    o_ref[0] = unturn(nn(grad, k_ref[...])).astype(BF)

    weights = jnp.exp(nt(ko_ref[...], qa_ref[...]) * scale + biast[...] - loga_ref[0])
    o_ref[2] = nn(weights.astype(BF), da_ref[...]).astype(BF)
    back = nt(vo_ref[...], da_ref[...])
    grad = (weights * (back - deltaa_ref[0]) * scale).astype(BF)
    o_ref[1] = unturn(nn(grad, qa_ref[...])).astype(BF)


def attend_back(me, qkv, grad_own, grad_all, log_own, delta_own, log_all, delta_all, first, cosine, sine):
    keys = qkv.shape[0]
    rows = grad_own.shape[0]
    first_own, first_all = first
    return pl.pallas_call(
        functools.partial(attend_back_kernel, HD**-0.5),
        out_shape=jax.ShapeDtypeStruct((3, rows, H * HD), BF),
        grid_spec=pltpu.PrefetchScalarGridSpec(
            num_scalar_prefetch=1,
            grid=(H,),
            in_specs=[
                pl.BlockSpec((rows, HD), lambda h, me: (me[0], h)),
                pl.BlockSpec((keys, HD), lambda h, me: (0, H + h)),
                pl.BlockSpec((keys, HD), lambda h, me: (0, 2 * H + h)),
                pl.BlockSpec((keys, HD), lambda h, me: (0, h)),
                pl.BlockSpec((rows, HD), lambda h, me: (me[0], H + h)),
                pl.BlockSpec((rows, HD), lambda h, me: (me[0], 2 * H + h)),
                pl.BlockSpec((rows, HD), lambda h, me: (0, h)),
                pl.BlockSpec((keys, HD), lambda h, me: (0, h)),
                pl.BlockSpec((1, rows, 8), lambda h, me: (h, 0, 0)),
                pl.BlockSpec((1, rows, 8), lambda h, me: (h, 0, 0)),
                pl.BlockSpec((1, 1, keys), lambda h, me: (h, 0, 0)),
                pl.BlockSpec((1, 1, keys), lambda h, me: (h, 0, 0)),
                pl.BlockSpec((rows, 1), lambda h, me: (0, 0)),
                pl.BlockSpec((1, keys), lambda h, me: (0, 0)),
                pl.BlockSpec((rows, HD), lambda h, me: (0, 0)),
                pl.BlockSpec((rows, HD), lambda h, me: (0, 0)),
            ],
            out_specs=pl.BlockSpec((3, rows, HD), lambda h, me: (0, 0, h)),
            scratch_shapes=[pltpu.VMEM((rows, keys), F32)] * 2,
        ),
        compiler_params=params(),
        cost_estimate=pl.CostEstimate(
            flops=14 * rows * keys * H * HD,
            bytes_accessed=8 * keys * H * HD,
            transcendentals=2 * H * rows * keys,
        ),
    )(
        me,
        qkv,
        qkv,
        qkv,
        qkv,
        qkv,
        qkv,
        grad_own,
        grad_all,
        log_own,
        delta_own,
        log_all,
        delta_all,
        first_own[:, None],
        first_all[None, :],
        cosine,
        sine,
    )


def moe_kernel(
    chips,
    experts,
    x_own,
    routes,
    grads,
    misc,
    weights,
    row_out,
    thin_out,
    mid_out,
    grad_out,
    x_all,
    g_all,
    w,
    hid,
    part,
    other,
    came,
    thin,
    dots,
    s_load,
    s_x,
    r_x,
    s_fwd,
    r_fwd,
    s_part,
    r_part,
    s_came,
    r_came,
    s_thin,
    r_thin,
):
    at = Place(chips)
    z, c = at.z, at.c
    chain = 2 * chips
    rows, width = x_own.shape
    both = w.shape[2]
    tiles = both // 256
    per_expert = both // 256
    greet([(at.d, lax.rem(at.e + k, chain)) for k in range(1, chain)], [None] * (chain - 1))

    near = jnp.minimum(z, chips - 1 - z)

    def order(j):
        step = (j + 1) // 2
        around = jnp.where(j % 2 == 1, z - step, z + step)
        return jnp.where(j <= 2 * near, around, jnp.where(2 * z < chips, j, chips - 1 - j))

    def own_load():
        return pltpu.make_async_copy(x_own, x_all.at[z, c], s_load.at[0])

    hidden = both // EXP_DEV

    def weight_load(k, e):
        return pltpu.make_async_copy(
            weights.at[k, e], w.at[k, :, pl.ds(e * hidden, hidden)], s_load.at[2 + 2 * k + e]
        )

    def grad_store(k, e):
        return pltpu.make_async_copy(
            w.at[k, :, pl.ds(e * hidden, hidden)], grad_out.at[k, e], s_load.at[2 + 2 * k + e]
        )

    def grads_load():
        return pltpu.make_async_copy(grads, g_all, s_load.at[1])

    def x_send(zz):
        return sent(x_own, x_all.at[z, c], s_x.at[zz], r_x.at[z], (at.d, 2 * zz + c))

    def x_came(zz):
        ref = x_all.at[zz, c]
        return sent(ref, ref, s_x.at[zz], r_x.at[zz], (at.d, 2 * zz + c))

    def forward(zz):
        ref = x_all.at[zz, c]
        return sent(ref, ref, s_fwd.at[zz], r_fwd.at[zz], at.sibling)

    def forwarded(zz):
        ref = x_all.at[zz, 1 - c]
        return sent(ref, ref, s_fwd.at[zz], r_fwd.at[zz], at.sibling)

    def part_send(zz):
        return sent(part.at[zz, 1 - c], other.at[zz], s_part.at[zz], r_part.at[zz], at.sibling)

    def came_send(zz):
        return sent(part.at[zz, c], came.at[z], s_came.at[zz], r_came.at[z], (at.d, 2 * zz + c))

    def came_here(zz):
        return sent(part.at[zz, c], came.at[zz], s_came.at[zz], r_came.at[zz], (at.d, 2 * zz + c))

    def thin_send(zz, cc):
        return sent(
            thin.at[zz], thin_out.at[at.e], s_thin.at[2 * zz + cc], r_thin.at[at.e], (at.d, 2 * zz + cc)
        )

    def thin_here(e):
        return sent(thin.at[0], thin_out.at[e], s_thin.at[e], r_thin.at[e], (at.d, e))

    own_load().start()
    sent(x_own, x_all.at[z, c], s_fwd.at[z], r_fwd.at[z], at.sibling).start()
    for j in range(1, chips):
        x_send(order(j)).start()
    for k in range(3):
        for e in range(EXP_DEV):
            weight_load(k, e).start()
    grads_load().start()
    own_load().wait()

    lanes = lax.broadcasted_iota(jnp.int32, (2 * rows, 128), 1)

    def gates_of(zz, x):
        logits = jnp.where(lanes < experts, nn(x, misc[...]), NEG)
        powers = jnp.exp(logits - jnp.max(logits, axis=1, keepdims=True))
        probs = powers / jnp.sum(powers, axis=1, keepdims=True)
        named = routes[zz][:, 0:1] == lanes
        for j in range(1, TOP):
            named = named | (routes[zz][:, j : j + 1] == lanes)
        chosen = jnp.where(named, probs, 0.0)
        gates = chosen / jnp.sum(chosen, axis=1, keepdims=True)
        return [
            jnp.sum(jnp.where(lanes == EXP_DEV * at.e + k, gates, 0.0), axis=1, keepdims=True)
            for k in range(EXP_DEV)
        ]

    def settle(zz):
        part_send(zz).wait_recv()
        total = part[zz, c].astype(F32) + other[zz].astype(F32)

        @pl.when(zz == z)
        def _():
            row_out[...] = total

        @pl.when(zz != z)
        def _():
            part[zz, c] = total.astype(BF)
            came_send(zz).start()

    def block(j, carry):
        zz = order(j)
        forwarded(zz).wait_recv()
        here = pl.ds(pl.multiple_of(zz * 2 * rows, 2 * rows), 2 * rows)
        x = x_all[zz].reshape(2 * rows, width)
        first, second = gates_of(zz, x)
        dots[...] = jnp.zeros_like(dots)

        @pl.when(j == 0)
        def _():
            for k in range(3):
                for e in range(EXP_DEV):
                    weight_load(k, e).wait()
            grads_load().wait()

        def tile(n, carry):
            cols = pl.ds(pl.multiple_of(n * 256, 256), 256)
            x = x_all[zz].reshape(2 * rows, width)
            g = g_all[zz].reshape(2 * rows, width)
            gate_v = nn(x, w[0, :, cols])
            up_v = nn(x, w[1, :, cols])
            back = nn(g, w[2, :, cols])
            for half in (0, 1):
                s = slice(half * 128, half * 128 + 128)
                is_first = 2 * n + half < per_expert
                gate = jnp.where(is_first, first, second)
                v, u, b = gate_v[:, s], up_v[:, s], back[:, s]
                sig = jax.nn.sigmoid(v)
                act = v * sig
                mid = act * u
                dots[0] += mid * b * is_first.astype(F32)
                dots[1] += mid * b * (1.0 - is_first.astype(F32))
                b = gate * b
                to = pl.ds(pl.multiple_of(n * 256 + half * 128, 128), 128)
                hid[2, here, to] = (gate * mid).astype(BF)
                hid[0, here, to] = (b * u * (sig * (1.0 + v * (1.0 - sig)))).astype(BF)
                hid[1, here, to] = (b * act).astype(BF)
            return carry

        early = (tiles + 1) // 2
        lax.fori_loop(0, early, tile, 0, unroll=True)

        @pl.when(j + 1 < chips)
        def _():
            x_came(order(j + 1)).wait_recv()
            forward(order(j + 1)).start()

        @pl.when(j > 0)
        def _():
            settle(order(j - 1))

        lax.fori_loop(early, tiles, tile, 0, unroll=True)

        def row_tile(n, carry):
            cols = pl.ds(pl.multiple_of(n * 256, 256), 256)
            row = nt(hid[0, here, :], w[0, cols, :]) + nt(hid[1, here, :], w[1, cols, :])
            part[zz, 0, :, cols] = row[:rows].astype(BF)
            part[zz, 1, :, cols] = row[rows:].astype(BF)
            return carry

        lax.fori_loop(0, width // 256, row_tile, 0, unroll=True)
        part_send(zz).start()
        column = jnp.where(
            lanes == 0,
            jnp.sum(dots[0], axis=1, keepdims=True),
            jnp.sum(dots[1], axis=1, keepdims=True),
        )
        thin[zz] = column.T[:8]

        @pl.when(zz == z)
        def _():
            thin_out[at.e] = thin[zz]

        for cc in (0, 1):

            @pl.when(2 * zz + cc != at.e)
            def _(cc=cc):
                thin_send(zz, cc).start()

        return carry

    lax.fori_loop(0, chips, block, 0)
    settle(order(chips - 1))
    mid_store = pltpu.make_async_copy(hid.at[2], mid_out, s_load.at[0])
    mid_store.start()
    for k in (2, 0, 1):

        def grad_tile(n, carry, k=k):
            cols = pl.ds(pl.multiple_of(n * 256, 256), 256)
            left = g_all if k == 2 else x_all
            left = left[...].reshape(chain * rows, width)
            w[k, :, cols] = tn(left, hid[k, :, cols]).astype(BF)
            return carry

        lax.fori_loop(0, tiles, grad_tile, 0, unroll=True)
        for e in range(EXP_DEV):
            grad_store(k, e).start()

    for zz in range(chips):

        @pl.when(zz != z)
        def _(zz=zz):
            came_here(zz).wait_recv()
            row_out[...] += came[zz].astype(F32)
            came_send(zz).wait_send()
            x_send(zz).wait_send()

        part_send(zz).wait_send()
        forward(zz).wait_send()
        for cc in (0, 1):

            @pl.when(2 * zz + cc != at.e)
            def _(zz=zz, cc=cc):
                thin_here(2 * zz + cc).wait_recv()
                thin_send(zz, cc).wait_send()

    mid_store.wait()
    for k in range(3):
        for e in range(EXP_DEV):
            grad_store(k, e).wait()


def moe_fused(normed, routes_all, grads_all, misc, weights, experts, collective_id):
    rows, width = normed.shape
    chain = routes_all.shape[0] // rows
    chips = chain // 2
    both = EXP_DEV * weights.shape[3]
    dma = pltpu.SemaphoreType.DMA
    blocks = (chips, 2, rows, width)
    anywhere = pl.BlockSpec(memory_space=pl.ANY)
    vmem = pl.BlockSpec(memory_space=pltpu.VMEM)
    return pl.pallas_call(
        functools.partial(moe_kernel, chips, experts),
        out_shape=[
            jax.ShapeDtypeStruct((rows, width), F32),
            jax.ShapeDtypeStruct((chain, 8, 2 * rows), F32),
            jax.ShapeDtypeStruct((chain * rows, both), BF),
            jax.ShapeDtypeStruct(weights.shape, BF),
        ],
        in_specs=[anywhere, vmem, anywhere, vmem, anywhere],
        out_specs=[vmem, vmem, anywhere, anywhere],
        scratch_shapes=[
            pltpu.VMEM(blocks, BF),
            pltpu.VMEM(blocks, BF),
            pltpu.VMEM((3, width, both), BF),
            pltpu.VMEM((3, chain * rows, both), BF),
            pltpu.VMEM(blocks, BF),
            pltpu.VMEM((chips, rows, width), BF),
            pltpu.VMEM((chips, rows, width), BF),
            pltpu.VMEM((chips, 8, 2 * rows), F32),
            pltpu.VMEM((2, 2 * rows, 128), F32),
            dma((8,)),
        ]
        + [dma((chips,))] * 8
        + [dma((chain,))] * 2,
        compiler_params=pltpu.CompilerParams(
            vmem_limit_bytes=MOE_VMEM, collective_id=collective_id, has_side_effects=True
        ),
        cost_estimate=pl.CostEstimate(
            flops=16 * chain * rows * width * both,
            bytes_accessed=4 * weights.size + 4 * chain * rows * both,
            transcendentals=chain * rows * both,
        ),
    )(
        normed,
        routes_all.reshape(chips, 2 * rows, TOP),
        grads_all.reshape(blocks),
        misc,
        weights,
    )


def moe_plain(moe_all, gates_here, grads_all, weights):
    keys, width = moe_all.shape
    hidden = weights.shape[3]
    at_once = 768 if keys % 768 == 0 else keys

    def some(rows):
        x, gates, g = rows
        row = jnp.zeros(x.shape, F32)
        dots, mids, gate_vs, up_vs = [], [], [], []
        for e in range(EXP_DEV):
            scale = gates[:, e : e + 1]
            gate_v = nn(x, weights[0, e])
            up_v = nn(x, weights[1, e])
            back = nn(g, weights[2, e])
            act, slope = silu_parts(gate_v)
            mid = act * up_v
            dots.append(jnp.sum(mid * back, axis=1))
            back = back * scale
            gate_vs.append((back * up_v * slope).astype(BF))
            up_vs.append((back * act).astype(BF))
            mids.append((mid * scale).astype(BF))
            row = row + nt(gate_vs[e], weights[0, e]) + nt(up_vs[e], weights[1, e])
        return (
            row.astype(BF),
            jnp.stack(dots, axis=1),
            jnp.concatenate(mids, axis=1),
            jnp.concatenate(gate_vs, axis=1),
            jnp.concatenate(up_vs, axis=1),
        )

    cut = jax.tree.map(
        lambda a: a.reshape((keys // at_once, at_once) + a.shape[1:]), (moe_all, gates_here, grads_all)
    )
    row, dots, mid, gate_v, up_v = jax.tree.map(
        lambda a: a.reshape((keys,) + a.shape[2:]), lax.map(some, cut)
    )

    def grad_of(x, h):
        grad = tn(x, h).astype(BF).reshape(width, EXP_DEV, hidden)
        return jnp.swapaxes(grad, 0, 1)

    weight_grads = jnp.stack(
        [grad_of(moe_all, gate_v), grad_of(moe_all, up_v), grad_of(grads_all, mid)]
    )
    return row, dots, mid, weight_grads


def spread_kernel(
    chips,
    own,
    side,
    mid,
    weights,
    rows_in,
    gate_in,
    up_in,
    cot_in,
    shared_in,
    attn_in,
    attended_in,
    all_out,
    side_out,
    mix_out,
    gate_out,
    up_out,
    down_out,
    out_out,
    mids,
    w,
    mix,
    dense,
    wide,
    s_load,
    s_dense,
    s_chain,
    r_chain,
    s_core,
    r_core,
    s_side,
    r_side,
    s_score,
    r_score,
):
    at = Place(chips)
    z, c = at.z, at.c
    hidden = gate_in.shape[1]
    rows = own.shape[0]
    others = [(at.d, 2 * lax.rem(z + k, chips) + c) for k in range(1, chips)]
    greet([at.sibling] + others, [None] * chips)

    pairs = ((own, all_out, s_chain, r_chain, s_core, r_core), (side, side_out, s_side, r_side, s_score, r_score))

    def along(p, k, src=None):
        source, out, ss, rs = pairs[p][:4]
        zz = lax.rem(z + k, chips)
        ref = out.at[2 * z + c]
        return sent(source if src is None else src, ref, ss.at[zz], rs.at[z], (at.d, 2 * zz + c))

    def along_here(p, zz):
        source, out, ss, rs = pairs[p][:4]
        ref = out.at[2 * zz + c]
        return sent(ref, ref, ss.at[zz], rs.at[zz], (at.d, 2 * zz + c))

    def over(p, zz, core, src=None):
        out, ss, rs = pairs[p][1], pairs[p][4], pairs[p][5]
        ref = out.at[2 * zz + core]
        return sent(ref if src is None else src, ref, ss.at[zz], rs.at[zz], at.sibling)

    near = jnp.minimum(z, chips - 1 - z)

    def order(j):
        step = (j + 1) // 2
        around = jnp.where(j % 2 == 1, z - step, z + step)
        return jnp.where(j <= 2 * near, around, jnp.where(2 * z < chips, j, chips - 1 - j))

    for j in range(1, chips):
        for p in (1, 0):
            along(p, lax.rem(order(j) - z + chips, chips)).start()
    locals_ = []
    for p in (1, 0):
        over(p, z, c, pairs[p][0]).start()
        copy = pltpu.make_async_copy(pairs[p][0], pairs[p][1].at[2 * z + c], s_load.at[p])
        copy.start()
        locals_.append(copy)
    loads = [
        pltpu.make_async_copy(weights.at[2, e], w.at[:, pl.ds(e * hidden, hidden)], s_load.at[2 + e])
        for e in range(EXP_DEV)
    ]
    loads.append(pltpu.make_async_copy(mid, mids, s_load.at[2 + EXP_DEV]))
    for copy in loads:
        copy.start()

    stores = []
    dense[0] = tn(rows_in[...], gate_in[...]).astype(BF)
    dense[1] = tn(rows_in[...], up_in[...]).astype(BF)
    dense[2] = tn(cot_in[...], shared_in[...]).astype(BF)
    wide[...] = tn(attn_in[...], attended_in[...]).astype(BF)
    for k, (src, dst) in enumerate(
        ((dense.at[0], gate_out), (dense.at[1], up_out), (dense.at[2], down_out), (wide, out_out))
    ):
        copy = pltpu.make_async_copy(src, dst, s_dense.at[k])
        copy.start()
        stores.append(copy)
    for copy in loads:
        copy.wait()

    def mix_chip(zz):
        here = pl.ds(zz * 2 * rows, 2 * rows)
        for n in range(0, own.shape[1], 256):
            tile = nt(mids[here, :], w[n : n + 256, :]).astype(BF)
            mix[zz, 0, :, n : n + 256] = tile[:rows]
            mix[zz, 1, :, n : n + 256] = tile[rows:]
        copy = pltpu.make_async_copy(mix.at[zz], mix_out.at[zz], s_dense.at[4 + zz])
        copy.start()
        stores.append(copy)

    for j in range(chips):
        mix_chip(j)
        if j >= 1:
            zz = order(j)
            for p in (1, 0):
                along_here(p, zz).wait_recv()
                over(p, zz, c).start()
    for p in (1, 0):
        for zz in range(chips):
            over(p, zz, 1 - c).wait_recv()
            over(p, zz, c).wait_send()

            @pl.when(zz != z)
            def _(p=p, zz=zz):
                along_here(p, zz).wait_send()

    for copy in locals_ + stores:
        copy.wait()


def spread(own, side, mid, weights, normed, gate_grad, up_grad, cot, shared_mid, attn, attended, collective_id):
    rows, width = own.shape
    keys, both = mid.shape
    chain = keys // rows
    chips = chain // 2
    hidden = gate_grad.shape[1]
    dma = pltpu.SemaphoreType.DMA
    anywhere = pl.BlockSpec(memory_space=pl.ANY)
    vmem = pl.BlockSpec(memory_space=pltpu.VMEM)
    return pl.pallas_call(
        functools.partial(spread_kernel, chips),
        out_shape=[
            jax.ShapeDtypeStruct((chain,) + own.shape, BF),
            jax.ShapeDtypeStruct((chain,) + side.shape, F32),
            jax.ShapeDtypeStruct((chips, 2, rows, width), BF),
            jax.ShapeDtypeStruct((width, hidden), BF),
            jax.ShapeDtypeStruct((width, hidden), BF),
            jax.ShapeDtypeStruct((width, hidden), BF),
            jax.ShapeDtypeStruct((width, width), BF),
        ],
        in_specs=[anywhere] * 4 + [vmem] * 7,
        out_specs=[anywhere] * 7,
        scratch_shapes=[
            pltpu.VMEM((keys, both), BF),
            pltpu.VMEM((width, both), BF),
            pltpu.VMEM((chips, 2, rows, width), BF),
            pltpu.VMEM((3, width, hidden), BF),
            pltpu.VMEM((width, width), BF),
            dma((3 + EXP_DEV,)),
            dma((4 + chips,)),
        ]
        + [dma((chips,))] * 8,
        compiler_params=params(collective_id=collective_id, has_side_effects=True),
        cost_estimate=pl.CostEstimate(
            flops=2 * keys * both * width, bytes_accessed=64 * keys * width, transcendentals=0
        ),
    )(own, side, mid, weights, normed, gate_grad, up_grad, cot, shared_mid, attn, attended)


def finish_kernel(chips, chunks, n_in, experts, *refs):
    ins = refs[:n_in]
    normed, projected, weight_in, misc_in, unit, inverse, gain, grad_middle, mix_in, base = refs[
        n_in : n_in + 10
    ]
    n_out = n_in + 2
    outs = refs[n_in + 10 : n_in + 10 + n_out]
    input_out, output_out = refs[n_in + 10 + n_out : n_in + 12 + n_out]
    rest = refs[n_in + 12 + n_out :]
    s_in, s_core, r_core, s_one, r_one, s_two, r_two, s_end, r_end = rest[:9]
    s_mix, s_mcore, r_mcore, s_mchain, r_mchain, s_weight = rest[9:15]
    weight, grad_ref, tile_ref, mix_mine, mix_other, mix_came = rest[15:21]
    buffers = rest[21:]
    n_chunks = len(chunks)
    at = Place(chips)
    z, c, x, y = at.z, at.c, at.x, at.y
    chain = 2 * chips
    others = [(at.d, 2 * lax.rem(z + k, chips) + c) for k in range(1, chips)]
    devices = [at.sibling, at.across_x, at.across_y] + others
    greet(devices, [None] * len(devices))

    class Chunk:
        def __init__(self, q):
            self.i, self.first, self.wide = chunks[q]
            self.q = q
            self.made = self.i >= n_in
            self.mine, self.other, one_x, one_y, two_x, two_y, self.end, self.give = buffers[
                8 * q : 8 * q + 8
            ]
            self.one, self.two = (one_x, one_y), (two_x, two_y)
            self.cols = pl.ds(self.first, self.wide)
            cut = self.wide // 256 * 128
            self.half = (pl.ds(0, cut), pl.ds(cut, self.wide - cut))

        def load(self):
            return pltpu.make_async_copy(
                ins[self.i].at[:, :, :, c, :, self.cols], self.mine, s_in.at[self.q]
            )

        def core(self):
            source = self.give if self.made else ins[self.i].at[:, :, :, 1 - c, :, self.cols]
            return sent(source, self.other, s_core.at[self.q], r_core.at[self.q], at.sibling)

        def first_x(self):
            return sent(
                self.mine.at[:, 1 - x, :, :, self.half[0]],
                self.one[0],
                s_one.at[self.q, 0],
                r_one.at[self.q, 0],
                at.across_x,
            )

        def first_y(self):
            return sent(
                self.mine.at[1 - y, :, :, :, self.half[1]],
                self.one[1],
                s_one.at[self.q, 1],
                r_one.at[self.q, 1],
                at.across_y,
            )

        def second_y(self):
            return sent(
                self.mine.at[1 - y, x, :, :, self.half[0]],
                self.two[0],
                s_two.at[self.q, 0],
                r_two.at[self.q, 0],
                at.across_y,
            )

        def second_x(self):
            return sent(
                self.mine.at[y, 1 - x, :, :, self.half[1]],
                self.two[1],
                s_two.at[self.q, 1],
                r_two.at[self.q, 1],
                at.across_x,
            )

        def last(self, k):
            zz = lax.rem(z + k, chips)
            return sent(
                self.mine.at[y, x, zz],
                self.end.at[k - 1],
                s_end.at[self.q, k - 1],
                r_end.at[self.q, k - 1],
                (at.d, 2 * zz + c),
            )

        def take(self):
            block = self.mine.shape[3]

            def body(k, carry):
                yy, xx, zz = k // (2 * chips), (k // chips) % 2, k % chips
                row = (2 * yy + xx) * chain + 2 * zz
                keep = pl.ds(pl.multiple_of((row + c) * block, block), block)
                away = pl.ds(pl.multiple_of((row + 1 - c) * block, block), block)
                self.mine[yy, xx, zz] = tile_ref[keep, : self.wide].astype(BF)
                self.give[yy, xx, zz] = tile_ref[away, : self.wide].astype(BF)
                return carry

            lax.fori_loop(0, 4 * chips, body, 0, unroll=4)
            self.core().start()

    parts = [Chunk(q) for q in range(n_chunks)]

    def stage_one(p):
        p.core().wait_recv()
        if not p.made:
            p.load().wait()

        def body(k, carry):
            yy, xx, zz = k // (2 * chips), (k // chips) % 2, k % chips
            p.mine[yy, xx, zz] = p.mine[yy, xx, zz] + p.other[yy, xx, zz]
            return carry

        lax.fori_loop(0, 4 * chips, body, 0, unroll=4)
        p.first_x().start()
        p.first_y().start()

    def stage_two(p):
        p.first_x().wait_recv()
        p.first_y().wait_recv()

        def body(k, carry):
            v, zz = k // chips, k % chips
            a, b = p.half
            p.mine[v, x, zz, :, a] = p.mine[v, x, zz, :, a] + p.one[0][v, zz]
            p.mine[y, v, zz, :, b] = p.mine[y, v, zz, :, b] + p.one[1][v, zz]
            return carry

        lax.fori_loop(0, 2 * chips, body, 0, unroll=2)
        p.second_y().start()
        p.second_x().start()

    def stage_three(p):
        p.second_y().wait_recv()
        p.second_x().wait_recv()

        def body(zz, carry):
            for w in (0, 1):
                s = p.half[w]
                p.mine[y, x, zz, :, s] = p.mine[y, x, zz, :, s] + p.two[w][zz]
            return carry

        lax.fori_loop(0, chips, body, 0, unroll=2)
        for k in range(1, chips):
            p.last(k).start()

    def stage_four(p):
        total = p.mine[y, x, z].astype(F32)
        for k in range(1, chips):
            p.last(k).wait_recv()
            total = total + p.end[k - 1].astype(F32)
        outs[p.i][:, p.first : p.first + p.wide] = total

    def mix_load(zz):
        return pltpu.make_async_copy(mix_in.at[zz, c], mix_mine.at[zz], s_mix.at[zz])

    def mix_core(zz):
        return sent(
            mix_in.at[zz, 1 - c], mix_other.at[zz], s_mcore.at[zz], r_mcore.at[zz], at.sibling
        )

    def mix_over(k):
        zz = lax.rem(z + k, chips)
        return sent(
            mix_mine.at[zz], mix_came.at[k], s_mchain.at[k], r_mchain.at[k], (at.d, 2 * zz + c)
        )

    def mix_settle():
        for k in range(1, chips):
            zz = lax.rem(z + k, chips)
            mix_core(zz).wait_recv()
            mix_load(zz).wait()
            mix_mine[zz] = (mix_mine[zz].astype(F32) + mix_other[zz].astype(F32)).astype(BF)
            mix_over(k).start()
        mix_core(z).wait_recv()
        mix_load(z).wait()

    part = projected.shape[2]

    def weight_load(k):
        return pltpu.make_async_copy(
            weight_in.at[:, pl.ds(k * part, part)], weight, s_weight.at[0]
        )

    def input_grads(k):
        weight_load(k).wait()
        if k == 0:
            grad_ref[...] = nt(projected[0], weight[...])
        else:
            grad_ref[...] += nt(projected[k], weight[...])
        if k < 2:
            weight_load(k + 1).start()
            return
        grad = grad_ref[...]
        gains = jnp.sum(grad * unit[...], axis=0, keepdims=True)
        column = jnp.broadcast_to(gains, (8, part)).T[:, :1]
        lanes = lax.broadcasted_iota(jnp.int32, misc_in.shape, 1)
        tile_ref[:, : misc_in.shape[1]] = jnp.where(lanes == experts, column, misc_in[...])
        scaled = grad * gain[...]
        mean = jnp.mean(scaled * unit[...], axis=1, keepdims=True)
        input_out[...] = (grad_middle[...] + inverse[...] * (scaled - unit[...] * mean)).astype(BF)

    for k in range(1, chips + 1):
        zz = lax.rem(z + k, chips)
        mix_core(zz).start()
        mix_load(zz).start()
    for p in parts:
        if not p.made:
            p.core().start()
            p.load().start()
    weight_load(0).start()
    mix_settle()
    n_known = sum(not p.made for p in parts)
    n_made = n_chunks - 1 - n_known
    stages = ((0, stage_one), (1, stage_two), (2, stage_three), (6, stage_four))
    for t in range(n_chunks + stages[-1][0]):
        for lag, stage in stages:
            if 0 <= t - lag < n_chunks:
                stage(parts[t - lag])
        if t < n_made:
            p = parts[n_known + t]
            k, first = p.first // part, p.first % part
            tile_ref[:, : p.wide] = tn(normed[...], projected[k, :, first : first + p.wide])
            p.take()
        elif t < n_made + 3:
            input_grads(t - n_made)
            if t == n_made + 2:
                parts[-1].take()
    total = base[...] + mix_mine[z].astype(F32) + mix_other[z].astype(F32)
    for k in range(1, chips):
        mix_over(k).wait_recv()
        total = total + mix_came[k].astype(F32)
    output_out[...] = total.astype(BF)
    for p in parts:
        p.core().wait_send()
        p.first_x().wait_send()
        p.first_y().wait_send()
        p.second_x().wait_send()
        p.second_y().wait_send()
        for k in range(1, chips):
            p.last(k).wait_send()
    for k in range(1, chips):
        mix_over(k).wait_send()
    for zz in range(chips):
        mix_core(zz).wait_send()


def finish(
    arrays,
    chunk_widths,
    experts,
    normed,
    projected,
    qkv_weight,
    misc,
    unit,
    inverse,
    gain,
    grad_middle,
    mix,
    base,
    collective_id,
):
    chain = lax.axis_size("expert")
    chips = chain // 2
    width = arrays[0].shape[0]
    block = width // (4 * chain)
    rows = normed.shape[0]
    columns = qkv_weight.shape[1]
    n = len(arrays)
    dma = pltpu.SemaphoreType.DMA
    sizes = [a.shape[1] for a in arrays] + [columns, misc.shape[1]]
    chunks = []
    for i, (size, wide) in enumerate(zip(sizes, chunk_widths)):
        assert size % wide == 0 and wide % 128 == 0 and wide >= 256
        chunks += [(i, first, wide) for first in range(0, size, wide)]
    q = len(chunks)
    scratch = [dma((q,)), dma((q,)), dma((q,))] + [dma((q, 2))] * 4 + [dma((q, chips - 1))] * 2
    scratch += [dma((chips,))] * 5 + [dma((1,))]
    scratch += [
        pltpu.VMEM((width, columns // 3), BF),
        pltpu.VMEM((rows, width), F32),
        pltpu.VMEM((width, max(chunk_widths[n:])), F32),
        pltpu.VMEM((chips, rows, width), BF),
        pltpu.VMEM((chips, rows, width), BF),
        pltpu.VMEM((chips, rows, width), BF),
    ]
    for i, first, wide in chunks:
        cut = wide // 256 * 128
        scratch += [
            pltpu.VMEM((2, 2, chips, block, wide), BF),
            pltpu.VMEM((2, 2, chips, block, wide), BF),
            pltpu.VMEM((2, chips, block, cut), BF),
            pltpu.VMEM((2, chips, block, wide - cut), BF),
            pltpu.VMEM((chips, block, cut), BF),
            pltpu.VMEM((chips, block, wide - cut), BF),
            pltpu.VMEM((chips - 1, block, wide), BF),
            pltpu.VMEM((2, 2, chips, block, wide) if i >= n else (16, 128), BF),
        ]
    anywhere = pl.BlockSpec(memory_space=pl.ANY)
    vmem = pl.BlockSpec(memory_space=pltpu.VMEM)
    return pl.pallas_call(
        functools.partial(finish_kernel, chips, tuple(chunks), n, experts),
        out_shape=[jax.ShapeDtypeStruct((block, size), F32) for size in sizes]
        + [jax.ShapeDtypeStruct((rows, width), BF)] * 2,
        in_specs=[anywhere] * n
        + [vmem, vmem, anywhere, vmem, vmem, vmem, vmem, vmem, anywhere, vmem],
        out_specs=[vmem] * (n + 4),
        scratch_shapes=scratch,
        compiler_params=pltpu.CompilerParams(
            vmem_limit_bytes=MOE_VMEM, collective_id=collective_id, has_side_effects=True
        ),
        cost_estimate=pl.CostEstimate(
            flops=4 * rows * width * columns, bytes_accessed=64 * width * columns, transcendentals=0
        ),
    )(
        *[a.reshape(2, 2, chips, 2, block, a.shape[1]) for a in arrays],
        normed,
        projected,
        qkv_weight,
        misc,
        unit,
        inverse,
        gain,
        grad_middle,
        mix,
        base,
    )


def silu_parts(values):
    s = jax.nn.sigmoid(values)
    return values * s, s * (1.0 + values * (1.0 - s))


def local(
    tokens,
    cotangent,
    lengths,
    routes,
    attn_qkv,
    attn_out,
    shared_gate,
    shared_up,
    shared_down,
    router,
    gains,
    expert_gate,
    expert_up,
    expert_down,
):
    rows = tokens.shape[1]
    width = tokens.shape[2]
    hidden = shared_gate.shape[1]
    chain = lax.axis_size("expert")
    index = lax.axis_index("expert")
    experts = EXP_DEV * chain
    everyone = ("dp", "expert")
    keys = rows * chain
    own_first = index * rows
    me = index.reshape(1).astype(jnp.int32)

    route_pad = 128 * (-(-(experts + 2) // 128))
    misc = jnp.concatenate([router.astype(BF), gains.astype(BF).T], axis=1)
    misc = jnp.pad(misc, ((0, 0), (0, route_pad - experts - 2)))
    near = jnp.concatenate([misc, attn_out.astype(BF).T], axis=1)
    expert_shard = jnp.stack(
        [expert_gate.astype(BF), expert_up.astype(BF), jnp.swapaxes(expert_down.astype(BF), 1, 2)]
    )
    expert_weight = lax.all_gather(expert_shard, "dp", axis=2, tiled=True)
    shared = jnp.concatenate(
        [shared_gate.astype(BF), shared_up.astype(BF), shared_down.astype(BF).T], axis=1
    )
    fits = 2 * width * EXP_DEV * hidden * 3 + 2 * keys * (3 * EXP_DEV * hidden + 5 * width) < MOE_VMEM
    chained = [tokens[0], routes[0], cotangent[0]] + ([shared] if fits else [])
    qkv_weight, near, tokens_all, routes_all, grads_all, *early = gather(
        [attn_qkv.astype(BF), near], chained, 0
    )
    shared = early[0] if fits else shared
    grads_all = grads_all.reshape(keys, width)
    qkv_weight = qkv_weight.reshape(width, 3 * H * HD)
    near = near.reshape(width, near.shape[-1])
    tokens_all = tokens_all.reshape(keys, width)
    routes_all = routes_all.reshape(keys, TOP)
    cuts = [route_pad, route_pad + width]
    cuts += [cuts[-1] + hidden, cuts[-1] + 2 * hidden]
    misc, out_t = jnp.split(near, cuts[:1], axis=1)
    route_weight = misc[:, :experts]
    gain_attn = misc[:, experts].astype(F32)
    gain_moe = misc[:, experts + 1].astype(F32)
    first_all, rope_all = doc_starts_of(lengths[0], jnp.arange(keys, dtype=jnp.int32))
    first_own = lax.dynamic_slice_in_dim(first_all, own_first, rows, 0)
    cosine, sine = turn_tables(rope_all)
    cosine_own = lax.dynamic_slice_in_dim(cosine, own_first, rows, 0)
    sine_own = lax.dynamic_slice_in_dim(sine, own_first, rows, 0)
    wide = tokens_all.astype(F32)
    normed_all = (wide * inverse_rms(wide) * gain_attn).astype(BF)
    inputs = tokens[0].astype(F32)
    inverse_one = inverse_rms(inputs)
    unit_one = inputs * inverse_one
    normed = (unit_one * gain_attn).astype(BF)
    qkv = project_qkv(normed_all, qkv_weight, cosine, sine)
    attended_full, log_own = attend(me, qkv, first_own)
    attended = attended_full.astype(BF)
    middle = inputs + nt(attended, out_t)
    inverse_two = inverse_rms(middle)
    unit_two = middle * inverse_two
    normed_moe = (unit_two * gain_moe).astype(BF)
    shared, expert_weight, normed_moe = lax.optimization_barrier((shared, expert_weight, normed_moe))
    shared = lax.all_gather(shared, "dp" if fits else everyone, axis=0, tiled=True)
    shared = shared.reshape(width, 3 * hidden)
    gate_shared, up_shared, down_t = jnp.split(shared, [hidden, 2 * hidden], axis=1)

    def routing(activations, route_ids):
        logits = nn(activations, route_weight)
        probs = jax.nn.softmax(logits, axis=-1)
        named = route_ids[:, :, None] == jnp.arange(experts, dtype=jnp.int32)[None, None, :]
        named = jnp.any(named, axis=1)
        chosen = jnp.where(named, probs, 0.0)
        total = jnp.sum(chosen, axis=1, keepdims=True)
        return probs, named, chosen / total, total

    probs, named, gates, chosen_total = routing(normed_moe, routes[0])

    shared_gate_v = nn(normed_moe, gate_shared)
    shared_up_v = nn(normed_moe, up_shared)
    shared_act, shared_slope = silu_parts(shared_gate_v)
    shared_mid = (shared_act * shared_up_v).astype(BF)
    shared_out = nt(shared_mid, down_t)
    grad_out = cotangent[0].astype(F32)
    grad_bf = cotangent[0]
    grad_shared_mid = nn(grad_bf, down_t)
    grad_shared_gate_v = (grad_shared_mid * shared_up_v * shared_slope).astype(BF)
    grad_shared_up_v = (grad_shared_mid * shared_act).astype(BF)
    grad_normed_moe = nt(grad_shared_gate_v, gate_shared) + nt(grad_shared_up_v, up_shared)

    if fits:
        row_sum, gate_grads, expert_mid, expert_grads = moe_fused(
            normed_moe, routes_all, grads_all, misc, expert_weight, experts, 1
        )
        core = index % 2
        gate_grads = gate_grads[:, :EXP_DEV].reshape(chain, EXP_DEV, 2, rows)
        gate_grads = jnp.where(core == 0, gate_grads[:, :, 0], gate_grads[:, :, 1])
    else:
        moe_all = gather([], [normed_moe], 1)[0].reshape(keys, width)
        unused, unused, gates_all, unused = routing(moe_all, routes_all)
        gates_here = lax.dynamic_slice_in_dim(gates_all, index * EXP_DEV, EXP_DEV, 1)
        row_part, gate_grads, expert_mid, expert_grads = moe_plain(
            moe_all, gates_here, grads_all, expert_weight
        )
        gate_grads = jnp.transpose(gate_grads.T.reshape(EXP_DEV, chain, rows), (1, 0, 2))
        row_sum, gate_grads = to_owner(row_part.reshape(chain, rows, width), gate_grads, 2)
    gate_grads = gate_grads.reshape(experts, rows).T
    expert_sum = lax.psum_scatter(expert_grads, "dp", scatter_dimension=2, tiled=True)
    grad_chosen = (gate_grads - jnp.sum(gates * gate_grads, axis=1, keepdims=True)) / chosen_total
    grad_probs = jnp.where(named, grad_chosen, 0.0)
    grad_logits = (
        probs * (grad_probs - jnp.sum(probs * grad_probs, axis=1, keepdims=True))
    ).astype(BF)
    grad_route = tn(normed_moe, grad_logits)
    grad_normed_moe = grad_normed_moe + row_sum + nt(grad_logits, route_weight)
    grad_gain_moe = jnp.sum(grad_normed_moe * unit_two, axis=0)
    scaled_two = grad_normed_moe * gain_moe
    grad_middle = grad_out + inverse_two * (
        scaled_two - unit_two * jnp.mean(scaled_two * unit_two, axis=-1, keepdims=True)
    )
    grad_attn = grad_middle.astype(BF)
    grad_attended = nn(grad_attn, out_t).astype(BF)

    delta = jnp.sum((grad_attended.astype(F32) * attended_full).reshape(rows, H, HD), axis=-1).T
    side = jnp.concatenate([log_own[:, :, 0], delta], axis=0)
    if fits:
        grad_all, side_all, mixture, grad_gate_shared, grad_up_shared, grad_down_t, grad_out_t = spread(
            grad_attended,
            side,
            expert_mid,
            expert_weight,
            normed_moe,
            grad_shared_gate_v,
            grad_shared_up_v,
            grad_bf,
            shared_mid,
            grad_attn,
            attended,
            3,
        )
    else:
        grad_all, side_all = gather([], [grad_attended, side], 3)
    grad_all = grad_all.reshape(keys, H * HD)
    side_all = jnp.transpose(side_all, (1, 0, 2)).reshape(2, H, 1, keys)
    grads = attend_back(
        me,
        qkv,
        grad_attended,
        grad_all,
        log_own,
        jnp.broadcast_to(delta[:, :, None], (H, rows, 8)),
        side_all[0],
        side_all[1],
        (first_own, first_all),
        cosine_own,
        sine_own,
    )
    grad_misc = jnp.concatenate(
        [grad_route, jnp.zeros((width, 1), F32), grad_gain_moe[:, None]], axis=1
    )
    grad_misc = jnp.pad(grad_misc, ((0, 0), (0, 256 - experts - 2)))
    if fits:
        out_sum, gate_sum, up_sum, down_sum, qkv_sum, misc_sum, grad_inputs, output = finish(
            [grad_out_t, grad_gate_shared, grad_up_shared, grad_down_t],
            (640, hidden, hidden, hidden, 640, 256),
            experts,
            normed,
            grads,
            qkv_weight,
            grad_misc,
            unit_one,
            inverse_one,
            gain_attn[None, :],
            grad_middle,
            mixture,
            middle + shared_out,
            4,
        )
    else:
        down = expert_weight[2]
        mixture = nt(expert_mid[:, :hidden], down[0])
        for e in range(1, EXP_DEV):
            mixture = mixture + nt(expert_mid[:, e * hidden : (e + 1) * hidden], down[e])
        mixture = lax.psum_scatter(mixture.astype(BF), "expert", scatter_dimension=0, tiled=True)
        output = (middle + shared_out + mixture.astype(F32)).astype(BF)
        grad_projected = jnp.concatenate([grads[0], grads[1], grads[2]], axis=1)
        grad_normed_one = nt(grad_projected, qkv_weight)
        grad_gain_attn = jnp.sum(grad_normed_one * unit_one, axis=0)
        scaled_one = grad_normed_one * gain_attn
        grad_inputs = grad_middle + inverse_one * (
            scaled_one - unit_one * jnp.mean(scaled_one * unit_one, axis=-1, keepdims=True)
        )
        grad_inputs = grad_inputs.astype(BF)
        out_sum, gate_sum, up_sum, down_sum, qkv_sum, misc_sum = sum_dense(
            [
                tn(grad_attn, attended).astype(BF),
                tn(normed_moe, grad_shared_gate_v).astype(BF),
                tn(normed_moe, grad_shared_up_v).astype(BF),
                tn(grad_bf, shared_mid).astype(BF),
                tn(normed, grad_projected).astype(BF),
                grad_misc.at[:, experts].set(grad_gain_attn).astype(BF),
            ],
            (640, hidden, hidden, hidden, 768, 256),
            4,
        )
    return (
        output[None],
        grad_inputs[None],
        qkv_sum,
        out_sum.T,
        gate_sum,
        up_sum,
        down_sum.T,
        misc_sum[:, :experts],
        misc_sum[:, experts : experts + 2].T,
        expert_sum[0].astype(F32),
        expert_sum[1].astype(F32),
        jnp.swapaxes(expert_sum[2], 1, 2).astype(F32),
    )


def solution(mesh):
    everyone = ("dp", "expert")
    in_specs = (
        P("dp", "expert", None),
        P("dp", "expert", None),
        P("dp", None),
        P("dp", "expert", None),
        P(everyone, None),
        P(None, everyone),
        P(everyone, None),
        P(everyone, None),
        P(None, everyone),
        P(everyone, None),
        P(None, everyone),
        P("expert", "dp", None),
        P("expert", "dp", None),
        P("expert", None, "dp"),
    )
    out_specs = (
        P("dp", "expert", None),
        P("dp", "expert", None),
        P(everyone, None),
        P(None, everyone),
        P(everyone, None),
        P(everyone, None),
        P(None, everyone),
        P(everyone, None),
        P(None, everyone),
        P("expert", "dp", None),
        P("expert", "dp", None),
        P("expert", None, "dp"),
    )
    return jax.shard_map(local, mesh=mesh, in_specs=in_specs, out_specs=out_specs, check_vma=False)
```

```python
import functools

import jax
import jax.numpy as jnp
from jax import lax
from jax.experimental import pallas as pl
from jax.experimental.pallas import tpu as pltpu
from jax.sharding import PartitionSpec as P

H = 10
HD = 128
TOP = 7
EXP_DEV = 2
EPS = 1e-06
NEG = -1e30
BF = jnp.bfloat16
F32 = jnp.float32
VMEM_LIMIT = 56 * 1024 * 1024
MOE_VMEM = 62 * 1024 * 1024


def params(**kw):
    return pltpu.CompilerParams(vmem_limit_bytes=VMEM_LIMIT, **kw)


def nn(a, b):
    return jnp.dot(a, b, preferred_element_type=F32)


def nt(a, b):
    return lax.dot_general(a, b, (((1,), (1,)), ((), ())), preferred_element_type=F32)


def tn(a, b):
    return lax.dot_general(a, b, (((0,), (0,)), ((), ())), preferred_element_type=F32)


def doc_starts_of(lengths, places):
    doc_ends = jnp.cumsum(lengths)
    doc_starts = doc_ends - lengths
    total = doc_ends[-1]
    doc_index = jnp.sum((places[:, None] >= doc_ends[None, :]).astype(jnp.int32), axis=1)
    live = places < total
    matches = doc_index[:, None] == jnp.arange(lengths.shape[0], dtype=jnp.int32)[None, :]
    first = jnp.sum(jnp.where(matches, doc_starts[None, :], 0), axis=1)
    return jnp.where(live, first, places), places - jnp.where(live, first, total)


def turn_tables(rope_pos):
    half = HD // 2
    frequency = 10000.0 ** (-jnp.arange(half, dtype=F32) / half)
    angles = rope_pos.astype(F32)[:, None] * frequency[None, :]
    return jnp.cos(angles), jnp.sin(angles)


def inverse_rms(values):
    return lax.rsqrt(jnp.mean(values * values, axis=-1, keepdims=True) + EPS)


MESH = pl.DeviceIdType.MESH


def sent(src, dst, send_sem, recv_sem, device):
    return pltpu.make_async_remote_copy(
        src_ref=src,
        dst_ref=dst,
        send_sem=send_sem,
        recv_sem=recv_sem,
        device_id=device,
        device_id_type=MESH,
    )


class Place:
    def __init__(self, chips):
        self.d = lax.axis_index("dp")
        self.e = lax.axis_index("expert")
        self.z = self.e // 2
        self.c = self.e % 2
        self.y = self.d // 2
        self.x = self.d % 2
        self.chips = chips
        self.sibling = (self.d, self.e + 1 - 2 * self.c)
        self.across_x = (self.d + 1 - 2 * self.x, self.e)
        self.across_y = (self.d + 2 - 4 * self.y, self.e)
        self.up = (self.d, self.e + 2)
        self.down = (self.d, self.e - 2)


def greet(devices, conditions):
    barrier = pltpu.get_barrier_semaphore()
    count = 0
    for device, condition in zip(devices, conditions):
        if condition is None:
            pl.semaphore_signal(barrier, inc=1, device_id=device, device_id_type=MESH)
            count = count + 1
        else:

            @pl.when(condition)
            def _(device=device):
                pl.semaphore_signal(barrier, inc=1, device_id=device, device_id_type=MESH)

            count = count + condition.astype(jnp.int32)
    pl.semaphore_wait(barrier, count)


def gather_kernel(chips, n_full, n_chain, *refs):
    n = n_full + n_chain
    ins, outs, sems = refs[:n], refs[n : 2 * n], refs[2 * n :]
    at = Place(chips)
    chain = 2 * chips
    z, c = at.z, at.c
    has_up, has_down = z < chips - 1, z > 0
    devices = [at.sibling, at.up, at.down]
    conditions = [None, has_up, has_down]
    if n_full:
        devices += [at.across_x, at.across_y]
        conditions += [None, None]
    greet(devices, conditions)
    x_dp, y_dp = at.across_x[0], at.across_y[0]
    far_dp = 3 - at.d

    class Array:
        pass

    arrays = []
    position = 0
    for i in range(n):
        a = Array()
        a.full = i < n_full
        a.own, a.out = ins[i], outs[i]
        a.local, a.s_chain, a.r_chain, a.s_core, a.r_core = sems[position : position + 5]
        position += 5
        if a.full:
            a.s_side, a.r_side, a.s_half, a.r_half = sems[position : position + 4]
            position += 4
            cut = a.own.shape[-1] // 256 * 128
            a.halves = (pl.ds(0, cut), pl.ds(cut, a.own.shape[-1] - cut))
        arrays.append(a)

    def slot(a, dd, zz, cc):
        return a.out.at[dd * chain + 2 * zz + cc] if a.full else a.out.at[2 * zz + cc]

    def core_index(a, dd, zz):
        return dd * chips + zz if a.full else zz

    def to_core(a, dd, zz, src=None):
        ref = slot(a, dd, zz, c)
        k = core_index(a, dd, zz)
        return sent(ref if src is None else src, ref, a.s_core.at[k], a.r_core.at[k], at.sibling)

    def from_core(a, dd, zz):
        ref = slot(a, dd, zz, 1 - c)
        k = core_index(a, dd, zz)
        return sent(ref, ref, a.s_core.at[k], a.r_core.at[k], at.sibling)

    def along(a, zz, direction, src=None):
        ref = slot(a, at.d, zz, c)
        device = at.up if direction == 0 else at.down
        return sent(ref if src is None else src, ref, a.s_chain.at[direction, zz], a.r_chain.at[zz], device)

    def side(a, dd, zz, axis, src=None):
        ref = slot(a, dd, zz, c)
        device = at.across_x if axis == 0 else at.across_y
        return sent(
            ref if src is None else src, ref, a.s_side.at[axis, zz], a.r_side.at[axis, zz], device
        )

    def half(a, dd, zz, which):
        ref = slot(a, dd, zz, c).at[:, a.halves[which]]
        device = at.across_y if which == 0 else at.across_x
        return sent(ref, ref, a.s_half.at[which, zz], a.r_half.at[which, zz], device)

    def present(zz):
        return (zz >= 0) & (zz < chips)

    def block_here(some, zz, direction):
        for a in some:
            along(a, zz, direction).wait_recv()
            if direction == 0:

                @pl.when(has_up)
                def _(a=a):
                    along(a, zz, 0).start()
            else:

                @pl.when(has_down)
                def _(a=a):
                    along(a, zz, 1).start()

            if a.full:
                side(a, at.d, zz, 0).start()
                side(a, at.d, zz, 1).start()
            to_core(a, at.d, zz).start()

    def side_here(zz):
        for a in arrays[:n_full]:
            side(a, x_dp, zz, 0).wait_recv()
            half(a, x_dp, zz, 0).start()
            to_core(a, x_dp, zz).start()
            side(a, y_dp, zz, 1).wait_recv()
            half(a, y_dp, zz, 1).start()
            to_core(a, y_dp, zz).start()

    def far_here(zz):
        for a in arrays[:n_full]:
            half(a, far_dp, zz, 0).wait_recv()
            half(a, far_dp, zz, 1).wait_recv()
            to_core(a, far_dp, zz).start()

    def own_here(some):
        for a in some:

            @pl.when(has_up)
            def _(a=a):
                along(a, z, 0, a.own).start()

            @pl.when(has_down)
            def _(a=a):
                along(a, z, 1, a.own).start()

            if a.full:
                side(a, at.d, z, 0, a.own).start()
                side(a, at.d, z, 1, a.own).start()
            to_core(a, at.d, z, a.own).start()
            pltpu.make_async_copy(a.own, slot(a, at.d, z, c), a.local).start()

    def at_distance(k, fn):
        @pl.when((k >= 0) & present(z - k))
        def _():
            fn(z - k)

        @pl.when((k >= 1) & present(z + k))
        def _():
            fn(z + k)

    def chain_step(some, k):
        @pl.when(present(z - k))
        def _():
            block_here(some, z - k, 0)

        @pl.when(present(z + k))
        def _():
            block_here(some, z + k, 1)

    full, chained = arrays[:n_full], arrays[n_full:]
    if n_full:
        own_here(full)

        def first_step(k, carry):
            chain_step(full, k)
            return carry

        lax.fori_loop(1, chips, first_step, 0)
    own_here(chained)

    def step(k, carry):
        if n_full:
            at_distance(k - 1, side_here)
        chain_step(chained, k)
        if n_full:
            at_distance(k - 2, far_here)
        return carry

    lax.fori_loop(1, chips + (2 if n_full else 0), step, 0)

    def finish(zz, carry):
        for a in arrays:
            for dd in range(4) if a.full else (0,):
                from_core(a, dd, zz).wait_recv()
                to_core(a, dd, zz).wait_send()

            @pl.when((zz <= z) & has_up)
            def _(a=a):
                along(a, zz, 0).wait_send()

            @pl.when((zz >= z) & has_down)
            def _(a=a):
                along(a, zz, 1).wait_send()

            if a.full:
                for axis in (0, 1):
                    side(a, at.d, zz, axis).wait_send()
                half(a, x_dp, zz, 0).wait_send()
                half(a, y_dp, zz, 1).wait_send()
        return carry

    lax.fori_loop(0, chips, finish, 0)
    for a in arrays:
        pltpu.make_async_copy(a.own, slot(a, at.d, z, c), a.local).wait()


def gather(full, chained, collective_id):
    chain = lax.axis_size("expert")
    chips = chain // 2
    spread = lax.axis_size("dp")
    assert spread == 4 and chain % 2 == 0
    dma = pltpu.SemaphoreType.DMA
    scratch = []
    for array in full:
        scratch += [dma, dma((2, chips)), dma((chips,)), dma((4 * chips,)), dma((4 * chips,))]
        scratch += [dma((2, chips))] * 4
    for array in chained:
        scratch += [dma, dma((2, chips)), dma((chips,)), dma((chips,)), dma((chips,))]
    shapes = [jax.ShapeDtypeStruct((spread * chain,) + a.shape, a.dtype) for a in full]
    shapes += [jax.ShapeDtypeStruct((chain,) + a.shape, a.dtype) for a in chained]
    n = len(full) + len(chained)
    moved = sum(s.size * s.dtype.itemsize for s in shapes)
    return pl.pallas_call(
        functools.partial(gather_kernel, chips, len(full), len(chained)),
        out_shape=shapes,
        in_specs=[pl.BlockSpec(memory_space=pl.ANY)] * n,
        out_specs=[pl.BlockSpec(memory_space=pl.ANY)] * n,
        scratch_shapes=scratch,
        compiler_params=params(collective_id=collective_id, has_side_effects=True),
        cost_estimate=pl.CostEstimate(flops=0, bytes_accessed=16 * moved, transcendentals=0),
    )(*full, *chained)


def to_owner_kernel(chips, wide_ref, thin_ref, out_ref, thin_out, mine, other, came, sems_in, s_core, r_core, s_chain, r_chain, s_thin, r_thin):
    at = Place(chips)
    chain = 2 * chips
    z, c = at.z, at.c
    devices = [(at.d, lax.rem(at.e + k, chain)) for k in range(1, chain)]
    greet(devices, [None] * (chain - 1))

    def load(zz):
        return pltpu.make_async_copy(wide_ref.at[2 * zz + c], mine.at[zz], sems_in.at[zz])

    def to_core(zz):
        return sent(
            wide_ref.at[2 * zz + 1 - c], other.at[zz], s_core.at[zz], r_core.at[zz], at.sibling
        )

    def thin(k):
        target = lax.rem(at.e + k, chain)
        return sent(
            thin_ref.at[target], thin_out.at[at.e], s_thin.at[k], r_thin.at[k], (at.d, target)
        )

    def over(k):
        zz = lax.rem(z + k, chips)
        return sent(
            mine.at[zz], came.at[k], s_chain.at[k], r_chain.at[k], (at.d, 2 * zz + c)
        )

    order = [lax.rem(z + k, chips) for k in range(1, chips)] + [z]
    for zz in order:
        to_core(zz).start()
        load(zz).start()
    for k in range(1, chain):
        thin(k).start()
    own_thin = pltpu.make_async_copy(thin_ref.at[at.e], thin_out.at[at.e], s_thin.at[0])
    own_thin.start()
    for k, zz in enumerate(order):
        to_core(zz).wait_recv()
        load(zz).wait()
        total = mine[zz].astype(F32) + other[zz].astype(F32)
        if k < chips - 1:
            mine[zz] = total.astype(BF)
            over(k + 1).start()
        else:
            out_ref[...] = total
    for k in range(1, chips):
        over(k).wait_recv()
        out_ref[...] += came[k].astype(F32)
    for k in range(1, chips):
        over(k).wait_send()
    for zz in order:
        to_core(zz).wait_send()
    own_thin.wait()
    for k in range(1, chain):
        thin(k).wait()


def to_owner(wide, thin, collective_id):
    chain, rows, width = wide.shape
    chips = chain // 2
    dma = pltpu.SemaphoreType.DMA
    return pl.pallas_call(
        functools.partial(to_owner_kernel, chips),
        out_shape=[
            jax.ShapeDtypeStruct((rows, width), F32),
            jax.ShapeDtypeStruct(thin.shape, thin.dtype),
        ],
        in_specs=[pl.BlockSpec(memory_space=pl.ANY), pl.BlockSpec(memory_space=pltpu.VMEM)],
        out_specs=[pl.BlockSpec(memory_space=pltpu.VMEM), pl.BlockSpec(memory_space=pltpu.VMEM)],
        scratch_shapes=[
            pltpu.VMEM((chips, rows, width), BF),
            pltpu.VMEM((chips, rows, width), BF),
            pltpu.VMEM((chips, rows, width), BF),
            dma((chips,)),
            dma((chips,)),
            dma((chips,)),
            dma((chips,)),
            dma((chips,)),
            dma((chain,)),
            dma((chain,)),
        ],
        compiler_params=params(collective_id=collective_id, has_side_effects=True),
        cost_estimate=pl.CostEstimate(
            flops=0, bytes_accessed=16 * wide.size * 2, transcendentals=0
        ),
    )(wide, thin)


def sum_dense_kernel(chips, chunks, n_in, *refs):
    ins, outs = refs[:n_in], refs[n_in : 2 * n_in]
    n_chunks = len(chunks)
    rest = refs[2 * n_in :]
    sems = rest[:10]
    s_in, s_core, r_core, s_one, r_one, s_two, r_two, s_end, r_end = sems[:9]
    buffers = rest[9:]
    at = Place(chips)
    z, c, x, y = at.z, at.c, at.x, at.y
    others = [(at.d, 2 * lax.rem(z + k, chips) + c) for k in range(1, chips)]
    devices = [at.sibling, at.across_x, at.across_y] + others
    greet(devices, [None] * len(devices))

    class Chunk:
        def __init__(self, q):
            i, first, wide = chunks[q]
            self.i, self.first, self.wide = i, first, wide
            self.q = q
            self.mine, self.other, one_x, one_y, two_x, two_y, self.end = buffers[7 * q : 7 * q + 7]
            self.one, self.two = (one_x, one_y), (two_x, two_y)
            self.cols = pl.ds(first, wide)
            cut = wide // 256 * 128
            self.half = (pl.ds(0, cut), pl.ds(cut, wide - cut))

        def load(self):
            return pltpu.make_async_copy(
                ins[self.i].at[:, :, :, c, :, self.cols], self.mine, s_in.at[self.q]
            )

        def core(self):
            return sent(
                ins[self.i].at[:, :, :, 1 - c, :, self.cols],
                self.other,
                s_core.at[self.q],
                r_core.at[self.q],
                at.sibling,
            )

        def first_x(self):
            return sent(
                self.mine.at[:, 1 - x, :, :, self.half[0]],
                self.one[0],
                s_one.at[self.q, 0],
                r_one.at[self.q, 0],
                at.across_x,
            )

        def first_y(self):
            return sent(
                self.mine.at[1 - y, :, :, :, self.half[1]],
                self.one[1],
                s_one.at[self.q, 1],
                r_one.at[self.q, 1],
                at.across_y,
            )

        def second_y(self):
            return sent(
                self.mine.at[1 - y, x, :, :, self.half[0]],
                self.two[0],
                s_two.at[self.q, 0],
                r_two.at[self.q, 0],
                at.across_y,
            )

        def second_x(self):
            return sent(
                self.mine.at[y, 1 - x, :, :, self.half[1]],
                self.two[1],
                s_two.at[self.q, 1],
                r_two.at[self.q, 1],
                at.across_x,
            )

        def last(self, k):
            zz = lax.rem(z + k, chips)
            return sent(
                self.mine.at[y, x, zz],
                self.end.at[k - 1],
                s_end.at[self.q, k - 1],
                r_end.at[self.q, k - 1],
                (at.d, 2 * zz + c),
            )

    parts = [Chunk(q) for q in range(n_chunks)]

    def add(ref, place, more):
        ref[place] = (ref[place].astype(F32) + more.astype(F32)).astype(BF)

    def stage_one(p):
        p.core().wait_recv()
        p.load().wait()

        def body(k, carry):
            yy, xx, zz = k // (2 * chips), (k // chips) % 2, k % chips
            p.mine[yy, xx, zz] = (
                p.mine[yy, xx, zz].astype(F32) + p.other[yy, xx, zz].astype(F32)
            ).astype(BF)
            return carry

        lax.fori_loop(0, 4 * chips, body, 0)
        p.first_x().start()
        p.first_y().start()

    def stage_two(p):
        p.first_x().wait_recv()
        p.first_y().wait_recv()

        def body(k, carry):
            v, zz = k // chips, k % chips
            a, b = p.half
            p.mine[v, x, zz, :, a] = (
                p.mine[v, x, zz, :, a].astype(F32) + p.one[0][v, zz].astype(F32)
            ).astype(BF)
            p.mine[y, v, zz, :, b] = (
                p.mine[y, v, zz, :, b].astype(F32) + p.one[1][v, zz].astype(F32)
            ).astype(BF)
            return carry

        lax.fori_loop(0, 2 * chips, body, 0)
        p.second_y().start()
        p.second_x().start()

    def stage_three(p):
        p.second_y().wait_recv()
        p.second_x().wait_recv()

        def body(zz, carry):
            for w in (0, 1):
                s = p.half[w]
                p.mine[y, x, zz, :, s] = (
                    p.mine[y, x, zz, :, s].astype(F32) + p.two[w][zz].astype(F32)
                ).astype(BF)
            return carry

        lax.fori_loop(0, chips, body, 0)
        for k in range(1, chips):
            p.last(k).start()

    def stage_four(p):
        total = p.mine[y, x, z].astype(F32)
        for k in range(1, chips):
            p.last(k).wait_recv()
            total = total + p.end[k - 1].astype(F32)
        outs[p.i][:, p.first : p.first + p.wide] = total

    for p in parts:
        p.core().start()
        p.load().start()
    stages = (stage_one, stage_two, stage_three, stage_four)
    for t in range(n_chunks + len(stages) - 1):
        for s, stage in enumerate(stages):
            if 0 <= t - s < n_chunks:
                stage(parts[t - s])
    for p in parts:
        p.core().wait_send()
        p.first_x().wait_send()
        p.first_y().wait_send()
        p.second_x().wait_send()
        p.second_y().wait_send()
        for k in range(1, chips):
            p.last(k).wait_send()


def sum_dense(arrays, chunk_widths, collective_id):
    chain = lax.axis_size("expert")
    chips = chain // 2
    assert lax.axis_size("dp") == 4
    block = arrays[0].shape[0] // (4 * chain)
    dma = pltpu.SemaphoreType.DMA
    chunks = []
    for i, (array, wide) in enumerate(zip(arrays, chunk_widths)):
        assert array.shape[1] % wide == 0 and wide % 128 == 0 and wide >= 256
        chunks += [(i, first, wide) for first in range(0, array.shape[1], wide)]
    q = len(chunks)
    scratch = [dma((q,)), dma((q,)), dma((q,))] + [dma((q, 2))] * 4 + [dma((q, max(1, chips - 1)))] * 2
    for i, first, wide in chunks:
        cut = wide // 256 * 128
        scratch += [
            pltpu.VMEM((2, 2, chips, block, wide), BF),
            pltpu.VMEM((2, 2, chips, block, wide), BF),
            pltpu.VMEM((2, chips, block, cut), BF),
            pltpu.VMEM((2, chips, block, wide - cut), BF),
            pltpu.VMEM((chips, block, cut), BF),
            pltpu.VMEM((chips, block, wide - cut), BF),
            pltpu.VMEM((max(1, chips - 1), block, wide), BF),
        ]
    n = len(arrays)
    return pl.pallas_call(
        functools.partial(sum_dense_kernel, chips, tuple(chunks), n),
        out_shape=[jax.ShapeDtypeStruct((block, a.shape[1]), F32) for a in arrays],
        in_specs=[pl.BlockSpec(memory_space=pl.ANY)] * n,
        out_specs=[pl.BlockSpec(memory_space=pltpu.VMEM)] * n,
        scratch_shapes=scratch,
        compiler_params=params(collective_id=collective_id, has_side_effects=True),
        cost_estimate=pl.CostEstimate(
            flops=0, bytes_accessed=16 * sum(a.size for a in arrays), transcendentals=0
        ),
    )(*[a.reshape(2, 2, chips, 2, block, a.shape[1]) for a in arrays])


def qkv_kernel(per_block, x_ref, w_ref, gain_ref, cos_ref, sin_ref, o_ref, normed, cosine, sine):
    column = pl.program_id(1)
    rows = x_ref.shape[0]
    step = 384 if rows % 384 == 0 else rows

    @pl.when(column == 0)
    def _():
        for r in range(0, rows, step):
            wide = x_ref[r : r + step, :].astype(F32)
            normed[r : r + step, :] = (wide * inverse_rms(wide) * gain_ref[...]).astype(BF)
        cosine[:, : HD // 2] = cos_ref[...]
        cosine[:, HD // 2 :] = cos_ref[...]
        sine[:, : HD // 2] = -sin_ref[...]
        sine[:, HD // 2 :] = sin_ref[...]

    for first in range(0, per_block, 2):
        for r in range(0, rows, step):
            product = nn(normed[r : r + step, :], w_ref[:, first * HD : (first + 2) * HD])
            for k in (0, 1):
                part = product[:, k * HD : (k + 1) * HD]
                head = column * per_block + first + k
                turned = (
                    part * cosine[r : r + step, :]
                    + pltpu.roll(part, HD // 2, 1) * sine[r : r + step, :]
                )
                o_ref[r : r + step, (first + k) * HD : (first + k + 1) * HD] = jnp.where(
                    head < 2 * H, turned, part
                ).astype(BF)


def project_qkv(tokens, weight, gain, cosine, sine):
    rows, width = tokens.shape
    columns = weight.shape[1]
    per_block = 6
    tile_m = min(rows, 1536)
    return pl.pallas_call(
        functools.partial(qkv_kernel, per_block),
        out_shape=jax.ShapeDtypeStruct((rows, columns), BF),
        grid=(rows // tile_m, columns // (per_block * HD)),
        in_specs=[
            pl.BlockSpec((tile_m, width), lambda m, n: (m, 0)),
            pl.BlockSpec((width, per_block * HD), lambda m, n: (0, n)),
            pl.BlockSpec((1, width), lambda m, n: (0, 0)),
            pl.BlockSpec((tile_m, HD // 2), lambda m, n: (m, 0)),
            pl.BlockSpec((tile_m, HD // 2), lambda m, n: (m, 0)),
        ],
        out_specs=pl.BlockSpec((tile_m, per_block * HD), lambda m, n: (m, n)),
        scratch_shapes=[
            pltpu.VMEM((tile_m, width), BF),
            pltpu.VMEM((tile_m, HD), F32),
            pltpu.VMEM((tile_m, HD), F32),
        ],
        compiler_params=params(),
        cost_estimate=pl.CostEstimate(
            flops=2 * rows * width * columns,
            bytes_accessed=2 * (rows * width + width * columns + rows * columns),
            transcendentals=0,
        ),
    )(tokens, weight, gain[None, :], cosine, sine)


def attend_kernel(scale, me_ref, q_ref, k_ref, v_ref, first_ref, o_ref, log_ref, bias):
    rows, keys = bias.shape

    @pl.when(pl.program_id(0) == 0)
    def _():
        key_place = lax.broadcasted_iota(jnp.int32, (rows, keys), 1)
        query_place = me_ref[0] * rows + lax.broadcasted_iota(jnp.int32, (rows, keys), 0)
        allowed = (key_place <= query_place) & (key_place >= first_ref[...])
        bias[...] = jnp.where(allowed, 0.0, NEG)

    scores = nt(q_ref[...], k_ref[...]) * scale + bias[...]
    top = jnp.max(scores, axis=-1, keepdims=True)
    weights = jnp.exp(scores - top)
    total = jnp.sum(weights, axis=-1, keepdims=True)
    o_ref[...] = nn(weights.astype(BF), v_ref[...]) / total
    log_ref[...] = jnp.broadcast_to(top + jnp.log(total), (rows, 8))[None]


def attend(me, qkv, first_own):
    keys = qkv.shape[0]
    rows = first_own.shape[0]
    return pl.pallas_call(
        functools.partial(attend_kernel, HD**-0.5),
        out_shape=[
            jax.ShapeDtypeStruct((rows, H * HD), F32),
            jax.ShapeDtypeStruct((H, rows, 8), F32),
        ],
        grid_spec=pltpu.PrefetchScalarGridSpec(
            num_scalar_prefetch=1,
            grid=(H,),
            in_specs=[
                pl.BlockSpec((rows, HD), lambda h, me: (me[0], h)),
                pl.BlockSpec((keys, HD), lambda h, me: (0, H + h)),
                pl.BlockSpec((keys, HD), lambda h, me: (0, 2 * H + h)),
                pl.BlockSpec((rows, 1), lambda h, me: (0, 0)),
            ],
            out_specs=[
                pl.BlockSpec((rows, HD), lambda h, me: (0, h)),
                pl.BlockSpec((1, rows, 8), lambda h, me: (h, 0, 0)),
            ],
            scratch_shapes=[pltpu.VMEM((rows, keys), F32)],
        ),
        compiler_params=params(),
        cost_estimate=pl.CostEstimate(
            flops=4 * rows * keys * H * HD,
            bytes_accessed=4 * keys * H * HD,
            transcendentals=H * rows * keys,
        ),
    )(me, qkv, qkv, qkv, first_own[:, None])


def attend_back_kernel(
    scale,
    me_ref,
    q_ref,
    k_ref,
    v_ref,
    qa_ref,
    ko_ref,
    vo_ref,
    do_ref,
    da_ref,
    log_ref,
    delta_ref,
    loga_ref,
    deltaa_ref,
    first_ref,
    firsta_ref,
    cos_ref,
    sin_ref,
    o_ref,
    bias,
    biast,
):
    rows, keys = bias.shape

    @pl.when(pl.program_id(0) == 0)
    def _():
        place = lax.broadcasted_iota(jnp.int32, (rows, keys), 1)
        own = me_ref[0] * rows + lax.broadcasted_iota(jnp.int32, (rows, keys), 0)
        bias[...] = jnp.where((place <= own) & (place >= first_ref[...]), 0.0, NEG)
        biast[...] = jnp.where((own <= place) & (own >= firsta_ref[...]), 0.0, NEG)

    def unturn(value):
        return value * cos_ref[...] - pltpu.roll(value, HD // 2, 1) * sin_ref[...]

    log_own = log_ref[0][:, :1]
    delta_own = delta_ref[0][:, :1]
    weights = jnp.exp(nt(q_ref[...], k_ref[...]) * scale + bias[...] - log_own)
    back = nt(do_ref[...], v_ref[...])
    grad = (weights * (back - delta_own) * scale).astype(BF)
    o_ref[0] = unturn(nn(grad, k_ref[...])).astype(BF)

    weights = jnp.exp(nt(ko_ref[...], qa_ref[...]) * scale + biast[...] - loga_ref[0])
    o_ref[2] = nn(weights.astype(BF), da_ref[...]).astype(BF)
    back = nt(vo_ref[...], da_ref[...])
    grad = (weights * (back - deltaa_ref[0]) * scale).astype(BF)
    o_ref[1] = unturn(nn(grad, qa_ref[...])).astype(BF)


def attend_back(me, qkv, grad_all, log_own, delta_own, log_all, delta_all, first, cosine, sine):
    keys = qkv.shape[0]
    first_own, first_all = first
    rows = first_own.shape[0]
    return pl.pallas_call(
        functools.partial(attend_back_kernel, HD**-0.5),
        out_shape=jax.ShapeDtypeStruct((3, rows, H * HD), BF),
        grid_spec=pltpu.PrefetchScalarGridSpec(
            num_scalar_prefetch=1,
            grid=(H,),
            in_specs=[
                pl.BlockSpec((rows, HD), lambda h, me: (me[0], h)),
                pl.BlockSpec((keys, HD), lambda h, me: (0, H + h)),
                pl.BlockSpec((keys, HD), lambda h, me: (0, 2 * H + h)),
                pl.BlockSpec((keys, HD), lambda h, me: (0, h)),
                pl.BlockSpec((rows, HD), lambda h, me: (me[0], H + h)),
                pl.BlockSpec((rows, HD), lambda h, me: (me[0], 2 * H + h)),
                pl.BlockSpec((rows, HD), lambda h, me: (me[0], h)),
                pl.BlockSpec((keys, HD), lambda h, me: (0, h)),
                pl.BlockSpec((1, rows, 8), lambda h, me: (h, 0, 0)),
                pl.BlockSpec((1, rows, 8), lambda h, me: (h, 0, 0)),
                pl.BlockSpec((1, 1, keys), lambda h, me: (h, 0, 0)),
                pl.BlockSpec((1, 1, keys), lambda h, me: (h, 0, 0)),
                pl.BlockSpec((rows, 1), lambda h, me: (0, 0)),
                pl.BlockSpec((1, keys), lambda h, me: (0, 0)),
                pl.BlockSpec((rows, HD), lambda h, me: (0, 0)),
                pl.BlockSpec((rows, HD), lambda h, me: (0, 0)),
            ],
            out_specs=pl.BlockSpec((3, rows, HD), lambda h, me: (0, 0, h)),
            scratch_shapes=[pltpu.VMEM((rows, keys), F32)] * 2,
        ),
        compiler_params=params(),
        cost_estimate=pl.CostEstimate(
            flops=14 * rows * keys * H * HD,
            bytes_accessed=8 * keys * H * HD,
            transcendentals=2 * H * rows * keys,
        ),
    )(
        me,
        qkv,
        qkv,
        qkv,
        qkv,
        qkv,
        qkv,
        grad_all,
        grad_all,
        log_own,
        delta_own,
        log_all,
        delta_all,
        first_own[:, None],
        first_all[None, :],
        cosine,
        sine,
    )


def moe_kernel(
    chips,
    experts,
    x_own,
    routes,
    grads,
    near_in,
    weights,
    row_out,
    thin_out,
    mid_out,
    grad_out,
    x_all,
    g_all,
    w,
    hid,
    part,
    other,
    came,
    thin,
    dots,
    misc,
    s_load,
    s_x,
    r_x,
    s_fwd,
    r_fwd,
    s_part,
    r_part,
    s_came,
    r_came,
    s_thin,
    r_thin,
):
    at = Place(chips)
    z, c = at.z, at.c
    chain = 2 * chips
    rows, width = x_own.shape
    both = w.shape[2]
    tiles = both // 256
    per_expert = both // 256
    greet([(at.d, lax.rem(at.e + k, chain)) for k in range(1, chain)], [None] * (chain - 1))

    near = jnp.minimum(z, chips - 1 - z)

    def order(j):
        step = (j + 1) // 2
        around = jnp.where(j % 2 == 1, z - step, z + step)
        return jnp.where(j <= 2 * near, around, jnp.where(2 * z < chips, j, chips - 1 - j))

    def own_load():
        return pltpu.make_async_copy(x_own, x_all.at[z, c], s_load.at[0])

    hidden = both // EXP_DEV

    def weight_load(k, e):
        return pltpu.make_async_copy(
            weights.at[k, e], w.at[k, :, pl.ds(e * hidden, hidden)], s_load.at[2 + 2 * k + e]
        )

    def grad_store(k, e):
        return pltpu.make_async_copy(
            w.at[k, :, pl.ds(e * hidden, hidden)], grad_out.at[k, e], s_load.at[2 + 2 * k + e]
        )

    def grads_load():
        return pltpu.make_async_copy(grads, g_all, s_load.at[1])

    def x_send(zz):
        return sent(x_own, x_all.at[z, c], s_x.at[zz], r_x.at[z], (at.d, 2 * zz + c))

    def x_came(zz):
        ref = x_all.at[zz, c]
        return sent(ref, ref, s_x.at[zz], r_x.at[zz], (at.d, 2 * zz + c))

    def forward(zz):
        ref = x_all.at[zz, c]
        return sent(ref, ref, s_fwd.at[zz], r_fwd.at[zz], at.sibling)

    def forwarded(zz):
        ref = x_all.at[zz, 1 - c]
        return sent(ref, ref, s_fwd.at[zz], r_fwd.at[zz], at.sibling)

    def part_send(zz):
        return sent(part.at[zz, 1 - c], other.at[zz], s_part.at[zz], r_part.at[zz], at.sibling)

    def came_send(zz):
        return sent(part.at[zz, c], came.at[z], s_came.at[zz], r_came.at[z], (at.d, 2 * zz + c))

    def came_here(zz):
        return sent(part.at[zz, c], came.at[zz], s_came.at[zz], r_came.at[zz], (at.d, 2 * zz + c))

    def thin_send(zz, cc):
        return sent(
            thin.at[zz], thin_out.at[at.e], s_thin.at[2 * zz + cc], r_thin.at[at.e], (at.d, 2 * zz + cc)
        )

    def thin_here(e):
        return sent(thin.at[0], thin_out.at[e], s_thin.at[e], r_thin.at[e], (at.d, e))

    misc_load = pltpu.make_async_copy(near_in.at[:, pl.ds(0, 128)], misc, s_load.at[8])
    misc_load.start()
    own_load().start()
    sent(x_own, x_all.at[z, c], s_fwd.at[z], r_fwd.at[z], at.sibling).start()
    for j in range(1, chips):
        x_send(order(j)).start()
    for k in range(3):
        for e in range(EXP_DEV):
            weight_load(k, e).start()
    grads_load().start()
    own_load().wait()
    misc_load.wait()

    lanes = lax.broadcasted_iota(jnp.int32, (2 * rows, 128), 1)

    def gates_of(zz, x):
        logits = jnp.where(lanes < experts, nn(x, misc[...]), NEG)
        powers = jnp.exp(logits - jnp.max(logits, axis=1, keepdims=True))
        probs = powers / jnp.sum(powers, axis=1, keepdims=True)
        named = routes[zz][:, 0:1] == lanes
        for j in range(1, TOP):
            named = named | (routes[zz][:, j : j + 1] == lanes)
        chosen = jnp.where(named, probs, 0.0)
        gates = chosen / jnp.sum(chosen, axis=1, keepdims=True)
        return [
            jnp.sum(jnp.where(lanes == EXP_DEV * at.e + k, gates, 0.0), axis=1, keepdims=True)
            for k in range(EXP_DEV)
        ]

    def settle(zz):
        part_send(zz).wait_recv()
        total = part[zz, c].astype(F32) + other[zz].astype(F32)

        @pl.when(zz == z)
        def _():
            row_out[...] = total

        @pl.when(zz != z)
        def _():
            part[zz, c] = total.astype(BF)
            came_send(zz).start()

    def block(j, carry):
        zz = order(j)
        forwarded(zz).wait_recv()
        here = pl.ds(pl.multiple_of(zz * 2 * rows, 2 * rows), 2 * rows)
        x = x_all[zz].reshape(2 * rows, width)
        first, second = gates_of(zz, x)
        dots[...] = jnp.zeros_like(dots)

        @pl.when(j == 0)
        def _():
            for k in range(3):
                for e in range(EXP_DEV):
                    weight_load(k, e).wait()
            grads_load().wait()

        def tile(n, carry):
            cols = pl.ds(pl.multiple_of(n * 256, 256), 256)
            x = x_all[zz].reshape(2 * rows, width)
            g = g_all[zz].reshape(2 * rows, width)
            gate_v = nn(x, w[0, :, cols])
            up_v = nn(x, w[1, :, cols])
            back = nn(g, w[2, :, cols])
            for half in (0, 1):
                s = slice(half * 128, half * 128 + 128)
                is_first = 2 * n + half < per_expert
                gate = jnp.where(is_first, first, second)
                v, u, b = gate_v[:, s], up_v[:, s], back[:, s]
                sig = jax.nn.sigmoid(v)
                act = v * sig
                mid = act * u
                dots[0] += mid * b * is_first.astype(F32)
                dots[1] += mid * b * (1.0 - is_first.astype(F32))
                b = gate * b
                to = pl.ds(pl.multiple_of(n * 256 + half * 128, 128), 128)
                hid[2, here, to] = (gate * mid).astype(BF)
                hid[0, here, to] = (b * u * (sig * (1.0 + v * (1.0 - sig)))).astype(BF)
                hid[1, here, to] = (b * act).astype(BF)
            return carry

        early = (tiles + 1) // 2
        lax.fori_loop(0, early, tile, 0, unroll=True)

        @pl.when(j + 1 < chips)
        def _():
            x_came(order(j + 1)).wait_recv()
            forward(order(j + 1)).start()

        @pl.when(j > 0)
        def _():
            settle(order(j - 1))

        lax.fori_loop(early, tiles, tile, 0, unroll=True)

        def row_tile(n, carry):
            cols = pl.ds(pl.multiple_of(n * 256, 256), 256)
            row = nt(hid[0, here, :], w[0, cols, :]) + nt(hid[1, here, :], w[1, cols, :])
            part[zz, 0, :, cols] = row[:rows].astype(BF)
            part[zz, 1, :, cols] = row[rows:].astype(BF)
            return carry

        lax.fori_loop(0, width // 256, row_tile, 0, unroll=True)
        part_send(zz).start()
        column = jnp.where(
            lanes == 0,
            jnp.sum(dots[0], axis=1, keepdims=True),
            jnp.sum(dots[1], axis=1, keepdims=True),
        )
        thin[zz] = column.T[:8]

        @pl.when(zz == z)
        def _():
            thin_out[at.e] = thin[zz]

        for cc in (0, 1):

            @pl.when(2 * zz + cc != at.e)
            def _(cc=cc):
                thin_send(zz, cc).start()

        return carry

    lax.fori_loop(0, chips, block, 0)
    settle(order(chips - 1))
    mid_store = pltpu.make_async_copy(hid.at[2], mid_out, s_load.at[0])
    mid_store.start()
    for k in (2, 0, 1):

        def grad_tile(n, carry, k=k):
            cols = pl.ds(pl.multiple_of(n * 256, 256), 256)
            left = g_all if k == 2 else x_all
            left = left[...].reshape(chain * rows, width)
            w[k, :, cols] = tn(left, hid[k, :, cols]).astype(BF)
            return carry

        lax.fori_loop(0, tiles, grad_tile, 0, unroll=True)
        for e in range(EXP_DEV):
            grad_store(k, e).start()

    for zz in range(chips):

        @pl.when(zz != z)
        def _(zz=zz):
            came_here(zz).wait_recv()
            row_out[...] += came[zz].astype(F32)
            came_send(zz).wait_send()
            x_send(zz).wait_send()

        part_send(zz).wait_send()
        forward(zz).wait_send()
        for cc in (0, 1):

            @pl.when(2 * zz + cc != at.e)
            def _(zz=zz, cc=cc):
                thin_here(2 * zz + cc).wait_recv()
                thin_send(zz, cc).wait_send()

    mid_store.wait()
    for k in range(3):
        for e in range(EXP_DEV):
            grad_store(k, e).wait()


def moe_fused(normed, routes_all, grads_all, near, weights, experts, collective_id):
    rows, width = normed.shape
    chain = routes_all.shape[0] // rows
    chips = chain // 2
    both = EXP_DEV * weights.shape[3]
    dma = pltpu.SemaphoreType.DMA
    blocks = (chips, 2, rows, width)
    anywhere = pl.BlockSpec(memory_space=pl.ANY)
    vmem = pl.BlockSpec(memory_space=pltpu.VMEM)
    return pl.pallas_call(
        functools.partial(moe_kernel, chips, experts),
        out_shape=[
            jax.ShapeDtypeStruct((rows, width), F32),
            jax.ShapeDtypeStruct((chain, 8, 2 * rows), F32),
            jax.ShapeDtypeStruct((chain * rows, both), BF),
            jax.ShapeDtypeStruct(weights.shape, BF),
        ],
        in_specs=[anywhere, vmem, anywhere, anywhere, anywhere],
        out_specs=[vmem, vmem, anywhere, anywhere],
        scratch_shapes=[
            pltpu.VMEM(blocks, BF),
            pltpu.VMEM(blocks, BF),
            pltpu.VMEM((3, width, both), BF),
            pltpu.VMEM((3, chain * rows, both), BF),
            pltpu.VMEM(blocks, BF),
            pltpu.VMEM((chips, rows, width), BF),
            pltpu.VMEM((chips, rows, width), BF),
            pltpu.VMEM((chips, 8, 2 * rows), F32),
            pltpu.VMEM((2, 2 * rows, 128), F32),
            pltpu.VMEM((width, 128), BF),
            dma((9,)),
        ]
        + [dma((chips,))] * 8
        + [dma((chain,))] * 2,
        compiler_params=pltpu.CompilerParams(
            vmem_limit_bytes=MOE_VMEM, collective_id=collective_id, has_side_effects=True
        ),
        cost_estimate=pl.CostEstimate(
            flops=16 * chain * rows * width * both,
            bytes_accessed=4 * weights.size + 4 * chain * rows * both,
            transcendentals=chain * rows * both,
        ),
    )(
        normed,
        routes_all.reshape(chips, 2 * rows, TOP),
        grads_all.reshape(blocks),
        near,
        weights,
    )


def moe_plain(moe_all, gates_here, grads_all, weights):
    keys, width = moe_all.shape
    hidden = weights.shape[3]
    at_once = 768 if keys % 768 == 0 else keys

    def some(rows):
        x, gates, g = rows
        row = jnp.zeros(x.shape, F32)
        dots, mids, gate_vs, up_vs = [], [], [], []
        for e in range(EXP_DEV):
            scale = gates[:, e : e + 1]
            gate_v = nn(x, weights[0, e])
            up_v = nn(x, weights[1, e])
            back = nn(g, weights[2, e])
            act, slope = silu_parts(gate_v)
            mid = act * up_v
            dots.append(jnp.sum(mid * back, axis=1))
            back = back * scale
            gate_vs.append((back * up_v * slope).astype(BF))
            up_vs.append((back * act).astype(BF))
            mids.append((mid * scale).astype(BF))
            row = row + nt(gate_vs[e], weights[0, e]) + nt(up_vs[e], weights[1, e])
        return (
            row.astype(BF),
            jnp.stack(dots, axis=1),
            jnp.concatenate(mids, axis=1),
            jnp.concatenate(gate_vs, axis=1),
            jnp.concatenate(up_vs, axis=1),
        )

    cut = jax.tree.map(
        lambda a: a.reshape((keys // at_once, at_once) + a.shape[1:]), (moe_all, gates_here, grads_all)
    )
    row, dots, mid, gate_v, up_v = jax.tree.map(
        lambda a: a.reshape((keys,) + a.shape[2:]), lax.map(some, cut)
    )

    def grad_of(x, h):
        grad = tn(x, h).astype(BF).reshape(width, EXP_DEV, hidden)
        return jnp.swapaxes(grad, 0, 1)

    weight_grads = jnp.stack(
        [grad_of(moe_all, gate_v), grad_of(moe_all, up_v), grad_of(grads_all, mid)]
    )
    return row, dots, mid, weight_grads


def spread_kernel(
    chips,
    experts,
    mid,
    weights,
    shared_in,
    near_in,
    normed,
    cot,
    row_sum,
    thin,
    routes,
    middle,
    gain,
    attended_full,
    log_own,
    all_out,
    side_out,
    mix_out,
    gate_out,
    up_out,
    down_out,
    out_out,
    base_out,
    middle_out,
    misc_out,
    delta_out,
    mids,
    w,
    mix,
    dense,
    wide,
    shared,
    near,
    own,
    side,
    turned,
    s_load,
    s_dense,
    s_chain,
    r_chain,
    s_core,
    r_core,
    s_side,
    r_side,
    s_score,
    r_score,
):
    at = Place(chips)
    z, c = at.z, at.c
    rows, width = normed.shape
    hidden = shared_in.shape[1] // 3
    has_up, has_down = z < chips - 1, z > 0
    loads = [
        pltpu.make_async_copy(
            shared_in.at[:, pl.ds(k * hidden, hidden)], shared.at[k], s_load.at[k]
        )
        for k in range(3)
    ]
    loads.append(pltpu.make_async_copy(near_in, near, s_load.at[3]))
    late = [
        pltpu.make_async_copy(weights.at[2, e], w.at[:, pl.ds(e * hidden, hidden)], s_load.at[4 + e])
        for e in range(EXP_DEV)
    ]
    late.append(pltpu.make_async_copy(mid, mids, s_load.at[4 + EXP_DEV]))
    for copy in loads + late:
        copy.start()
    greet([at.sibling, at.up, at.down], [None, has_up, has_down])

    lanes = lax.broadcasted_iota(jnp.int32, (rows, 128), 1)
    turned[...] = jnp.zeros_like(turned)
    for e in range(2 * chips):
        turned[EXP_DEV * e : EXP_DEV * (e + 1), :] = thin[e, :EXP_DEV, :]
    flipped = turned[...].T
    grad_gates = jnp.where(c == 0, flipped[:rows], flipped[rows:])
    loads[3].wait()
    logits = jnp.where(lanes < experts, nn(normed[...], near[:, :128]), NEG)
    powers = jnp.exp(logits - jnp.max(logits, axis=1, keepdims=True))
    probs = powers / jnp.sum(powers, axis=1, keepdims=True)
    named = routes[:, 0:1] == lanes
    for j in range(1, TOP):
        named = named | (routes[:, j : j + 1] == lanes)
    chosen = jnp.where(named, probs, 0.0)
    total = jnp.sum(chosen, axis=1, keepdims=True)
    gates = chosen / total
    grad_chosen = (grad_gates - jnp.sum(gates * grad_gates, axis=1, keepdims=True)) / total
    grad_probs = jnp.where(named, grad_chosen, 0.0)
    grad_logits = (
        probs * (grad_probs - jnp.sum(probs * grad_probs, axis=1, keepdims=True))
    ).astype(BF)
    grad_normed = row_sum[...] + nt(grad_logits, near[:, :128])

    for k in range(3):
        loads[k].wait()
    gate_v = nn(normed[...], shared[0])
    up_v = nn(normed[...], shared[1])
    back = nn(cot[...], shared[2])
    act, slope = silu_parts(gate_v)
    shared_mid = (act * up_v).astype(BF)
    gate_grad = (back * up_v * slope).astype(BF)
    up_grad = (back * act).astype(BF)
    grad_normed = grad_normed + nt(gate_grad, shared[0]) + nt(up_grad, shared[1])

    inverse = inverse_rms(middle[...])
    unit = middle[...] * inverse
    gain_grad = jnp.sum(grad_normed * unit, axis=0, keepdims=True)
    scaled = grad_normed * gain[...]
    grad_middle = cot[...].astype(F32) + inverse * (
        scaled - unit * jnp.mean(scaled * unit, axis=-1, keepdims=True)
    )
    middle_out[...] = grad_middle
    attn = grad_middle.astype(BF)
    own[...] = nn(attn, near[:, 128:]).astype(BF)
    columns = jnp.zeros((rows, 128), F32)
    for h in range(H):
        s = slice(h * HD, (h + 1) * HD)
        delta = jnp.sum(own[:, s].astype(F32) * attended_full[:, s], axis=1, keepdims=True)
        delta_out[h] = jnp.broadcast_to(delta, (rows, 8))
        columns = jnp.where(lanes == h, log_own[h][:, :1], columns)
        columns = jnp.where(lanes == H + h, delta, columns)
    tall = side.shape[1]
    columns = jnp.concatenate([columns, jnp.zeros((tall - rows, 128), F32)], axis=0)
    side[...] = columns.T[: side.shape[0]]

    pairs = (
        (own, all_out, s_chain, r_chain, s_core, r_core),
        (side, side_out, s_side, r_side, s_score, r_score),
    )

    def along(p, zz, direction, src=None):
        out, ss, rs = pairs[p][1:4]
        ref = out.at[2 * zz + c]
        device = at.up if direction == 0 else at.down
        return sent(ref if src is None else src, ref, ss.at[direction, zz], rs.at[zz], device)

    def over(p, zz, core, src=None):
        out, ss, rs = pairs[p][1], pairs[p][4], pairs[p][5]
        ref = out.at[2 * zz + core]
        return sent(ref if src is None else src, ref, ss.at[zz], rs.at[zz], at.sibling)

    locals_ = []
    for p in (1, 0):

        @pl.when(has_up)
        def _(p=p):
            along(p, z, 0, pairs[p][0]).start()

        @pl.when(has_down)
        def _(p=p):
            along(p, z, 1, pairs[p][0]).start()

        over(p, z, c, pairs[p][0]).start()
        copy = pltpu.make_async_copy(
            pairs[p][0], pairs[p][1].at[2 * z + c], s_load.at[5 + EXP_DEV + p]
        )
        copy.start()
        locals_.append(copy)

    def arrived(zz, direction):
        for p in (1, 0):
            along(p, zz, direction).wait_recv()

            @pl.when(has_up if direction == 0 else has_down)
            def _(p=p):
                along(p, zz, direction).start()

            over(p, zz, c).start()

    def at_distance(k):
        @pl.when(z - k >= 0)
        def _():
            arrived(z - k, 0)

        @pl.when(z + k < chips)
        def _():
            arrived(z + k, 1)

    stores = []

    def store(src, dst, k):
        copy = pltpu.make_async_copy(src, dst, s_dense.at[k])
        copy.start()
        stores.append(copy)

    def mix_chip(zz):
        here = pl.ds(zz * 2 * rows, 2 * rows)
        for n in range(0, width, 256):
            tile = nt(mids[here, :], w[n : n + 256, :]).astype(BF)
            mix[zz, 0, :, n : n + 256] = tile[:rows]
            mix[zz, 1, :, n : n + 256] = tile[rows:]
        store(mix.at[zz], mix_out.at[zz], 4 + zz)

    dense[0] = tn(normed[...], gate_grad).astype(BF)
    store(dense.at[0], gate_out, 0)
    dense[1] = tn(normed[...], up_grad).astype(BF)
    store(dense.at[1], up_out, 1)
    dense[2] = tn(cot[...], shared_mid).astype(BF)
    store(dense.at[2], down_out, 2)
    wide[...] = tn(attn, attended_full[...].astype(BF)).astype(BF)
    store(wide, out_out, 3)
    base_out[...] = middle[...] + nt(shared_mid, shared[2])
    at_distance(1)
    for copy in late:
        copy.wait()
    half = (chips + 1) // 2
    for j in range(half):
        mix_chip(j)
    for k in range(2, chips):
        at_distance(k)
        if k == 2:
            for j in range(half, chips):
                mix_chip(j)
            all_lanes = lax.broadcasted_iota(jnp.int32, (width, 128), 1)
            column = jnp.broadcast_to(gain_grad, (8, width)).T[:, :1]
            misc_out[:, :128] = jnp.where(
                all_lanes == experts + 1, column, tn(normed[...], grad_logits)
            )
            misc_out[:, 128:] = jnp.zeros((width, 128), F32)
    for p in (1, 0):
        for zz in range(chips):
            over(p, zz, 1 - c).wait_recv()
            over(p, zz, c).wait_send()

            @pl.when((zz <= z) & has_up)
            def _(p=p, zz=zz):
                along(p, zz, 0).wait_send()

            @pl.when((zz >= z) & has_down)
            def _(p=p, zz=zz):
                along(p, zz, 1).wait_send()

    for copy in locals_ + stores:
        copy.wait()


def spread(
    mid, weights, shared, near, normed, cot, row_sum, thin, routes, middle, gain, attended, log_own, experts, collective_id
):
    rows, width = normed.shape
    keys, both = mid.shape
    chain = keys // rows
    chips = chain // 2
    hidden = both // EXP_DEV
    assert experts + 2 <= 128 and chips > 2
    tall = 128 * (-(-rows // 128))
    lines = 8 * (-(-2 * H // 8))
    dma = pltpu.SemaphoreType.DMA
    anywhere = pl.BlockSpec(memory_space=pl.ANY)
    vmem = pl.BlockSpec(memory_space=pltpu.VMEM)
    out = jax.ShapeDtypeStruct
    return pl.pallas_call(
        functools.partial(spread_kernel, chips, experts),
        out_shape=[
            out((chain, rows, width), BF),
            out((chain, lines, tall), F32),
            out((chips, 2, rows, width), BF),
            out((width, hidden), BF),
            out((width, hidden), BF),
            out((width, hidden), BF),
            out((width, width), BF),
            out((rows, width), F32),
            out((rows, width), F32),
            out((width, 256), F32),
            out((H, rows, 8), F32),
        ],
        in_specs=[anywhere] * 4 + [vmem] * 9,
        out_specs=[anywhere] * 7 + [vmem] * 4,
        scratch_shapes=[
            pltpu.VMEM((keys, both), BF),
            pltpu.VMEM((width, both), BF),
            pltpu.VMEM((chips, 2, rows, width), BF),
            pltpu.VMEM((3, width, hidden), BF),
            pltpu.VMEM((width, width), BF),
            pltpu.VMEM((3, width, hidden), BF),
            pltpu.VMEM(near.shape, BF),
            pltpu.VMEM((rows, width), BF),
            pltpu.VMEM((lines, tall), F32),
            pltpu.VMEM((128, 2 * rows), F32),
            dma((7 + EXP_DEV,)),
            dma((4 + chips,)),
        ]
        + [dma((2, chips)), dma((chips,)), dma((chips,)), dma((chips,))] * 2,
        compiler_params=pltpu.CompilerParams(
            vmem_limit_bytes=MOE_VMEM, collective_id=collective_id, has_side_effects=True
        ),
        cost_estimate=pl.CostEstimate(
            flops=2 * keys * both * width, bytes_accessed=64 * keys * width, transcendentals=0
        ),
    )(mid, weights, shared, near, normed, cot, row_sum, thin, routes, middle, gain, attended, log_own)


def finish_kernel(chips, chunks, n_in, experts, *refs):
    ins = refs[:n_in]
    normed, projected, weight_in, misc_in, unit, inverse, gain, grad_middle, mix_in, base = refs[
        n_in : n_in + 10
    ]
    n_out = n_in + 2
    outs = refs[n_in + 10 : n_in + 10 + n_out]
    input_out, output_out = refs[n_in + 10 + n_out : n_in + 12 + n_out]
    rest = refs[n_in + 12 + n_out :]
    s_in, s_core, r_core, s_one, r_one, s_two, r_two, s_end, r_end = rest[:9]
    s_mix, s_mcore, r_mcore, s_mchain, r_mchain, s_weight = rest[9:15]
    weight, grad_ref, tile_ref, mix_mine, mix_other, mix_came = rest[15:21]
    buffers = rest[21:]
    n_chunks = len(chunks)
    at = Place(chips)
    z, c, x, y = at.z, at.c, at.x, at.y
    chain = 2 * chips
    others = [(at.d, 2 * lax.rem(z + k, chips) + c) for k in range(1, chips)]
    devices = [at.sibling, at.across_x, at.across_y] + others
    greet(devices, [None] * len(devices))

    class Chunk:
        def __init__(self, q):
            self.i, self.first, self.wide = chunks[q]
            self.q = q
            self.made = self.i >= n_in
            self.mine, self.other, one_x, one_y, two_x, two_y, self.end, self.give = buffers[
                8 * q : 8 * q + 8
            ]
            self.one, self.two = (one_x, one_y), (two_x, two_y)
            self.cols = pl.ds(self.first, self.wide)
            cut = self.wide // 256 * 128
            self.half = (pl.ds(0, cut), pl.ds(cut, self.wide - cut))

        def load(self):
            return pltpu.make_async_copy(
                ins[self.i].at[:, :, :, c, :, self.cols], self.mine, s_in.at[self.q]
            )

        def core(self):
            source = self.give if self.made else ins[self.i].at[:, :, :, 1 - c, :, self.cols]
            return sent(source, self.other, s_core.at[self.q], r_core.at[self.q], at.sibling)

        def first_x(self):
            return sent(
                self.mine.at[:, 1 - x, :, :, self.half[0]],
                self.one[0],
                s_one.at[self.q, 0],
                r_one.at[self.q, 0],
                at.across_x,
            )

        def first_y(self):
            return sent(
                self.mine.at[1 - y, :, :, :, self.half[1]],
                self.one[1],
                s_one.at[self.q, 1],
                r_one.at[self.q, 1],
                at.across_y,
            )

        def second_y(self):
            return sent(
                self.mine.at[1 - y, x, :, :, self.half[0]],
                self.two[0],
                s_two.at[self.q, 0],
                r_two.at[self.q, 0],
                at.across_y,
            )

        def second_x(self):
            return sent(
                self.mine.at[y, 1 - x, :, :, self.half[1]],
                self.two[1],
                s_two.at[self.q, 1],
                r_two.at[self.q, 1],
                at.across_x,
            )

        def last(self, k):
            zz = lax.rem(z + k, chips)
            return sent(
                self.mine.at[y, x, zz],
                self.end.at[k - 1],
                s_end.at[self.q, k - 1],
                r_end.at[self.q, k - 1],
                (at.d, 2 * zz + c),
            )

        def take(self):
            block = self.mine.shape[3]

            def body(k, carry):
                yy, xx, zz = k // (2 * chips), (k // chips) % 2, k % chips
                row = (2 * yy + xx) * chain + 2 * zz
                keep = pl.ds(pl.multiple_of((row + c) * block, block), block)
                away = pl.ds(pl.multiple_of((row + 1 - c) * block, block), block)
                self.mine[yy, xx, zz] = tile_ref[keep, : self.wide].astype(BF)
                self.give[yy, xx, zz] = tile_ref[away, : self.wide].astype(BF)
                return carry

            lax.fori_loop(0, 4 * chips, body, 0, unroll=4)
            self.core().start()

    parts = [Chunk(q) for q in range(n_chunks)]

    def stage_one(p):
        p.core().wait_recv()
        if not p.made:
            p.load().wait()

        def body(k, carry):
            yy, xx, zz = k // (2 * chips), (k // chips) % 2, k % chips
            p.mine[yy, xx, zz] = p.mine[yy, xx, zz] + p.other[yy, xx, zz]
            return carry

        lax.fori_loop(0, 4 * chips, body, 0, unroll=4)
        p.first_x().start()
        p.first_y().start()

    def stage_two(p):
        p.first_x().wait_recv()
        p.first_y().wait_recv()

        def body(k, carry):
            v, zz = k // chips, k % chips
            a, b = p.half
            p.mine[v, x, zz, :, a] = p.mine[v, x, zz, :, a] + p.one[0][v, zz]
            p.mine[y, v, zz, :, b] = p.mine[y, v, zz, :, b] + p.one[1][v, zz]
            return carry

        lax.fori_loop(0, 2 * chips, body, 0, unroll=2)
        p.second_y().start()
        p.second_x().start()

    def stage_three(p):
        p.second_y().wait_recv()
        p.second_x().wait_recv()

        def body(zz, carry):
            for w in (0, 1):
                s = p.half[w]
                p.mine[y, x, zz, :, s] = p.mine[y, x, zz, :, s] + p.two[w][zz]
            return carry

        lax.fori_loop(0, chips, body, 0, unroll=2)
        for k in range(1, chips):
            p.last(k).start()

    def stage_four(p):
        total = p.mine[y, x, z].astype(F32)
        for k in range(1, chips):
            p.last(k).wait_recv()
            total = total + p.end[k - 1].astype(F32)
        outs[p.i][:, p.first : p.first + p.wide] = total

    def mix_load(zz):
        return pltpu.make_async_copy(mix_in.at[zz, c], mix_mine.at[zz], s_mix.at[zz])

    def mix_core(zz):
        return sent(
            mix_in.at[zz, 1 - c], mix_other.at[zz], s_mcore.at[zz], r_mcore.at[zz], at.sibling
        )

    def mix_over(k):
        zz = lax.rem(z + k, chips)
        return sent(
            mix_mine.at[zz], mix_came.at[k], s_mchain.at[k], r_mchain.at[k], (at.d, 2 * zz + c)
        )

    def mix_settle():
        for k in range(1, chips):
            zz = lax.rem(z + k, chips)
            mix_core(zz).wait_recv()
            mix_load(zz).wait()
            mix_mine[zz] = (mix_mine[zz].astype(F32) + mix_other[zz].astype(F32)).astype(BF)
            mix_over(k).start()
        mix_core(z).wait_recv()
        mix_load(z).wait()

    part = projected.shape[2]

    def weight_load(k):
        return pltpu.make_async_copy(
            weight_in.at[:, pl.ds(k * part, part)], weight, s_weight.at[0]
        )

    def input_grads(k):
        weight_load(k).wait()
        if k == 0:
            grad_ref[...] = nt(projected[0], weight[...])
        else:
            grad_ref[...] += nt(projected[k], weight[...])
        if k < 2:
            weight_load(k + 1).start()
            return
        grad = grad_ref[...]
        gains = jnp.sum(grad * unit[...], axis=0, keepdims=True)
        column = jnp.broadcast_to(gains, (8, part)).T[:, :1]
        lanes = lax.broadcasted_iota(jnp.int32, misc_in.shape, 1)
        tile_ref[:, : misc_in.shape[1]] = jnp.where(lanes == experts, column, misc_in[...])
        scaled = grad * gain[...]
        mean = jnp.mean(scaled * unit[...], axis=1, keepdims=True)
        input_out[...] = (grad_middle[...] + inverse[...] * (scaled - unit[...] * mean)).astype(BF)

    for k in range(1, chips + 1):
        zz = lax.rem(z + k, chips)
        mix_core(zz).start()
        mix_load(zz).start()
    for p in parts:
        if not p.made:
            p.core().start()
            p.load().start()
    weight_load(0).start()
    mix_settle()
    n_known = sum(not p.made for p in parts)
    n_made = n_chunks - 1 - n_known
    stages = ((0, stage_one), (1, stage_two), (2, stage_three), (6, stage_four))
    for t in range(n_chunks + stages[-1][0]):
        for lag, stage in stages:
            if 0 <= t - lag < n_chunks:
                stage(parts[t - lag])
        if t < n_made:
            p = parts[n_known + t]
            k, first = p.first // part, p.first % part
            tile_ref[:, : p.wide] = tn(normed[...], projected[k, :, first : first + p.wide])
            p.take()
        elif t < n_made + 3:
            input_grads(t - n_made)
            if t == n_made + 2:
                parts[-1].take()
    total = base[...] + mix_mine[z].astype(F32) + mix_other[z].astype(F32)
    for k in range(1, chips):
        mix_over(k).wait_recv()
        total = total + mix_came[k].astype(F32)
    output_out[...] = total.astype(BF)
    for p in parts:
        p.core().wait_send()
        p.first_x().wait_send()
        p.first_y().wait_send()
        p.second_x().wait_send()
        p.second_y().wait_send()
        for k in range(1, chips):
            p.last(k).wait_send()
    for k in range(1, chips):
        mix_over(k).wait_send()
    for zz in range(chips):
        mix_core(zz).wait_send()


def finish(
    arrays,
    chunk_widths,
    experts,
    normed,
    projected,
    qkv_weight,
    misc,
    unit,
    inverse,
    gain,
    grad_middle,
    mix,
    base,
    collective_id,
):
    chain = lax.axis_size("expert")
    chips = chain // 2
    width = arrays[0].shape[0]
    block = width // (4 * chain)
    rows = normed.shape[0]
    columns = qkv_weight.shape[1]
    n = len(arrays)
    dma = pltpu.SemaphoreType.DMA
    sizes = [a.shape[1] for a in arrays] + [columns, misc.shape[1]]
    chunks = []
    for i, (size, wide) in enumerate(zip(sizes, chunk_widths)):
        assert size % wide == 0 and wide % 128 == 0 and wide >= 256
        chunks += [(i, first, wide) for first in range(0, size, wide)]
    q = len(chunks)
    scratch = [dma((q,)), dma((q,)), dma((q,))] + [dma((q, 2))] * 4 + [dma((q, chips - 1))] * 2
    scratch += [dma((chips,))] * 5 + [dma((1,))]
    scratch += [
        pltpu.VMEM((width, columns // 3), BF),
        pltpu.VMEM((rows, width), F32),
        pltpu.VMEM((width, max(chunk_widths[n:])), F32),
        pltpu.VMEM((chips, rows, width), BF),
        pltpu.VMEM((chips, rows, width), BF),
        pltpu.VMEM((chips, rows, width), BF),
    ]
    for i, first, wide in chunks:
        cut = wide // 256 * 128
        scratch += [
            pltpu.VMEM((2, 2, chips, block, wide), BF),
            pltpu.VMEM((2, 2, chips, block, wide), BF),
            pltpu.VMEM((2, chips, block, cut), BF),
            pltpu.VMEM((2, chips, block, wide - cut), BF),
            pltpu.VMEM((chips, block, cut), BF),
            pltpu.VMEM((chips, block, wide - cut), BF),
            pltpu.VMEM((chips - 1, block, wide), BF),
            pltpu.VMEM((2, 2, chips, block, wide) if i >= n else (16, 128), BF),
        ]
    anywhere = pl.BlockSpec(memory_space=pl.ANY)
    vmem = pl.BlockSpec(memory_space=pltpu.VMEM)
    return pl.pallas_call(
        functools.partial(finish_kernel, chips, tuple(chunks), n, experts),
        out_shape=[jax.ShapeDtypeStruct((block, size), F32) for size in sizes]
        + [jax.ShapeDtypeStruct((rows, width), BF)] * 2,
        in_specs=[anywhere] * n
        + [vmem, vmem, anywhere, vmem, vmem, vmem, vmem, vmem, anywhere, vmem],
        out_specs=[vmem] * (n + 4),
        scratch_shapes=scratch,
        compiler_params=pltpu.CompilerParams(
            vmem_limit_bytes=MOE_VMEM, collective_id=collective_id, has_side_effects=True
        ),
        cost_estimate=pl.CostEstimate(
            flops=4 * rows * width * columns, bytes_accessed=64 * width * columns, transcendentals=0
        ),
    )(
        *[a.reshape(2, 2, chips, 2, block, a.shape[1]) for a in arrays],
        normed,
        projected,
        qkv_weight,
        misc,
        unit,
        inverse,
        gain,
        grad_middle,
        mix,
        base,
    )


def silu_parts(values):
    s = jax.nn.sigmoid(values)
    return values * s, s * (1.0 + values * (1.0 - s))


def local(
    tokens,
    cotangent,
    lengths,
    routes,
    attn_qkv,
    attn_out,
    shared_gate,
    shared_up,
    shared_down,
    router,
    gains,
    expert_gate,
    expert_up,
    expert_down,
):
    rows = tokens.shape[1]
    width = tokens.shape[2]
    hidden = shared_gate.shape[1]
    chain = lax.axis_size("expert")
    index = lax.axis_index("expert")
    experts = EXP_DEV * chain
    everyone = ("dp", "expert")
    keys = rows * chain
    own_first = index * rows
    me = index.reshape(1).astype(jnp.int32)

    route_pad = 128 * (-(-(experts + 2) // 128))
    misc = jnp.concatenate([router.astype(BF), gains.astype(BF).T], axis=1)
    misc = jnp.pad(misc, ((0, 0), (0, route_pad - experts - 2)))
    near = jnp.concatenate([misc, attn_out.astype(BF).T], axis=1)
    expert_shard = jnp.stack(
        [expert_gate.astype(BF), expert_up.astype(BF), jnp.swapaxes(expert_down.astype(BF), 1, 2)]
    )
    expert_weight = lax.all_gather(expert_shard, "dp", axis=2, tiled=True)
    shared = jnp.concatenate(
        [shared_gate.astype(BF), shared_up.astype(BF), shared_down.astype(BF).T], axis=1
    )
    fits = 2 * width * EXP_DEV * hidden * 3 + 2 * keys * (3 * EXP_DEV * hidden + 5 * width) < MOE_VMEM
    chained = [tokens[0], routes[0], cotangent[0]] + ([shared] if fits else [])
    qkv_weight, near, tokens_all, routes_all, grads_all, *early = gather(
        [attn_qkv.astype(BF), near], chained, 0
    )
    shared = early[0] if fits else shared
    grads_all = grads_all.reshape(keys, width)
    qkv_weight = qkv_weight.reshape(width, 3 * H * HD)
    near = near.reshape(width, near.shape[-1])
    tokens_all = tokens_all.reshape(keys, width)
    routes_all = routes_all.reshape(keys, TOP)
    cuts = [route_pad, route_pad + width]
    cuts += [cuts[-1] + hidden, cuts[-1] + 2 * hidden]
    misc, out_t = jnp.split(near, cuts[:1], axis=1)
    route_weight = misc[:, :experts]
    gain_attn = misc[:, experts].astype(F32)
    gain_moe = misc[:, experts + 1].astype(F32)
    first_all, rope_all = doc_starts_of(lengths[0], jnp.arange(keys, dtype=jnp.int32))
    first_own = lax.dynamic_slice_in_dim(first_all, own_first, rows, 0)
    cosine, sine = turn_tables(rope_all)
    cosine_own = lax.dynamic_slice_in_dim(cosine, own_first, rows, 0)
    sine_own = lax.dynamic_slice_in_dim(sine, own_first, rows, 0)
    cosine_own = jnp.concatenate([cosine_own, cosine_own], axis=1)
    sine_own = jnp.concatenate([-sine_own, sine_own], axis=1)
    inputs = tokens[0].astype(F32)
    inverse_one = inverse_rms(inputs)
    unit_one = inputs * inverse_one
    normed = (unit_one * gain_attn).astype(BF)
    qkv = project_qkv(tokens_all, qkv_weight, gain_attn, cosine, sine)
    attended_full, log_own = attend(me, qkv, first_own)
    attended = attended_full.astype(BF)
    middle = inputs + nt(attended, out_t)
    inverse_two = inverse_rms(middle)
    unit_two = middle * inverse_two
    normed_moe = (unit_two * gain_moe).astype(BF)
    shared, expert_weight, normed_moe = lax.optimization_barrier((shared, expert_weight, normed_moe))
    shared = lax.all_gather(shared, "dp" if fits else everyone, axis=0, tiled=True)
    shared = shared.reshape(width, 3 * hidden)
    gate_shared, up_shared, down_t = jnp.split(shared, [hidden, 2 * hidden], axis=1)

    def routing(activations, route_ids):
        logits = nn(activations, route_weight)
        probs = jax.nn.softmax(logits, axis=-1)
        named = route_ids[:, :, None] == jnp.arange(experts, dtype=jnp.int32)[None, None, :]
        named = jnp.any(named, axis=1)
        chosen = jnp.where(named, probs, 0.0)
        total = jnp.sum(chosen, axis=1, keepdims=True)
        return probs, named, chosen / total, total

    if fits:
        row_sum, gate_grads, expert_mid, expert_grads = moe_fused(
            normed_moe, routes_all, grads_all, near, expert_weight, experts, 1
        )
        (
            grad_all,
            side_all,
            mixture,
            grad_gate_shared,
            grad_up_shared,
            grad_down_t,
            grad_out_t,
            base,
            grad_middle,
            grad_misc,
            delta_own,
        ) = spread(
            expert_mid,
            expert_weight,
            shared,
            near,
            normed_moe,
            cotangent[0],
            row_sum,
            gate_grads,
            routes[0],
            middle,
            gain_moe[None, :],
            attended_full,
            log_own,
            experts,
            3,
        )
        side_all = side_all[:, : 2 * H, :rows]
    else:
        probs, named, gates, chosen_total = routing(normed_moe, routes[0])

        shared_gate_v = nn(normed_moe, gate_shared)
        shared_up_v = nn(normed_moe, up_shared)
        shared_act, shared_slope = silu_parts(shared_gate_v)
        shared_mid = (shared_act * shared_up_v).astype(BF)
        shared_out = nt(shared_mid, down_t)
        grad_out = cotangent[0].astype(F32)
        grad_bf = cotangent[0]
        grad_shared_mid = nn(grad_bf, down_t)
        grad_shared_gate_v = (grad_shared_mid * shared_up_v * shared_slope).astype(BF)
        grad_shared_up_v = (grad_shared_mid * shared_act).astype(BF)
        grad_normed_moe = nt(grad_shared_gate_v, gate_shared) + nt(grad_shared_up_v, up_shared)

        moe_all = gather([], [normed_moe], 1)[0].reshape(keys, width)
        unused, unused, gates_all, unused = routing(moe_all, routes_all)
        gates_here = lax.dynamic_slice_in_dim(gates_all, index * EXP_DEV, EXP_DEV, 1)
        row_part, gate_grads, expert_mid, expert_grads = moe_plain(
            moe_all, gates_here, grads_all, expert_weight
        )
        gate_grads = jnp.transpose(gate_grads.T.reshape(EXP_DEV, chain, rows), (1, 0, 2))
        row_sum, gate_grads = to_owner(row_part.reshape(chain, rows, width), gate_grads, 2)
        gate_grads = gate_grads.reshape(experts, rows).T
        grad_chosen = (gate_grads - jnp.sum(gates * gate_grads, axis=1, keepdims=True)) / chosen_total
        grad_probs = jnp.where(named, grad_chosen, 0.0)
        grad_logits = (
            probs * (grad_probs - jnp.sum(probs * grad_probs, axis=1, keepdims=True))
        ).astype(BF)
        grad_route = tn(normed_moe, grad_logits)
        grad_normed_moe = grad_normed_moe + row_sum + nt(grad_logits, route_weight)
        grad_gain_moe = jnp.sum(grad_normed_moe * unit_two, axis=0)
        scaled_two = grad_normed_moe * gain_moe
        grad_middle = grad_out + inverse_two * (
            scaled_two - unit_two * jnp.mean(scaled_two * unit_two, axis=-1, keepdims=True)
        )
        grad_attn = grad_middle.astype(BF)
        grad_attended = nn(grad_attn, out_t).astype(BF)

        delta = jnp.sum((grad_attended.astype(F32) * attended_full).reshape(rows, H, HD), axis=-1).T
        side = jnp.concatenate([log_own[:, :, 0], delta], axis=0)
        grad_all, side_all = gather([], [grad_attended, side], 3)
        delta_own = jnp.broadcast_to(delta[:, :, None], (H, rows, 8))
    expert_sum = lax.psum_scatter(expert_grads, "dp", scatter_dimension=2, tiled=True)
    grad_all = grad_all.reshape(keys, H * HD)
    side_all = jnp.transpose(side_all, (1, 0, 2)).reshape(2, H, 1, keys)
    grads = attend_back(
        me,
        qkv,
        grad_all,
        log_own,
        delta_own,
        side_all[0],
        side_all[1],
        (first_own, first_all),
        cosine_own,
        sine_own,
    )
    if fits:
        out_sum, gate_sum, up_sum, down_sum, qkv_sum, misc_sum, grad_inputs, output = finish(
            [grad_out_t, grad_gate_shared, grad_up_shared, grad_down_t],
            (640, hidden, hidden, hidden, 640, 256),
            experts,
            normed,
            grads,
            qkv_weight,
            grad_misc,
            unit_one,
            inverse_one,
            gain_attn[None, :],
            grad_middle,
            mixture,
            base,
            4,
        )
    else:
        grad_misc = jnp.concatenate(
            [grad_route, jnp.zeros((width, 1), F32), grad_gain_moe[:, None]], axis=1
        )
        grad_misc = jnp.pad(grad_misc, ((0, 0), (0, 256 - experts - 2)))
        down = expert_weight[2]
        mixture = nt(expert_mid[:, :hidden], down[0])
        for e in range(1, EXP_DEV):
            mixture = mixture + nt(expert_mid[:, e * hidden : (e + 1) * hidden], down[e])
        mixture = lax.psum_scatter(mixture.astype(BF), "expert", scatter_dimension=0, tiled=True)
        output = (middle + shared_out + mixture.astype(F32)).astype(BF)
        grad_projected = jnp.concatenate([grads[0], grads[1], grads[2]], axis=1)
        grad_normed_one = nt(grad_projected, qkv_weight)
        grad_gain_attn = jnp.sum(grad_normed_one * unit_one, axis=0)
        scaled_one = grad_normed_one * gain_attn
        grad_inputs = grad_middle + inverse_one * (
            scaled_one - unit_one * jnp.mean(scaled_one * unit_one, axis=-1, keepdims=True)
        )
        grad_inputs = grad_inputs.astype(BF)
        out_sum, gate_sum, up_sum, down_sum, qkv_sum, misc_sum = sum_dense(
            [
                tn(grad_attn, attended).astype(BF),
                tn(normed_moe, grad_shared_gate_v).astype(BF),
                tn(normed_moe, grad_shared_up_v).astype(BF),
                tn(grad_bf, shared_mid).astype(BF),
                tn(normed, grad_projected).astype(BF),
                grad_misc.at[:, experts].set(grad_gain_attn).astype(BF),
            ],
            (640, hidden, hidden, hidden, 768, 256),
            4,
        )
    return (
        output[None],
        grad_inputs[None],
        qkv_sum,
        out_sum.T,
        gate_sum,
        up_sum,
        down_sum.T,
        misc_sum[:, :experts],
        misc_sum[:, experts : experts + 2].T,
        expert_sum[0].astype(F32),
        expert_sum[1].astype(F32),
        jnp.swapaxes(expert_sum[2], 1, 2).astype(F32),
    )


def solution(mesh):
    everyone = ("dp", "expert")
    in_specs = (
        P("dp", "expert", None),
        P("dp", "expert", None),
        P("dp", None),
        P("dp", "expert", None),
        P(everyone, None),
        P(None, everyone),
        P(everyone, None),
        P(everyone, None),
        P(None, everyone),
        P(everyone, None),
        P(None, everyone),
        P("expert", "dp", None),
        P("expert", "dp", None),
        P("expert", None, "dp"),
    )
    out_specs = (
        P("dp", "expert", None),
        P("dp", "expert", None),
        P(everyone, None),
        P(None, everyone),
        P(everyone, None),
        P(everyone, None),
        P(None, everyone),
        P(everyone, None),
        P(None, everyone),
        P("expert", "dp", None),
        P("expert", "dp", None),
        P("expert", None, "dp"),
    )
    return jax.shard_map(local, mesh=mesh, in_specs=in_specs, out_specs=out_specs, check_vma=False)
```

```python
import functools

import jax
import jax.numpy as jnp
from jax import lax
from jax.experimental import pallas as pl
from jax.experimental.pallas import tpu as pltpu
from jax.sharding import PartitionSpec as P

H = 10
HD = 128
TOP = 7
EXP_DEV = 2
EPS = 1e-06
NEG = -1e30
BF = jnp.bfloat16
F32 = jnp.float32
VMEM_LIMIT = 56 * 1024 * 1024
MOE_VMEM = 62 * 1024 * 1024


def params(**kw):
    return pltpu.CompilerParams(vmem_limit_bytes=VMEM_LIMIT, **kw)


def nn(a, b):
    return jnp.dot(a, b, preferred_element_type=F32)


def nt(a, b):
    return lax.dot_general(a, b, (((1,), (1,)), ((), ())), preferred_element_type=F32)


def tn(a, b):
    return lax.dot_general(a, b, (((0,), (0,)), ((), ())), preferred_element_type=F32)


def doc_starts_of(lengths, places):
    doc_ends = jnp.cumsum(lengths)
    doc_starts = doc_ends - lengths
    total = doc_ends[-1]
    doc_index = jnp.sum((places[:, None] >= doc_ends[None, :]).astype(jnp.int32), axis=1)
    live = places < total
    matches = doc_index[:, None] == jnp.arange(lengths.shape[0], dtype=jnp.int32)[None, :]
    first = jnp.sum(jnp.where(matches, doc_starts[None, :], 0), axis=1)
    return jnp.where(live, first, places), places - jnp.where(live, first, total)


def turn_tables(rope_pos):
    half = HD // 2
    frequency = 10000.0 ** (-jnp.arange(half, dtype=F32) / half)
    angles = rope_pos.astype(F32)[:, None] * frequency[None, :]
    return jnp.cos(angles), jnp.sin(angles)


def inverse_rms(values):
    return lax.rsqrt(jnp.mean(values * values, axis=-1, keepdims=True) + EPS)


MESH = pl.DeviceIdType.MESH


def sent(src, dst, send_sem, recv_sem, device):
    return pltpu.make_async_remote_copy(
        src_ref=src,
        dst_ref=dst,
        send_sem=send_sem,
        recv_sem=recv_sem,
        device_id=device,
        device_id_type=MESH,
    )


class Place:
    def __init__(self, chips):
        self.d = lax.axis_index("dp")
        self.e = lax.axis_index("expert")
        self.z = self.e // 2
        self.c = self.e % 2
        self.y = self.d // 2
        self.x = self.d % 2
        self.chips = chips
        self.sibling = (self.d, self.e + 1 - 2 * self.c)
        self.across_x = (self.d + 1 - 2 * self.x, self.e)
        self.across_y = (self.d + 2 - 4 * self.y, self.e)
        self.up = (self.d, self.e + 2)
        self.down = (self.d, self.e - 2)


def greet(devices, conditions):
    barrier = pltpu.get_barrier_semaphore()
    count = 0
    for device, condition in zip(devices, conditions):
        if condition is None:
            pl.semaphore_signal(barrier, inc=1, device_id=device, device_id_type=MESH)
            count = count + 1
        else:

            @pl.when(condition)
            def _(device=device):
                pl.semaphore_signal(barrier, inc=1, device_id=device, device_id_type=MESH)

            count = count + condition.astype(jnp.int32)
    pl.semaphore_wait(barrier, count)


def gather_kernel(chips, n_full, n_chain, *refs):
    n = n_full + n_chain
    ins, outs, sems = refs[:n], refs[n : 2 * n], refs[2 * n :]
    at = Place(chips)
    chain = 2 * chips
    z, c = at.z, at.c
    has_up, has_down = z < chips - 1, z > 0
    devices = [at.sibling, at.up, at.down]
    conditions = [None, has_up, has_down]
    if n_full:
        devices += [at.across_x, at.across_y]
        conditions += [None, None]
    greet(devices, conditions)
    x_dp, y_dp = at.across_x[0], at.across_y[0]
    far_dp = 3 - at.d

    class Array:
        pass

    arrays = []
    position = 0
    for i in range(n):
        a = Array()
        a.full = i < n_full
        a.own, a.out = ins[i], outs[i]
        a.local, a.s_chain, a.r_chain, a.s_core, a.r_core = sems[position : position + 5]
        position += 5
        if a.full:
            a.s_side, a.r_side, a.s_half, a.r_half = sems[position : position + 4]
            position += 4
            cut = a.own.shape[-1] // 256 * 128
            a.halves = (pl.ds(0, cut), pl.ds(cut, a.own.shape[-1] - cut))
        arrays.append(a)

    def slot(a, dd, zz, cc):
        return a.out.at[dd * chain + 2 * zz + cc] if a.full else a.out.at[2 * zz + cc]

    def core_index(a, dd, zz):
        return dd * chips + zz if a.full else zz

    def to_core(a, dd, zz, src=None):
        ref = slot(a, dd, zz, c)
        k = core_index(a, dd, zz)
        return sent(ref if src is None else src, ref, a.s_core.at[k], a.r_core.at[k], at.sibling)

    def from_core(a, dd, zz):
        ref = slot(a, dd, zz, 1 - c)
        k = core_index(a, dd, zz)
        return sent(ref, ref, a.s_core.at[k], a.r_core.at[k], at.sibling)

    def along(a, zz, direction, src=None):
        ref = slot(a, at.d, zz, c)
        device = at.up if direction == 0 else at.down
        return sent(ref if src is None else src, ref, a.s_chain.at[direction, zz], a.r_chain.at[zz], device)

    def side(a, dd, zz, axis, src=None):
        ref = slot(a, dd, zz, c)
        device = at.across_x if axis == 0 else at.across_y
        return sent(
            ref if src is None else src, ref, a.s_side.at[axis, zz], a.r_side.at[axis, zz], device
        )

    def half(a, dd, zz, which):
        ref = slot(a, dd, zz, c).at[:, a.halves[which]]
        device = at.across_y if which == 0 else at.across_x
        return sent(ref, ref, a.s_half.at[which, zz], a.r_half.at[which, zz], device)

    def present(zz):
        return (zz >= 0) & (zz < chips)

    def block_here(some, zz, direction):
        for a in some:
            along(a, zz, direction).wait_recv()
            if direction == 0:

                @pl.when(has_up)
                def _(a=a):
                    along(a, zz, 0).start()
            else:

                @pl.when(has_down)
                def _(a=a):
                    along(a, zz, 1).start()

            if a.full:
                side(a, at.d, zz, 0).start()
                side(a, at.d, zz, 1).start()
            to_core(a, at.d, zz).start()

    def side_here(zz):
        for a in arrays[:n_full]:
            side(a, x_dp, zz, 0).wait_recv()
            half(a, x_dp, zz, 0).start()
            to_core(a, x_dp, zz).start()
            side(a, y_dp, zz, 1).wait_recv()
            half(a, y_dp, zz, 1).start()
            to_core(a, y_dp, zz).start()

    def far_here(zz):
        for a in arrays[:n_full]:
            half(a, far_dp, zz, 0).wait_recv()
            half(a, far_dp, zz, 1).wait_recv()
            to_core(a, far_dp, zz).start()

    def own_here(some):
        for a in some:

            @pl.when(has_up)
            def _(a=a):
                along(a, z, 0, a.own).start()

            @pl.when(has_down)
            def _(a=a):
                along(a, z, 1, a.own).start()

            if a.full:
                side(a, at.d, z, 0, a.own).start()
                side(a, at.d, z, 1, a.own).start()
            to_core(a, at.d, z, a.own).start()
            pltpu.make_async_copy(a.own, slot(a, at.d, z, c), a.local).start()

    def at_distance(k, fn):
        @pl.when((k >= 0) & present(z - k))
        def _():
            fn(z - k)

        @pl.when((k >= 1) & present(z + k))
        def _():
            fn(z + k)

    def chain_step(some, k):
        @pl.when(present(z - k))
        def _():
            block_here(some, z - k, 0)

        @pl.when(present(z + k))
        def _():
            block_here(some, z + k, 1)

    full, chained = arrays[:n_full], arrays[n_full:]
    if n_full:
        own_here(full)

        def first_step(k, carry):
            chain_step(full, k)
            return carry

        lax.fori_loop(1, chips, first_step, 0)
    own_here(chained)

    def step(k, carry):
        if n_full:
            at_distance(k - 1, side_here)
        chain_step(chained, k)
        if n_full:
            at_distance(k - 2, far_here)
        return carry

    lax.fori_loop(1, chips + (2 if n_full else 0), step, 0)

    def finish(zz, carry):
        for a in arrays:
            for dd in range(4) if a.full else (0,):
                from_core(a, dd, zz).wait_recv()
                to_core(a, dd, zz).wait_send()

            @pl.when((zz <= z) & has_up)
            def _(a=a):
                along(a, zz, 0).wait_send()

            @pl.when((zz >= z) & has_down)
            def _(a=a):
                along(a, zz, 1).wait_send()

            if a.full:
                for axis in (0, 1):
                    side(a, at.d, zz, axis).wait_send()
                half(a, x_dp, zz, 0).wait_send()
                half(a, y_dp, zz, 1).wait_send()
        return carry

    lax.fori_loop(0, chips, finish, 0)
    for a in arrays:
        pltpu.make_async_copy(a.own, slot(a, at.d, z, c), a.local).wait()


def gather(full, chained, collective_id):
    chain = lax.axis_size("expert")
    chips = chain // 2
    spread = lax.axis_size("dp")
    assert spread == 4 and chain % 2 == 0
    dma = pltpu.SemaphoreType.DMA
    scratch = []
    for array in full:
        scratch += [dma, dma((2, chips)), dma((chips,)), dma((4 * chips,)), dma((4 * chips,))]
        scratch += [dma((2, chips))] * 4
    for array in chained:
        scratch += [dma, dma((2, chips)), dma((chips,)), dma((chips,)), dma((chips,))]
    shapes = [jax.ShapeDtypeStruct((spread * chain,) + a.shape, a.dtype) for a in full]
    shapes += [jax.ShapeDtypeStruct((chain,) + a.shape, a.dtype) for a in chained]
    n = len(full) + len(chained)
    moved = sum(s.size * s.dtype.itemsize for s in shapes)
    return pl.pallas_call(
        functools.partial(gather_kernel, chips, len(full), len(chained)),
        out_shape=shapes,
        in_specs=[pl.BlockSpec(memory_space=pl.ANY)] * n,
        out_specs=[pl.BlockSpec(memory_space=pl.ANY)] * n,
        scratch_shapes=scratch,
        compiler_params=params(collective_id=collective_id, has_side_effects=True),
        cost_estimate=pl.CostEstimate(flops=0, bytes_accessed=16 * moved, transcendentals=0),
    )(*full, *chained)


def to_owner_kernel(chips, wide_ref, thin_ref, out_ref, thin_out, mine, other, came, sems_in, s_core, r_core, s_chain, r_chain, s_thin, r_thin):
    at = Place(chips)
    chain = 2 * chips
    z, c = at.z, at.c
    devices = [(at.d, lax.rem(at.e + k, chain)) for k in range(1, chain)]
    greet(devices, [None] * (chain - 1))

    def load(zz):
        return pltpu.make_async_copy(wide_ref.at[2 * zz + c], mine.at[zz], sems_in.at[zz])

    def to_core(zz):
        return sent(
            wide_ref.at[2 * zz + 1 - c], other.at[zz], s_core.at[zz], r_core.at[zz], at.sibling
        )

    def thin(k):
        target = lax.rem(at.e + k, chain)
        return sent(
            thin_ref.at[target], thin_out.at[at.e], s_thin.at[k], r_thin.at[k], (at.d, target)
        )

    def over(k):
        zz = lax.rem(z + k, chips)
        return sent(
            mine.at[zz], came.at[k], s_chain.at[k], r_chain.at[k], (at.d, 2 * zz + c)
        )

    order = [lax.rem(z + k, chips) for k in range(1, chips)] + [z]
    for zz in order:
        to_core(zz).start()
        load(zz).start()
    for k in range(1, chain):
        thin(k).start()
    own_thin = pltpu.make_async_copy(thin_ref.at[at.e], thin_out.at[at.e], s_thin.at[0])
    own_thin.start()
    for k, zz in enumerate(order):
        to_core(zz).wait_recv()
        load(zz).wait()
        total = mine[zz].astype(F32) + other[zz].astype(F32)
        if k < chips - 1:
            mine[zz] = total.astype(BF)
            over(k + 1).start()
        else:
            out_ref[...] = total
    for k in range(1, chips):
        over(k).wait_recv()
        out_ref[...] += came[k].astype(F32)
    for k in range(1, chips):
        over(k).wait_send()
    for zz in order:
        to_core(zz).wait_send()
    own_thin.wait()
    for k in range(1, chain):
        thin(k).wait()


def to_owner(wide, thin, collective_id):
    chain, rows, width = wide.shape
    chips = chain // 2
    dma = pltpu.SemaphoreType.DMA
    return pl.pallas_call(
        functools.partial(to_owner_kernel, chips),
        out_shape=[
            jax.ShapeDtypeStruct((rows, width), F32),
            jax.ShapeDtypeStruct(thin.shape, thin.dtype),
        ],
        in_specs=[pl.BlockSpec(memory_space=pl.ANY), pl.BlockSpec(memory_space=pltpu.VMEM)],
        out_specs=[pl.BlockSpec(memory_space=pltpu.VMEM), pl.BlockSpec(memory_space=pltpu.VMEM)],
        scratch_shapes=[
            pltpu.VMEM((chips, rows, width), BF),
            pltpu.VMEM((chips, rows, width), BF),
            pltpu.VMEM((chips, rows, width), BF),
            dma((chips,)),
            dma((chips,)),
            dma((chips,)),
            dma((chips,)),
            dma((chips,)),
            dma((chain,)),
            dma((chain,)),
        ],
        compiler_params=params(collective_id=collective_id, has_side_effects=True),
        cost_estimate=pl.CostEstimate(
            flops=0, bytes_accessed=16 * wide.size * 2, transcendentals=0
        ),
    )(wide, thin)


def sum_dense_kernel(chips, chunks, n_in, *refs):
    ins, outs = refs[:n_in], refs[n_in : 2 * n_in]
    n_chunks = len(chunks)
    rest = refs[2 * n_in :]
    sems = rest[:10]
    s_in, s_core, r_core, s_one, r_one, s_two, r_two, s_end, r_end = sems[:9]
    buffers = rest[9:]
    at = Place(chips)
    z, c, x, y = at.z, at.c, at.x, at.y
    others = [(at.d, 2 * lax.rem(z + k, chips) + c) for k in range(1, chips)]
    devices = [at.sibling, at.across_x, at.across_y] + others
    greet(devices, [None] * len(devices))

    class Chunk:
        def __init__(self, q):
            i, first, wide = chunks[q]
            self.i, self.first, self.wide = i, first, wide
            self.q = q
            self.mine, self.other, one_x, one_y, two_x, two_y, self.end = buffers[7 * q : 7 * q + 7]
            self.one, self.two = (one_x, one_y), (two_x, two_y)
            self.cols = pl.ds(first, wide)
            cut = wide // 256 * 128
            self.half = (pl.ds(0, cut), pl.ds(cut, wide - cut))

        def load(self):
            return pltpu.make_async_copy(
                ins[self.i].at[:, :, :, c, :, self.cols], self.mine, s_in.at[self.q]
            )

        def core(self):
            return sent(
                ins[self.i].at[:, :, :, 1 - c, :, self.cols],
                self.other,
                s_core.at[self.q],
                r_core.at[self.q],
                at.sibling,
            )

        def first_x(self):
            return sent(
                self.mine.at[:, 1 - x, :, :, self.half[0]],
                self.one[0],
                s_one.at[self.q, 0],
                r_one.at[self.q, 0],
                at.across_x,
            )

        def first_y(self):
            return sent(
                self.mine.at[1 - y, :, :, :, self.half[1]],
                self.one[1],
                s_one.at[self.q, 1],
                r_one.at[self.q, 1],
                at.across_y,
            )

        def second_y(self):
            return sent(
                self.mine.at[1 - y, x, :, :, self.half[0]],
                self.two[0],
                s_two.at[self.q, 0],
                r_two.at[self.q, 0],
                at.across_y,
            )

        def second_x(self):
            return sent(
                self.mine.at[y, 1 - x, :, :, self.half[1]],
                self.two[1],
                s_two.at[self.q, 1],
                r_two.at[self.q, 1],
                at.across_x,
            )

        def last(self, k):
            zz = lax.rem(z + k, chips)
            return sent(
                self.mine.at[y, x, zz],
                self.end.at[k - 1],
                s_end.at[self.q, k - 1],
                r_end.at[self.q, k - 1],
                (at.d, 2 * zz + c),
            )

    parts = [Chunk(q) for q in range(n_chunks)]

    def add(ref, place, more):
        ref[place] = (ref[place].astype(F32) + more.astype(F32)).astype(BF)

    def stage_one(p):
        p.core().wait_recv()
        p.load().wait()

        def body(k, carry):
            yy, xx, zz = k // (2 * chips), (k // chips) % 2, k % chips
            p.mine[yy, xx, zz] = (
                p.mine[yy, xx, zz].astype(F32) + p.other[yy, xx, zz].astype(F32)
            ).astype(BF)
            return carry

        lax.fori_loop(0, 4 * chips, body, 0)
        p.first_x().start()
        p.first_y().start()

    def stage_two(p):
        p.first_x().wait_recv()
        p.first_y().wait_recv()

        def body(k, carry):
            v, zz = k // chips, k % chips
            a, b = p.half
            p.mine[v, x, zz, :, a] = (
                p.mine[v, x, zz, :, a].astype(F32) + p.one[0][v, zz].astype(F32)
            ).astype(BF)
            p.mine[y, v, zz, :, b] = (
                p.mine[y, v, zz, :, b].astype(F32) + p.one[1][v, zz].astype(F32)
            ).astype(BF)
            return carry

        lax.fori_loop(0, 2 * chips, body, 0)
        p.second_y().start()
        p.second_x().start()

    def stage_three(p):
        p.second_y().wait_recv()
        p.second_x().wait_recv()

        def body(zz, carry):
            for w in (0, 1):
                s = p.half[w]
                p.mine[y, x, zz, :, s] = (
                    p.mine[y, x, zz, :, s].astype(F32) + p.two[w][zz].astype(F32)
                ).astype(BF)
            return carry

        lax.fori_loop(0, chips, body, 0)
        for k in range(1, chips):
            p.last(k).start()

    def stage_four(p):
        total = p.mine[y, x, z].astype(F32)
        for k in range(1, chips):
            p.last(k).wait_recv()
            total = total + p.end[k - 1].astype(F32)
        outs[p.i][:, p.first : p.first + p.wide] = total

    for p in parts:
        p.core().start()
        p.load().start()
    stages = (stage_one, stage_two, stage_three, stage_four)
    for t in range(n_chunks + len(stages) - 1):
        for s, stage in enumerate(stages):
            if 0 <= t - s < n_chunks:
                stage(parts[t - s])
    for p in parts:
        p.core().wait_send()
        p.first_x().wait_send()
        p.first_y().wait_send()
        p.second_x().wait_send()
        p.second_y().wait_send()
        for k in range(1, chips):
            p.last(k).wait_send()


def sum_dense(arrays, chunk_widths, collective_id):
    chain = lax.axis_size("expert")
    chips = chain // 2
    assert lax.axis_size("dp") == 4
    block = arrays[0].shape[0] // (4 * chain)
    dma = pltpu.SemaphoreType.DMA
    chunks = []
    for i, (array, wide) in enumerate(zip(arrays, chunk_widths)):
        assert array.shape[1] % wide == 0 and wide % 128 == 0 and wide >= 256
        chunks += [(i, first, wide) for first in range(0, array.shape[1], wide)]
    q = len(chunks)
    scratch = [dma((q,)), dma((q,)), dma((q,))] + [dma((q, 2))] * 4 + [dma((q, max(1, chips - 1)))] * 2
    for i, first, wide in chunks:
        cut = wide // 256 * 128
        scratch += [
            pltpu.VMEM((2, 2, chips, block, wide), BF),
            pltpu.VMEM((2, 2, chips, block, wide), BF),
            pltpu.VMEM((2, chips, block, cut), BF),
            pltpu.VMEM((2, chips, block, wide - cut), BF),
            pltpu.VMEM((chips, block, cut), BF),
            pltpu.VMEM((chips, block, wide - cut), BF),
            pltpu.VMEM((max(1, chips - 1), block, wide), BF),
        ]
    n = len(arrays)
    return pl.pallas_call(
        functools.partial(sum_dense_kernel, chips, tuple(chunks), n),
        out_shape=[jax.ShapeDtypeStruct((block, a.shape[1]), F32) for a in arrays],
        in_specs=[pl.BlockSpec(memory_space=pl.ANY)] * n,
        out_specs=[pl.BlockSpec(memory_space=pltpu.VMEM)] * n,
        scratch_shapes=scratch,
        compiler_params=params(collective_id=collective_id, has_side_effects=True),
        cost_estimate=pl.CostEstimate(
            flops=0, bytes_accessed=16 * sum(a.size for a in arrays), transcendentals=0
        ),
    )(*[a.reshape(2, 2, chips, 2, block, a.shape[1]) for a in arrays])


def qkv_kernel(per_block, x_ref, w_ref, gain_ref, cos_ref, sin_ref, o_ref, normed, cosine, sine):
    column = pl.program_id(1)
    rows = x_ref.shape[0]
    step = 384 if rows % 384 == 0 else rows

    @pl.when(column == 0)
    def _():
        for r in range(0, rows, step):
            wide = x_ref[r : r + step, :].astype(F32)
            normed[r : r + step, :] = (wide * inverse_rms(wide) * gain_ref[...]).astype(BF)
        cosine[:, : HD // 2] = cos_ref[...]
        cosine[:, HD // 2 :] = cos_ref[...]
        sine[:, : HD // 2] = -sin_ref[...]
        sine[:, HD // 2 :] = sin_ref[...]

    for first in range(0, per_block, 2):
        for r in range(0, rows, step):
            product = nn(normed[r : r + step, :], w_ref[:, first * HD : (first + 2) * HD])
            for k in (0, 1):
                part = product[:, k * HD : (k + 1) * HD]
                head = column * per_block + first + k
                turned = (
                    part * cosine[r : r + step, :]
                    + pltpu.roll(part, HD // 2, 1) * sine[r : r + step, :]
                )
                o_ref[r : r + step, (first + k) * HD : (first + k + 1) * HD] = jnp.where(
                    head < 2 * H, turned, part
                ).astype(BF)


def project_qkv(tokens, weight, gain, cosine, sine):
    rows, width = tokens.shape
    columns = weight.shape[1]
    per_block = 6
    tile_m = min(rows, 1536)
    return pl.pallas_call(
        functools.partial(qkv_kernel, per_block),
        out_shape=jax.ShapeDtypeStruct((rows, columns), BF),
        grid=(rows // tile_m, columns // (per_block * HD)),
        in_specs=[
            pl.BlockSpec((tile_m, width), lambda m, n: (m, 0)),
            pl.BlockSpec((width, per_block * HD), lambda m, n: (0, n)),
            pl.BlockSpec((1, width), lambda m, n: (0, 0)),
            pl.BlockSpec((tile_m, HD // 2), lambda m, n: (m, 0)),
            pl.BlockSpec((tile_m, HD // 2), lambda m, n: (m, 0)),
        ],
        out_specs=pl.BlockSpec((tile_m, per_block * HD), lambda m, n: (m, n)),
        scratch_shapes=[
            pltpu.VMEM((tile_m, width), BF),
            pltpu.VMEM((tile_m, HD), F32),
            pltpu.VMEM((tile_m, HD), F32),
        ],
        compiler_params=params(),
        cost_estimate=pl.CostEstimate(
            flops=2 * rows * width * columns,
            bytes_accessed=2 * (rows * width + width * columns + rows * columns),
            transcendentals=0,
        ),
    )(tokens, weight, gain[None, :], cosine, sine)


def attend_kernel(scale, me_ref, q_ref, k_ref, v_ref, first_ref, o_ref, log_ref, bias):
    rows, keys = bias.shape

    @pl.when(pl.program_id(0) == 0)
    def _():
        key_place = lax.broadcasted_iota(jnp.int32, (rows, keys), 1)
        query_place = me_ref[0] * rows + lax.broadcasted_iota(jnp.int32, (rows, keys), 0)
        allowed = (key_place <= query_place) & (key_place >= first_ref[...])
        bias[...] = jnp.where(allowed, 0.0, NEG)

    scores = nt(q_ref[...], k_ref[...]) * scale + bias[...]
    top = jnp.max(scores, axis=-1, keepdims=True)
    weights = jnp.exp(scores - top)
    total = jnp.sum(weights, axis=-1, keepdims=True)
    o_ref[...] = nn(weights.astype(BF), v_ref[...]) / total
    log_ref[...] = jnp.broadcast_to(top + jnp.log(total), (rows, 8))[None]


def attend(me, qkv, first_own):
    keys = qkv.shape[0]
    rows = first_own.shape[0]
    return pl.pallas_call(
        functools.partial(attend_kernel, HD**-0.5),
        out_shape=[
            jax.ShapeDtypeStruct((rows, H * HD), F32),
            jax.ShapeDtypeStruct((H, rows, 8), F32),
        ],
        grid_spec=pltpu.PrefetchScalarGridSpec(
            num_scalar_prefetch=1,
            grid=(H,),
            in_specs=[
                pl.BlockSpec((rows, HD), lambda h, me: (me[0], h)),
                pl.BlockSpec((keys, HD), lambda h, me: (0, H + h)),
                pl.BlockSpec((keys, HD), lambda h, me: (0, 2 * H + h)),
                pl.BlockSpec((rows, 1), lambda h, me: (0, 0)),
            ],
            out_specs=[
                pl.BlockSpec((rows, HD), lambda h, me: (0, h)),
                pl.BlockSpec((1, rows, 8), lambda h, me: (h, 0, 0)),
            ],
            scratch_shapes=[pltpu.VMEM((rows, keys), F32)],
        ),
        compiler_params=params(),
        cost_estimate=pl.CostEstimate(
            flops=4 * rows * keys * H * HD,
            bytes_accessed=4 * keys * H * HD,
            transcendentals=H * rows * keys,
        ),
    )(me, qkv, qkv, qkv, first_own[:, None])


def attend_back_kernel(
    scale,
    me_ref,
    q_ref,
    k_ref,
    v_ref,
    qa_ref,
    ko_ref,
    vo_ref,
    do_ref,
    da_ref,
    log_ref,
    delta_ref,
    loga_ref,
    deltaa_ref,
    first_ref,
    firsta_ref,
    cos_ref,
    sin_ref,
    o_ref,
    bias,
    biast,
):
    rows, keys = bias.shape

    @pl.when(pl.program_id(0) == 0)
    def _():
        place = lax.broadcasted_iota(jnp.int32, (rows, keys), 1)
        own = me_ref[0] * rows + lax.broadcasted_iota(jnp.int32, (rows, keys), 0)
        bias[...] = jnp.where((place <= own) & (place >= first_ref[...]), 0.0, NEG)
        biast[...] = jnp.where((own <= place) & (own >= firsta_ref[...]), 0.0, NEG)

    def unturn(value):
        return value * cos_ref[...] - pltpu.roll(value, HD // 2, 1) * sin_ref[...]

    log_own = log_ref[0][:, :1]
    delta_own = delta_ref[0][:, :1]
    weights = jnp.exp(nt(q_ref[...], k_ref[...]) * scale + bias[...] - log_own)
    back = nt(do_ref[...], v_ref[...])
    grad = (weights * (back - delta_own) * scale).astype(BF)
    o_ref[0] = unturn(nn(grad, k_ref[...])).astype(BF)

    weights = jnp.exp(nt(ko_ref[...], qa_ref[...]) * scale + biast[...] - loga_ref[0])
    o_ref[2] = nn(weights.astype(BF), da_ref[...]).astype(BF)
    back = nt(vo_ref[...], da_ref[...])
    grad = (weights * (back - deltaa_ref[0]) * scale).astype(BF)
    o_ref[1] = unturn(nn(grad, qa_ref[...])).astype(BF)


def attend_back(me, qkv, grad_all, log_own, delta_own, log_all, delta_all, first, cosine, sine):
    keys = qkv.shape[0]
    first_own, first_all = first
    rows = first_own.shape[0]
    return pl.pallas_call(
        functools.partial(attend_back_kernel, HD**-0.5),
        out_shape=jax.ShapeDtypeStruct((3, rows, H * HD), BF),
        grid_spec=pltpu.PrefetchScalarGridSpec(
            num_scalar_prefetch=1,
            grid=(H,),
            in_specs=[
                pl.BlockSpec((rows, HD), lambda h, me: (me[0], h)),
                pl.BlockSpec((keys, HD), lambda h, me: (0, H + h)),
                pl.BlockSpec((keys, HD), lambda h, me: (0, 2 * H + h)),
                pl.BlockSpec((keys, HD), lambda h, me: (0, h)),
                pl.BlockSpec((rows, HD), lambda h, me: (me[0], H + h)),
                pl.BlockSpec((rows, HD), lambda h, me: (me[0], 2 * H + h)),
                pl.BlockSpec((rows, HD), lambda h, me: (me[0], h)),
                pl.BlockSpec((keys, HD), lambda h, me: (0, h)),
                pl.BlockSpec((1, rows, 8), lambda h, me: (h, 0, 0)),
                pl.BlockSpec((1, rows, 8), lambda h, me: (h, 0, 0)),
                pl.BlockSpec((1, 1, keys), lambda h, me: (h, 0, 0)),
                pl.BlockSpec((1, 1, keys), lambda h, me: (h, 0, 0)),
                pl.BlockSpec((rows, 1), lambda h, me: (0, 0)),
                pl.BlockSpec((1, keys), lambda h, me: (0, 0)),
                pl.BlockSpec((rows, HD), lambda h, me: (0, 0)),
                pl.BlockSpec((rows, HD), lambda h, me: (0, 0)),
            ],
            out_specs=pl.BlockSpec((3, rows, HD), lambda h, me: (0, 0, h)),
            scratch_shapes=[pltpu.VMEM((rows, keys), F32)] * 2,
        ),
        compiler_params=params(),
        cost_estimate=pl.CostEstimate(
            flops=14 * rows * keys * H * HD,
            bytes_accessed=8 * keys * H * HD,
            transcendentals=2 * H * rows * keys,
        ),
    )(
        me,
        qkv,
        qkv,
        qkv,
        qkv,
        qkv,
        qkv,
        grad_all,
        grad_all,
        log_own,
        delta_own,
        log_all,
        delta_all,
        first_own[:, None],
        first_all[None, :],
        cosine,
        sine,
    )


def moe_kernel(
    chips,
    experts,
    x_own,
    routes,
    grads,
    near_in,
    weights,
    row_out,
    thin_out,
    mid_out,
    grad_out,
    x_all,
    g_all,
    w,
    hid,
    part,
    other,
    came,
    thin,
    dots,
    misc,
    s_load,
    s_x,
    r_x,
    s_fwd,
    r_fwd,
    s_part,
    r_part,
    s_came,
    r_came,
    s_thin,
    r_thin,
):
    at = Place(chips)
    z, c = at.z, at.c
    chain = 2 * chips
    rows, width = x_own.shape
    both = w.shape[2]
    tiles = both // 256
    per_expert = both // 256
    greet([(at.d, lax.rem(at.e + k, chain)) for k in range(1, chain)], [None] * (chain - 1))

    near = jnp.minimum(z, chips - 1 - z)

    def order(j):
        step = (j + 1) // 2
        around = jnp.where(j % 2 == 1, z - step, z + step)
        return jnp.where(j <= 2 * near, around, jnp.where(2 * z < chips, j, chips - 1 - j))

    def own_load():
        return pltpu.make_async_copy(x_own, x_all.at[z, c], s_load.at[0])

    hidden = both // EXP_DEV

    def weight_load(k, e):
        return pltpu.make_async_copy(
            weights.at[k, e], w.at[k, :, pl.ds(e * hidden, hidden)], s_load.at[2 + 2 * k + e]
        )

    def grad_store(k, e):
        return pltpu.make_async_copy(
            w.at[k, :, pl.ds(e * hidden, hidden)], grad_out.at[k, e], s_load.at[2 + 2 * k + e]
        )

    def grads_load():
        return pltpu.make_async_copy(grads, g_all, s_load.at[1])

    def x_send(zz):
        return sent(x_own, x_all.at[z, c], s_x.at[zz], r_x.at[z], (at.d, 2 * zz + c))

    def x_came(zz):
        ref = x_all.at[zz, c]
        return sent(ref, ref, s_x.at[zz], r_x.at[zz], (at.d, 2 * zz + c))

    def forward(zz):
        ref = x_all.at[zz, c]
        return sent(ref, ref, s_fwd.at[zz], r_fwd.at[zz], at.sibling)

    def forwarded(zz):
        ref = x_all.at[zz, 1 - c]
        return sent(ref, ref, s_fwd.at[zz], r_fwd.at[zz], at.sibling)

    def part_send(zz):
        return sent(part.at[zz, 1 - c], other.at[zz], s_part.at[zz], r_part.at[zz], at.sibling)

    def came_send(zz):
        return sent(part.at[zz, c], came.at[z], s_came.at[zz], r_came.at[z], (at.d, 2 * zz + c))

    def came_here(zz):
        return sent(part.at[zz, c], came.at[zz], s_came.at[zz], r_came.at[zz], (at.d, 2 * zz + c))

    def thin_send(zz, cc):
        return sent(
            thin.at[zz], thin_out.at[at.e], s_thin.at[2 * zz + cc], r_thin.at[at.e], (at.d, 2 * zz + cc)
        )

    def thin_here(e):
        return sent(thin.at[0], thin_out.at[e], s_thin.at[e], r_thin.at[e], (at.d, e))

    misc_load = pltpu.make_async_copy(near_in.at[:, pl.ds(0, 128)], misc, s_load.at[8])
    misc_load.start()
    own_load().start()
    sent(x_own, x_all.at[z, c], s_fwd.at[z], r_fwd.at[z], at.sibling).start()
    for j in range(1, chips):
        x_send(order(j)).start()
    for k in range(3):
        for e in range(EXP_DEV):
            weight_load(k, e).start()
    grads_load().start()
    own_load().wait()
    misc_load.wait()

    lanes = lax.broadcasted_iota(jnp.int32, (2 * rows, 128), 1)

    def gates_of(zz, x):
        logits = jnp.where(lanes < experts, nn(x, misc[...]), NEG)
        powers = jnp.exp(logits - jnp.max(logits, axis=1, keepdims=True))
        probs = powers / jnp.sum(powers, axis=1, keepdims=True)
        named = routes[zz][:, 0:1] == lanes
        for j in range(1, TOP):
            named = named | (routes[zz][:, j : j + 1] == lanes)
        chosen = jnp.where(named, probs, 0.0)
        gates = chosen / jnp.sum(chosen, axis=1, keepdims=True)
        return [
            jnp.sum(jnp.where(lanes == EXP_DEV * at.e + k, gates, 0.0), axis=1, keepdims=True)
            for k in range(EXP_DEV)
        ]

    def settle(zz):
        part_send(zz).wait_recv()
        total = part[zz, c].astype(F32) + other[zz].astype(F32)

        @pl.when(zz == z)
        def _():
            row_out[...] = total

        @pl.when(zz != z)
        def _():
            part[zz, c] = total.astype(BF)
            came_send(zz).start()

    def block(j, carry):
        zz = order(j)
        forwarded(zz).wait_recv()
        here = pl.ds(pl.multiple_of(zz * 2 * rows, 2 * rows), 2 * rows)
        x = x_all[zz].reshape(2 * rows, width)
        first, second = gates_of(zz, x)
        dots[...] = jnp.zeros_like(dots)

        @pl.when(j == 0)
        def _():
            for k in range(3):
                for e in range(EXP_DEV):
                    weight_load(k, e).wait()
            grads_load().wait()

        def tile(n, carry):
            cols = pl.ds(pl.multiple_of(n * 256, 256), 256)
            x = x_all[zz].reshape(2 * rows, width)
            g = g_all[zz].reshape(2 * rows, width)
            gate_v = nn(x, w[0, :, cols])
            up_v = nn(x, w[1, :, cols])
            back = nn(g, w[2, :, cols])
            for half in (0, 1):
                s = slice(half * 128, half * 128 + 128)
                is_first = 2 * n + half < per_expert
                gate = jnp.where(is_first, first, second)
                v, u, b = gate_v[:, s], up_v[:, s], back[:, s]
                sig = jax.nn.sigmoid(v)
                act = v * sig
                mid = act * u
                dots[0] += mid * b * is_first.astype(F32)
                dots[1] += mid * b * (1.0 - is_first.astype(F32))
                b = gate * b
                to = pl.ds(pl.multiple_of(n * 256 + half * 128, 128), 128)
                hid[2, here, to] = (gate * mid).astype(BF)
                hid[0, here, to] = (b * u * (sig * (1.0 + v * (1.0 - sig)))).astype(BF)
                hid[1, here, to] = (b * act).astype(BF)
            return carry

        early = (tiles + 1) // 2
        lax.fori_loop(0, early, tile, 0, unroll=True)

        @pl.when(j + 1 < chips)
        def _():
            x_came(order(j + 1)).wait_recv()
            forward(order(j + 1)).start()

        @pl.when(j > 0)
        def _():
            settle(order(j - 1))

        lax.fori_loop(early, tiles, tile, 0, unroll=True)

        def row_tile(n, carry):
            cols = pl.ds(pl.multiple_of(n * 256, 256), 256)
            row = nt(hid[0, here, :], w[0, cols, :]) + nt(hid[1, here, :], w[1, cols, :])
            part[zz, 0, :, cols] = row[:rows].astype(BF)
            part[zz, 1, :, cols] = row[rows:].astype(BF)
            return carry

        lax.fori_loop(0, width // 256, row_tile, 0, unroll=True)
        part_send(zz).start()
        column = jnp.where(
            lanes == 0,
            jnp.sum(dots[0], axis=1, keepdims=True),
            jnp.sum(dots[1], axis=1, keepdims=True),
        )
        thin[zz] = column.T[:8]

        @pl.when(zz == z)
        def _():
            thin_out[at.e] = thin[zz]

        for cc in (0, 1):

            @pl.when(2 * zz + cc != at.e)
            def _(cc=cc):
                thin_send(zz, cc).start()

        return carry

    lax.fori_loop(0, chips, block, 0)
    settle(order(chips - 1))
    mid_store = pltpu.make_async_copy(hid.at[2], mid_out, s_load.at[0])
    mid_store.start()
    for k in (2, 0, 1):

        def grad_tile(n, carry, k=k):
            cols = pl.ds(pl.multiple_of(n * 256, 256), 256)
            left = g_all if k == 2 else x_all
            left = left[...].reshape(chain * rows, width)
            w[k, :, cols] = tn(left, hid[k, :, cols]).astype(BF)
            return carry

        lax.fori_loop(0, tiles, grad_tile, 0, unroll=True)
        for e in range(EXP_DEV):
            grad_store(k, e).start()

    for zz in range(chips):

        @pl.when(zz != z)
        def _(zz=zz):
            came_here(zz).wait_recv()
            row_out[...] += came[zz].astype(F32)
            came_send(zz).wait_send()
            x_send(zz).wait_send()

        part_send(zz).wait_send()
        forward(zz).wait_send()
        for cc in (0, 1):

            @pl.when(2 * zz + cc != at.e)
            def _(zz=zz, cc=cc):
                thin_here(2 * zz + cc).wait_recv()
                thin_send(zz, cc).wait_send()

    mid_store.wait()
    for k in range(3):
        for e in range(EXP_DEV):
            grad_store(k, e).wait()


def moe_fused(normed, routes_all, grads_all, near, weights, experts, collective_id):
    rows, width = normed.shape
    chain = routes_all.shape[0] // rows
    chips = chain // 2
    both = EXP_DEV * weights.shape[3]
    dma = pltpu.SemaphoreType.DMA
    blocks = (chips, 2, rows, width)
    anywhere = pl.BlockSpec(memory_space=pl.ANY)
    vmem = pl.BlockSpec(memory_space=pltpu.VMEM)
    return pl.pallas_call(
        functools.partial(moe_kernel, chips, experts),
        out_shape=[
            jax.ShapeDtypeStruct((rows, width), F32),
            jax.ShapeDtypeStruct((chain, 8, 2 * rows), F32),
            jax.ShapeDtypeStruct((chain * rows, both), BF),
            jax.ShapeDtypeStruct(weights.shape, BF),
        ],
        in_specs=[anywhere, vmem, anywhere, anywhere, anywhere],
        out_specs=[vmem, vmem, anywhere, anywhere],
        scratch_shapes=[
            pltpu.VMEM(blocks, BF),
            pltpu.VMEM(blocks, BF),
            pltpu.VMEM((3, width, both), BF),
            pltpu.VMEM((3, chain * rows, both), BF),
            pltpu.VMEM(blocks, BF),
            pltpu.VMEM((chips, rows, width), BF),
            pltpu.VMEM((chips, rows, width), BF),
            pltpu.VMEM((chips, 8, 2 * rows), F32),
            pltpu.VMEM((2, 2 * rows, 128), F32),
            pltpu.VMEM((width, 128), BF),
            dma((9,)),
        ]
        + [dma((chips,))] * 8
        + [dma((chain,))] * 2,
        compiler_params=pltpu.CompilerParams(
            vmem_limit_bytes=MOE_VMEM, collective_id=collective_id, has_side_effects=True
        ),
        cost_estimate=pl.CostEstimate(
            flops=16 * chain * rows * width * both,
            bytes_accessed=4 * weights.size + 4 * chain * rows * both,
            transcendentals=chain * rows * both,
        ),
    )(
        normed,
        routes_all.reshape(chips, 2 * rows, TOP),
        grads_all.reshape(blocks),
        near,
        weights,
    )


def moe_plain(moe_all, gates_here, grads_all, weights):
    keys, width = moe_all.shape
    hidden = weights.shape[3]
    at_once = 768 if keys % 768 == 0 else keys

    def some(rows):
        x, gates, g = rows
        row = jnp.zeros(x.shape, F32)
        dots, mids, gate_vs, up_vs = [], [], [], []
        for e in range(EXP_DEV):
            scale = gates[:, e : e + 1]
            gate_v = nn(x, weights[0, e])
            up_v = nn(x, weights[1, e])
            back = nn(g, weights[2, e])
            act, slope = silu_parts(gate_v)
            mid = act * up_v
            dots.append(jnp.sum(mid * back, axis=1))
            back = back * scale
            gate_vs.append((back * up_v * slope).astype(BF))
            up_vs.append((back * act).astype(BF))
            mids.append((mid * scale).astype(BF))
            row = row + nt(gate_vs[e], weights[0, e]) + nt(up_vs[e], weights[1, e])
        return (
            row.astype(BF),
            jnp.stack(dots, axis=1),
            jnp.concatenate(mids, axis=1),
            jnp.concatenate(gate_vs, axis=1),
            jnp.concatenate(up_vs, axis=1),
        )

    cut = jax.tree.map(
        lambda a: a.reshape((keys // at_once, at_once) + a.shape[1:]), (moe_all, gates_here, grads_all)
    )
    row, dots, mid, gate_v, up_v = jax.tree.map(
        lambda a: a.reshape((keys,) + a.shape[2:]), lax.map(some, cut)
    )

    def grad_of(x, h):
        grad = tn(x, h).astype(BF).reshape(width, EXP_DEV, hidden)
        return jnp.swapaxes(grad, 0, 1)

    weight_grads = jnp.stack(
        [grad_of(moe_all, gate_v), grad_of(moe_all, up_v), grad_of(grads_all, mid)]
    )
    return row, dots, mid, weight_grads


def spread_kernel(
    chips,
    experts,
    mid,
    weights,
    shared_in,
    near_in,
    normed,
    cot,
    row_sum,
    thin,
    routes,
    middle,
    gain,
    attended_full,
    log_own,
    all_out,
    side_out,
    mix_out,
    gate_out,
    up_out,
    down_out,
    out_out,
    base_out,
    middle_out,
    misc_out,
    delta_out,
    mids,
    w,
    mix,
    dense,
    wide,
    shared,
    near,
    own,
    side,
    turned,
    s_load,
    s_dense,
    s_chain,
    r_chain,
    s_core,
    r_core,
    s_side,
    r_side,
    s_score,
    r_score,
):
    at = Place(chips)
    z, c = at.z, at.c
    rows, width = normed.shape
    hidden = shared_in.shape[1] // 3
    has_up, has_down = z < chips - 1, z > 0
    loads = [
        pltpu.make_async_copy(
            shared_in.at[:, pl.ds(k * hidden, hidden)], shared.at[k], s_load.at[k]
        )
        for k in range(3)
    ]
    loads.append(pltpu.make_async_copy(near_in, near, s_load.at[3]))
    late = [
        pltpu.make_async_copy(weights.at[2, e], w.at[:, pl.ds(e * hidden, hidden)], s_load.at[4 + e])
        for e in range(EXP_DEV)
    ]
    late.append(pltpu.make_async_copy(mid, mids, s_load.at[4 + EXP_DEV]))
    for copy in loads + late:
        copy.start()
    greet([at.sibling, at.up, at.down], [None, has_up, has_down])

    lanes = lax.broadcasted_iota(jnp.int32, (rows, 128), 1)
    turned[...] = jnp.zeros_like(turned)
    for e in range(2 * chips):
        turned[EXP_DEV * e : EXP_DEV * (e + 1), :] = thin[e, :EXP_DEV, :]
    flipped = turned[...].T
    grad_gates = jnp.where(c == 0, flipped[:rows], flipped[rows:])
    loads[3].wait()
    logits = jnp.where(lanes < experts, nn(normed[...], near[:, :128]), NEG)
    powers = jnp.exp(logits - jnp.max(logits, axis=1, keepdims=True))
    probs = powers / jnp.sum(powers, axis=1, keepdims=True)
    named = routes[:, 0:1] == lanes
    for j in range(1, TOP):
        named = named | (routes[:, j : j + 1] == lanes)
    chosen = jnp.where(named, probs, 0.0)
    total = jnp.sum(chosen, axis=1, keepdims=True)
    gates = chosen / total
    grad_chosen = (grad_gates - jnp.sum(gates * grad_gates, axis=1, keepdims=True)) / total
    grad_probs = jnp.where(named, grad_chosen, 0.0)
    grad_logits = (
        probs * (grad_probs - jnp.sum(probs * grad_probs, axis=1, keepdims=True))
    ).astype(BF)
    grad_normed = row_sum[...] + nt(grad_logits, near[:, :128])

    for k in range(3):
        loads[k].wait()
    gate_v = nn(normed[...], shared[0])
    up_v = nn(normed[...], shared[1])
    back = nn(cot[...], shared[2])
    act, slope = silu_parts(gate_v)
    shared_mid = (act * up_v).astype(BF)
    gate_grad = (back * up_v * slope).astype(BF)
    up_grad = (back * act).astype(BF)
    grad_normed = grad_normed + nt(gate_grad, shared[0]) + nt(up_grad, shared[1])

    inverse = inverse_rms(middle[...])
    unit = middle[...] * inverse
    gain_grad = jnp.sum(grad_normed * unit, axis=0, keepdims=True)
    scaled = grad_normed * gain[...]
    grad_middle = cot[...].astype(F32) + inverse * (
        scaled - unit * jnp.mean(scaled * unit, axis=-1, keepdims=True)
    )
    middle_out[...] = grad_middle
    attn = grad_middle.astype(BF)
    own[...] = nn(attn, near[:, 128:]).astype(BF)
    columns = jnp.zeros((rows, 128), F32)
    for h in range(H):
        s = slice(h * HD, (h + 1) * HD)
        delta = jnp.sum(own[:, s].astype(F32) * attended_full[:, s], axis=1, keepdims=True)
        delta_out[h] = jnp.broadcast_to(delta, (rows, 8))
        columns = jnp.where(lanes == h, log_own[h][:, :1], columns)
        columns = jnp.where(lanes == H + h, delta, columns)
    tall = side.shape[1]
    columns = jnp.concatenate([columns, jnp.zeros((tall - rows, 128), F32)], axis=0)
    side[...] = columns.T[: side.shape[0]]

    pairs = (
        (own, all_out, s_chain, r_chain, s_core, r_core),
        (side, side_out, s_side, r_side, s_score, r_score),
    )

    def along(p, zz, direction, src=None):
        out, ss, rs = pairs[p][1:4]
        ref = out.at[2 * zz + c]
        device = at.up if direction == 0 else at.down
        return sent(ref if src is None else src, ref, ss.at[direction, zz], rs.at[zz], device)

    def over(p, zz, core, src=None):
        out, ss, rs = pairs[p][1], pairs[p][4], pairs[p][5]
        ref = out.at[2 * zz + core]
        return sent(ref if src is None else src, ref, ss.at[zz], rs.at[zz], at.sibling)

    locals_ = []
    for p in (1, 0):

        @pl.when(has_up)
        def _(p=p):
            along(p, z, 0, pairs[p][0]).start()

        @pl.when(has_down)
        def _(p=p):
            along(p, z, 1, pairs[p][0]).start()

        over(p, z, c, pairs[p][0]).start()
        copy = pltpu.make_async_copy(
            pairs[p][0], pairs[p][1].at[2 * z + c], s_load.at[5 + EXP_DEV + p]
        )
        copy.start()
        locals_.append(copy)

    def arrived(zz, direction):
        for p in (1, 0):
            along(p, zz, direction).wait_recv()

            @pl.when(has_up if direction == 0 else has_down)
            def _(p=p):
                along(p, zz, direction).start()

            over(p, zz, c).start()

    def at_distance(k):
        @pl.when(z - k >= 0)
        def _():
            arrived(z - k, 0)

        @pl.when(z + k < chips)
        def _():
            arrived(z + k, 1)

    stores = []

    def store(src, dst, k):
        copy = pltpu.make_async_copy(src, dst, s_dense.at[k])
        copy.start()
        stores.append(copy)

    def mix_chip(zz):
        here = pl.ds(zz * 2 * rows, 2 * rows)
        for n in range(0, width, 256):
            tile = nt(mids[here, :], w[n : n + 256, :]).astype(BF)
            mix[zz, 0, :, n : n + 256] = tile[:rows]
            mix[zz, 1, :, n : n + 256] = tile[rows:]
        store(mix.at[zz], mix_out.at[zz], 4 + zz)

    dense[0] = tn(normed[...], gate_grad).astype(BF)
    store(dense.at[0], gate_out, 0)
    dense[1] = tn(normed[...], up_grad).astype(BF)
    store(dense.at[1], up_out, 1)
    dense[2] = tn(cot[...], shared_mid).astype(BF)
    store(dense.at[2], down_out, 2)
    wide[...] = tn(attn, attended_full[...].astype(BF)).astype(BF)
    store(wide, out_out, 3)
    base_out[...] = middle[...] + nt(shared_mid, shared[2])
    at_distance(1)
    for copy in late:
        copy.wait()
    half = (chips + 1) // 2
    for j in range(half):
        mix_chip(j)
    for k in range(2, chips):
        at_distance(k)
        if k == 2:
            for j in range(half, chips):
                mix_chip(j)
            all_lanes = lax.broadcasted_iota(jnp.int32, (width, 128), 1)
            column = jnp.broadcast_to(gain_grad, (8, width)).T[:, :1]
            misc_out[:, :128] = jnp.where(
                all_lanes == experts + 1, column, tn(normed[...], grad_logits)
            )
            misc_out[:, 128:] = jnp.zeros((width, 128), F32)
    for p in (1, 0):
        for zz in range(chips):
            over(p, zz, 1 - c).wait_recv()
            over(p, zz, c).wait_send()

            @pl.when((zz <= z) & has_up)
            def _(p=p, zz=zz):
                along(p, zz, 0).wait_send()

            @pl.when((zz >= z) & has_down)
            def _(p=p, zz=zz):
                along(p, zz, 1).wait_send()

    for copy in locals_ + stores:
        copy.wait()


def spread(
    mid, weights, shared, near, normed, cot, row_sum, thin, routes, middle, gain, attended, log_own, experts, collective_id
):
    rows, width = normed.shape
    keys, both = mid.shape
    chain = keys // rows
    chips = chain // 2
    hidden = both // EXP_DEV
    assert experts + 2 <= 128 and chips > 2
    tall = 128 * (-(-rows // 128))
    lines = 8 * (-(-2 * H // 8))
    dma = pltpu.SemaphoreType.DMA
    anywhere = pl.BlockSpec(memory_space=pl.ANY)
    vmem = pl.BlockSpec(memory_space=pltpu.VMEM)
    out = jax.ShapeDtypeStruct
    return pl.pallas_call(
        functools.partial(spread_kernel, chips, experts),
        out_shape=[
            out((chain, rows, width), BF),
            out((chain, lines, tall), F32),
            out((chips, 2, rows, width), BF),
            out((width, hidden), BF),
            out((width, hidden), BF),
            out((width, hidden), BF),
            out((width, width), BF),
            out((rows, width), F32),
            out((rows, width), F32),
            out((width, 256), F32),
            out((H, rows, 8), F32),
        ],
        in_specs=[anywhere] * 4 + [vmem] * 9,
        out_specs=[anywhere] * 7 + [vmem] * 4,
        scratch_shapes=[
            pltpu.VMEM((keys, both), BF),
            pltpu.VMEM((width, both), BF),
            pltpu.VMEM((chips, 2, rows, width), BF),
            pltpu.VMEM((3, width, hidden), BF),
            pltpu.VMEM((width, width), BF),
            pltpu.VMEM((3, width, hidden), BF),
            pltpu.VMEM(near.shape, BF),
            pltpu.VMEM((rows, width), BF),
            pltpu.VMEM((lines, tall), F32),
            pltpu.VMEM((128, 2 * rows), F32),
            dma((7 + EXP_DEV,)),
            dma((4 + chips,)),
        ]
        + [dma((2, chips)), dma((chips,)), dma((chips,)), dma((chips,))] * 2,
        compiler_params=pltpu.CompilerParams(
            vmem_limit_bytes=MOE_VMEM, collective_id=collective_id, has_side_effects=True
        ),
        cost_estimate=pl.CostEstimate(
            flops=2 * keys * both * width, bytes_accessed=64 * keys * width, transcendentals=0
        ),
    )(mid, weights, shared, near, normed, cot, row_sum, thin, routes, middle, gain, attended, log_own)


def finish_kernel(chips, chunks, n_in, experts, *refs):
    ins = refs[:n_in]
    normed, projected, weight_in, misc_in, unit, inverse, gain, grad_middle, mix_in, base = refs[
        n_in : n_in + 10
    ]
    n_out = n_in + 2
    outs = refs[n_in + 10 : n_in + 10 + n_out]
    input_out, output_out = refs[n_in + 10 + n_out : n_in + 12 + n_out]
    rest = refs[n_in + 12 + n_out :]
    s_in, s_core, r_core, s_one, r_one, s_two, r_two, s_end, r_end = rest[:9]
    s_mix, s_mcore, r_mcore, s_mchain, r_mchain, s_weight = rest[9:15]
    weight, grad_ref, tile_ref, mix_mine, mix_other, mix_came = rest[15:21]
    buffers = rest[21:]
    n_chunks = len(chunks)
    at = Place(chips)
    z, c, x, y = at.z, at.c, at.x, at.y
    chain = 2 * chips
    others = [(at.d, 2 * lax.rem(z + k, chips) + c) for k in range(1, chips)]
    devices = [at.sibling, at.across_x, at.across_y] + others
    greet(devices, [None] * len(devices))

    class Chunk:
        def __init__(self, q):
            self.i, self.first, self.wide = chunks[q]
            self.q = q
            self.made = self.i >= n_in
            self.mine, self.other, one_x, one_y, two_x, two_y, self.end, self.give = buffers[
                8 * q : 8 * q + 8
            ]
            self.one, self.two = (one_x, one_y), (two_x, two_y)
            self.cols = pl.ds(self.first, self.wide)
            cut = self.wide // 256 * 128
            self.half = (pl.ds(0, cut), pl.ds(cut, self.wide - cut))

        def load(self):
            return pltpu.make_async_copy(
                ins[self.i].at[:, :, :, c, :, self.cols], self.mine, s_in.at[self.q]
            )

        def core(self):
            source = self.give if self.made else ins[self.i].at[:, :, :, 1 - c, :, self.cols]
            return sent(source, self.other, s_core.at[self.q], r_core.at[self.q], at.sibling)

        def first_x(self):
            return sent(
                self.mine.at[:, 1 - x, :, :, self.half[0]],
                self.one[0],
                s_one.at[self.q, 0],
                r_one.at[self.q, 0],
                at.across_x,
            )

        def first_y(self):
            return sent(
                self.mine.at[1 - y, :, :, :, self.half[1]],
                self.one[1],
                s_one.at[self.q, 1],
                r_one.at[self.q, 1],
                at.across_y,
            )

        def second_y(self):
            return sent(
                self.mine.at[1 - y, x, :, :, self.half[0]],
                self.two[0],
                s_two.at[self.q, 0],
                r_two.at[self.q, 0],
                at.across_y,
            )

        def second_x(self):
            return sent(
                self.mine.at[y, 1 - x, :, :, self.half[1]],
                self.two[1],
                s_two.at[self.q, 1],
                r_two.at[self.q, 1],
                at.across_x,
            )

        def last(self, k):
            zz = lax.rem(z + k, chips)
            return sent(
                self.mine.at[y, x, zz],
                self.end.at[k - 1],
                s_end.at[self.q, k - 1],
                r_end.at[self.q, k - 1],
                (at.d, 2 * zz + c),
            )

        def take(self):
            block = self.mine.shape[3]

            def body(k, carry):
                yy, xx, zz = k // (2 * chips), (k // chips) % 2, k % chips
                row = (2 * yy + xx) * chain + 2 * zz
                keep = pl.ds(pl.multiple_of((row + c) * block, block), block)
                away = pl.ds(pl.multiple_of((row + 1 - c) * block, block), block)
                self.mine[yy, xx, zz] = tile_ref[keep, : self.wide].astype(BF)
                self.give[yy, xx, zz] = tile_ref[away, : self.wide].astype(BF)
                return carry

            lax.fori_loop(0, 4 * chips, body, 0, unroll=4)
            self.core().start()

    parts = [Chunk(q) for q in range(n_chunks)]

    def stage_one(p):
        p.core().wait_recv()
        if not p.made:
            p.load().wait()

        def body(k, carry):
            yy, xx, zz = k // (2 * chips), (k // chips) % 2, k % chips
            p.mine[yy, xx, zz] = p.mine[yy, xx, zz] + p.other[yy, xx, zz]
            return carry

        lax.fori_loop(0, 4 * chips, body, 0, unroll=4)
        p.first_x().start()
        p.first_y().start()

    def stage_two(p):
        p.first_x().wait_recv()
        p.first_y().wait_recv()

        def body(k, carry):
            v, zz = k // chips, k % chips
            a, b = p.half
            p.mine[v, x, zz, :, a] = p.mine[v, x, zz, :, a] + p.one[0][v, zz]
            p.mine[y, v, zz, :, b] = p.mine[y, v, zz, :, b] + p.one[1][v, zz]
            return carry

        lax.fori_loop(0, 2 * chips, body, 0, unroll=2)
        p.second_y().start()
        p.second_x().start()

    def stage_three(p):
        p.second_y().wait_recv()
        p.second_x().wait_recv()

        def body(zz, carry):
            for w in (0, 1):
                s = p.half[w]
                p.mine[y, x, zz, :, s] = p.mine[y, x, zz, :, s] + p.two[w][zz]
            return carry

        lax.fori_loop(0, chips, body, 0, unroll=2)
        for k in range(1, chips):
            p.last(k).start()

    def stage_four(p):
        total = p.mine[y, x, z].astype(F32)
        for k in range(1, chips):
            p.last(k).wait_recv()
            total = total + p.end[k - 1].astype(F32)
        outs[p.i][:, p.first : p.first + p.wide] = total

    def mix_load(zz):
        return pltpu.make_async_copy(mix_in.at[zz, c], mix_mine.at[zz], s_mix.at[zz])

    def mix_core(zz):
        return sent(
            mix_in.at[zz, 1 - c], mix_other.at[zz], s_mcore.at[zz], r_mcore.at[zz], at.sibling
        )

    def mix_over(k):
        zz = lax.rem(z + k, chips)
        return sent(
            mix_mine.at[zz], mix_came.at[k], s_mchain.at[k], r_mchain.at[k], (at.d, 2 * zz + c)
        )

    def mix_settle():
        for k in range(1, chips):
            zz = lax.rem(z + k, chips)
            mix_core(zz).wait_recv()
            mix_load(zz).wait()
            mix_mine[zz] = (mix_mine[zz].astype(F32) + mix_other[zz].astype(F32)).astype(BF)
            mix_over(k).start()
        mix_core(z).wait_recv()
        mix_load(z).wait()

    part = projected.shape[2]

    def weight_load(k):
        return pltpu.make_async_copy(
            weight_in.at[:, pl.ds(k * part, part)], weight, s_weight.at[0]
        )

    def input_grads(k):
        weight_load(k).wait()
        if k == 0:
            grad_ref[...] = nt(projected[0], weight[...])
        else:
            grad_ref[...] += nt(projected[k], weight[...])
        if k < 2:
            weight_load(k + 1).start()
            return
        grad = grad_ref[...]
        gains = jnp.sum(grad * unit[...], axis=0, keepdims=True)
        column = jnp.broadcast_to(gains, (8, part)).T[:, :1]
        lanes = lax.broadcasted_iota(jnp.int32, misc_in.shape, 1)
        tile_ref[:, : misc_in.shape[1]] = jnp.where(lanes == experts, column, misc_in[...])
        scaled = grad * gain[...]
        mean = jnp.mean(scaled * unit[...], axis=1, keepdims=True)
        input_out[...] = (grad_middle[...] + inverse[...] * (scaled - unit[...] * mean)).astype(BF)

    for k in range(1, chips + 1):
        zz = lax.rem(z + k, chips)
        mix_core(zz).start()
        mix_load(zz).start()
    for p in parts:
        if not p.made:
            p.core().start()
            p.load().start()
    weight_load(0).start()
    mix_settle()
    n_known = sum(not p.made for p in parts)
    n_made = n_chunks - 1 - n_known
    stages = ((0, stage_one), (1, stage_two), (2, stage_three), (6, stage_four))
    for t in range(n_chunks + stages[-1][0]):
        for lag, stage in stages:
            if 0 <= t - lag < n_chunks:
                stage(parts[t - lag])
        if t < n_made:
            p = parts[n_known + t]
            k, first = p.first // part, p.first % part
            tile_ref[:, : p.wide] = tn(normed[...], projected[k, :, first : first + p.wide])
            p.take()
        elif t < n_made + 3:
            input_grads(t - n_made)
            if t == n_made + 2:
                parts[-1].take()
    total = base[...] + mix_mine[z].astype(F32) + mix_other[z].astype(F32)
    for k in range(1, chips):
        mix_over(k).wait_recv()
        total = total + mix_came[k].astype(F32)
    output_out[...] = total.astype(BF)
    for p in parts:
        p.core().wait_send()
        p.first_x().wait_send()
        p.first_y().wait_send()
        p.second_x().wait_send()
        p.second_y().wait_send()
        for k in range(1, chips):
            p.last(k).wait_send()
    for k in range(1, chips):
        mix_over(k).wait_send()
    for zz in range(chips):
        mix_core(zz).wait_send()


def finish(
    arrays,
    chunk_widths,
    experts,
    normed,
    projected,
    qkv_weight,
    misc,
    unit,
    inverse,
    gain,
    grad_middle,
    mix,
    base,
    collective_id,
):
    chain = lax.axis_size("expert")
    chips = chain // 2
    width = arrays[0].shape[0]
    block = width // (4 * chain)
    rows = normed.shape[0]
    columns = qkv_weight.shape[1]
    n = len(arrays)
    dma = pltpu.SemaphoreType.DMA
    sizes = [a.shape[1] for a in arrays] + [columns, misc.shape[1]]
    chunks = []
    for i, (size, wide) in enumerate(zip(sizes, chunk_widths)):
        assert size % wide == 0 and wide % 128 == 0 and wide >= 256
        chunks += [(i, first, wide) for first in range(0, size, wide)]
    q = len(chunks)
    scratch = [dma((q,)), dma((q,)), dma((q,))] + [dma((q, 2))] * 4 + [dma((q, chips - 1))] * 2
    scratch += [dma((chips,))] * 5 + [dma((1,))]
    scratch += [
        pltpu.VMEM((width, columns // 3), BF),
        pltpu.VMEM((rows, width), F32),
        pltpu.VMEM((width, max(chunk_widths[n:])), F32),
        pltpu.VMEM((chips, rows, width), BF),
        pltpu.VMEM((chips, rows, width), BF),
        pltpu.VMEM((chips, rows, width), BF),
    ]
    for i, first, wide in chunks:
        cut = wide // 256 * 128
        scratch += [
            pltpu.VMEM((2, 2, chips, block, wide), BF),
            pltpu.VMEM((2, 2, chips, block, wide), BF),
            pltpu.VMEM((2, chips, block, cut), BF),
            pltpu.VMEM((2, chips, block, wide - cut), BF),
            pltpu.VMEM((chips, block, cut), BF),
            pltpu.VMEM((chips, block, wide - cut), BF),
            pltpu.VMEM((chips - 1, block, wide), BF),
            pltpu.VMEM((2, 2, chips, block, wide) if i >= n else (16, 128), BF),
        ]
    anywhere = pl.BlockSpec(memory_space=pl.ANY)
    vmem = pl.BlockSpec(memory_space=pltpu.VMEM)
    return pl.pallas_call(
        functools.partial(finish_kernel, chips, tuple(chunks), n, experts),
        out_shape=[jax.ShapeDtypeStruct((block, size), F32) for size in sizes]
        + [jax.ShapeDtypeStruct((rows, width), BF)] * 2,
        in_specs=[anywhere] * n
        + [vmem, vmem, anywhere, vmem, vmem, vmem, vmem, vmem, anywhere, vmem],
        out_specs=[vmem] * (n + 4),
        scratch_shapes=scratch,
        compiler_params=pltpu.CompilerParams(
            vmem_limit_bytes=MOE_VMEM, collective_id=collective_id, has_side_effects=True
        ),
        cost_estimate=pl.CostEstimate(
            flops=4 * rows * width * columns, bytes_accessed=64 * width * columns, transcendentals=0
        ),
    )(
        *[a.reshape(2, 2, chips, 2, block, a.shape[1]) for a in arrays],
        normed,
        projected,
        qkv_weight,
        misc,
        unit,
        inverse,
        gain,
        grad_middle,
        mix,
        base,
    )


def silu_parts(values):
    s = jax.nn.sigmoid(values)
    return values * s, s * (1.0 + values * (1.0 - s))


def local(
    tokens,
    cotangent,
    lengths,
    routes,
    attn_qkv,
    attn_out,
    shared_gate,
    shared_up,
    shared_down,
    router,
    gains,
    expert_gate,
    expert_up,
    expert_down,
):
    rows = tokens.shape[1]
    width = tokens.shape[2]
    hidden = shared_gate.shape[1]
    chain = lax.axis_size("expert")
    index = lax.axis_index("expert")
    experts = EXP_DEV * chain
    everyone = ("dp", "expert")
    keys = rows * chain
    own_first = index * rows
    me = index.reshape(1).astype(jnp.int32)

    route_pad = 128 * (-(-(experts + 2) // 128))
    misc = jnp.concatenate([router.astype(BF), gains.astype(BF).T], axis=1)
    misc = jnp.pad(misc, ((0, 0), (0, route_pad - experts - 2)))
    near = jnp.concatenate([misc, attn_out.astype(BF).T], axis=1)
    expert_shard = jnp.stack(
        [expert_gate.astype(BF), expert_up.astype(BF), jnp.swapaxes(expert_down.astype(BF), 1, 2)]
    )
    expert_weight = lax.all_gather(expert_shard, "dp", axis=2, tiled=True)
    shared = jnp.concatenate(
        [shared_gate.astype(BF), shared_up.astype(BF), shared_down.astype(BF).T], axis=1
    )
    fits = 2 * width * EXP_DEV * hidden * 3 + 2 * keys * (3 * EXP_DEV * hidden + 5 * width) < MOE_VMEM
    chained = [tokens[0], routes[0].T, cotangent[0]] + ([shared] if fits else [])
    qkv_weight, near, tokens_all, routes_all, grads_all, *early = gather(
        [attn_qkv.astype(BF), near], chained, 0
    )
    shared = early[0] if fits else shared
    grads_all = grads_all.reshape(keys, width)
    qkv_weight = qkv_weight.reshape(width, 3 * H * HD)
    near = near.reshape(width, near.shape[-1])
    tokens_all = tokens_all.reshape(keys, width)
    routes_all = jnp.swapaxes(routes_all, 1, 2).reshape(keys, TOP)
    cuts = [route_pad, route_pad + width]
    cuts += [cuts[-1] + hidden, cuts[-1] + 2 * hidden]
    misc, out_t = jnp.split(near, cuts[:1], axis=1)
    route_weight = misc[:, :experts]
    gain_attn = misc[:, experts].astype(F32)
    gain_moe = misc[:, experts + 1].astype(F32)
    first_all, rope_all = doc_starts_of(lengths[0], jnp.arange(keys, dtype=jnp.int32))
    first_own = lax.dynamic_slice_in_dim(first_all, own_first, rows, 0)
    cosine, sine = turn_tables(rope_all)
    cosine_own = lax.dynamic_slice_in_dim(cosine, own_first, rows, 0)
    sine_own = lax.dynamic_slice_in_dim(sine, own_first, rows, 0)
    cosine_own = jnp.concatenate([cosine_own, cosine_own], axis=1)
    sine_own = jnp.concatenate([-sine_own, sine_own], axis=1)
    inputs = tokens[0].astype(F32)
    inverse_one = inverse_rms(inputs)
    unit_one = inputs * inverse_one
    normed = (unit_one * gain_attn).astype(BF)
    qkv = project_qkv(tokens_all, qkv_weight, gain_attn, cosine, sine)
    attended_full, log_own = attend(me, qkv, first_own)
    attended = attended_full.astype(BF)
    middle = inputs + nt(attended, out_t)
    inverse_two = inverse_rms(middle)
    unit_two = middle * inverse_two
    normed_moe = (unit_two * gain_moe).astype(BF)
    shared, expert_weight, normed_moe = lax.optimization_barrier((shared, expert_weight, normed_moe))
    shared = lax.all_gather(shared, "dp" if fits else everyone, axis=0, tiled=True)
    shared = shared.reshape(width, 3 * hidden)
    gate_shared, up_shared, down_t = jnp.split(shared, [hidden, 2 * hidden], axis=1)

    def routing(activations, route_ids):
        logits = nn(activations, route_weight)
        probs = jax.nn.softmax(logits, axis=-1)
        named = route_ids[:, :, None] == jnp.arange(experts, dtype=jnp.int32)[None, None, :]
        named = jnp.any(named, axis=1)
        chosen = jnp.where(named, probs, 0.0)
        total = jnp.sum(chosen, axis=1, keepdims=True)
        return probs, named, chosen / total, total

    if fits:
        row_sum, gate_grads, expert_mid, expert_grads = moe_fused(
            normed_moe, routes_all, grads_all, near, expert_weight, experts, 1
        )
        (
            grad_all,
            side_all,
            mixture,
            grad_gate_shared,
            grad_up_shared,
            grad_down_t,
            grad_out_t,
            base,
            grad_middle,
            grad_misc,
            delta_own,
        ) = spread(
            expert_mid,
            expert_weight,
            shared,
            near,
            normed_moe,
            cotangent[0],
            row_sum,
            gate_grads,
            routes[0],
            middle,
            gain_moe[None, :],
            attended_full,
            log_own,
            experts,
            3,
        )
        side_all = side_all[:, : 2 * H, :rows]
    else:
        probs, named, gates, chosen_total = routing(normed_moe, routes[0])

        shared_gate_v = nn(normed_moe, gate_shared)
        shared_up_v = nn(normed_moe, up_shared)
        shared_act, shared_slope = silu_parts(shared_gate_v)
        shared_mid = (shared_act * shared_up_v).astype(BF)
        shared_out = nt(shared_mid, down_t)
        grad_out = cotangent[0].astype(F32)
        grad_bf = cotangent[0]
        grad_shared_mid = nn(grad_bf, down_t)
        grad_shared_gate_v = (grad_shared_mid * shared_up_v * shared_slope).astype(BF)
        grad_shared_up_v = (grad_shared_mid * shared_act).astype(BF)
        grad_normed_moe = nt(grad_shared_gate_v, gate_shared) + nt(grad_shared_up_v, up_shared)

        moe_all = gather([], [normed_moe], 1)[0].reshape(keys, width)
        unused, unused, gates_all, unused = routing(moe_all, routes_all)
        gates_here = lax.dynamic_slice_in_dim(gates_all, index * EXP_DEV, EXP_DEV, 1)
        row_part, gate_grads, expert_mid, expert_grads = moe_plain(
            moe_all, gates_here, grads_all, expert_weight
        )
        gate_grads = jnp.transpose(gate_grads.T.reshape(EXP_DEV, chain, rows), (1, 0, 2))
        row_sum, gate_grads = to_owner(row_part.reshape(chain, rows, width), gate_grads, 2)
        gate_grads = gate_grads.reshape(experts, rows).T
        grad_chosen = (gate_grads - jnp.sum(gates * gate_grads, axis=1, keepdims=True)) / chosen_total
        grad_probs = jnp.where(named, grad_chosen, 0.0)
        grad_logits = (
            probs * (grad_probs - jnp.sum(probs * grad_probs, axis=1, keepdims=True))
        ).astype(BF)
        grad_route = tn(normed_moe, grad_logits)
        grad_normed_moe = grad_normed_moe + row_sum + nt(grad_logits, route_weight)
        grad_gain_moe = jnp.sum(grad_normed_moe * unit_two, axis=0)
        scaled_two = grad_normed_moe * gain_moe
        grad_middle = grad_out + inverse_two * (
            scaled_two - unit_two * jnp.mean(scaled_two * unit_two, axis=-1, keepdims=True)
        )
        grad_attn = grad_middle.astype(BF)
        grad_attended = nn(grad_attn, out_t).astype(BF)

        delta = jnp.sum((grad_attended.astype(F32) * attended_full).reshape(rows, H, HD), axis=-1).T
        side = jnp.concatenate([log_own[:, :, 0], delta], axis=0)
        grad_all, side_all = gather([], [grad_attended, side], 3)
        delta_own = jnp.broadcast_to(delta[:, :, None], (H, rows, 8))
    expert_sum = lax.psum_scatter(expert_grads, "dp", scatter_dimension=2, tiled=True)
    grad_all = grad_all.reshape(keys, H * HD)
    side_all = jnp.transpose(side_all, (1, 0, 2)).reshape(2, H, 1, keys)
    grads = attend_back(
        me,
        qkv,
        grad_all,
        log_own,
        delta_own,
        side_all[0],
        side_all[1],
        (first_own, first_all),
        cosine_own,
        sine_own,
    )
    if fits:
        out_sum, gate_sum, up_sum, down_sum, qkv_sum, misc_sum, grad_inputs, output = finish(
            [grad_out_t, grad_gate_shared, grad_up_shared, grad_down_t],
            (640, hidden, hidden, hidden, 640, 256),
            experts,
            normed,
            grads,
            qkv_weight,
            grad_misc,
            unit_one,
            inverse_one,
            gain_attn[None, :],
            grad_middle,
            mixture,
            base,
            4,
        )
    else:
        grad_misc = jnp.concatenate(
            [grad_route, jnp.zeros((width, 1), F32), grad_gain_moe[:, None]], axis=1
        )
        grad_misc = jnp.pad(grad_misc, ((0, 0), (0, 256 - experts - 2)))
        down = expert_weight[2]
        mixture = nt(expert_mid[:, :hidden], down[0])
        for e in range(1, EXP_DEV):
            mixture = mixture + nt(expert_mid[:, e * hidden : (e + 1) * hidden], down[e])
        mixture = lax.psum_scatter(mixture.astype(BF), "expert", scatter_dimension=0, tiled=True)
        output = (middle + shared_out + mixture.astype(F32)).astype(BF)
        grad_projected = jnp.concatenate([grads[0], grads[1], grads[2]], axis=1)
        grad_normed_one = nt(grad_projected, qkv_weight)
        grad_gain_attn = jnp.sum(grad_normed_one * unit_one, axis=0)
        scaled_one = grad_normed_one * gain_attn
        grad_inputs = grad_middle + inverse_one * (
            scaled_one - unit_one * jnp.mean(scaled_one * unit_one, axis=-1, keepdims=True)
        )
        grad_inputs = grad_inputs.astype(BF)
        out_sum, gate_sum, up_sum, down_sum, qkv_sum, misc_sum = sum_dense(
            [
                tn(grad_attn, attended).astype(BF),
                tn(normed_moe, grad_shared_gate_v).astype(BF),
                tn(normed_moe, grad_shared_up_v).astype(BF),
                tn(grad_bf, shared_mid).astype(BF),
                tn(normed, grad_projected).astype(BF),
                grad_misc.at[:, experts].set(grad_gain_attn).astype(BF),
            ],
            (640, hidden, hidden, hidden, 768, 256),
            4,
        )
    return (
        output[None],
        grad_inputs[None],
        qkv_sum,
        out_sum.T,
        gate_sum,
        up_sum,
        down_sum.T,
        misc_sum[:, :experts],
        misc_sum[:, experts : experts + 2].T,
        expert_sum[0].astype(F32),
        expert_sum[1].astype(F32),
        jnp.swapaxes(expert_sum[2], 1, 2).astype(F32),
    )


def solution(mesh):
    everyone = ("dp", "expert")
    in_specs = (
        P("dp", "expert", None),
        P("dp", "expert", None),
        P("dp", None),
        P("dp", "expert", None),
        P(everyone, None),
        P(None, everyone),
        P(everyone, None),
        P(everyone, None),
        P(None, everyone),
        P(everyone, None),
        P(None, everyone),
        P("expert", "dp", None),
        P("expert", "dp", None),
        P("expert", None, "dp"),
    )
    out_specs = (
        P("dp", "expert", None),
        P("dp", "expert", None),
        P(everyone, None),
        P(None, everyone),
        P(everyone, None),
        P(everyone, None),
        P(None, everyone),
        P(everyone, None),
        P(None, everyone),
        P("expert", "dp", None),
        P("expert", "dp", None),
        P("expert", None, "dp"),
    )
    return jax.shard_map(local, mesh=mesh, in_specs=in_specs, out_specs=out_specs, check_vma=False)
```
